128 devices in a mesh: seq: 8 (over y_lo, x), table: 16 (over z, y_hi, core).
Axes of the slice: x: 4, y: 4 (y_hi: 2, y_lo: 2; y = y_hi * 2 + y_lo), z: 4, core: 2. Of those that a mesh axis runs over, the one named last changes fastest.
Arguments:
- item_table: bfloat16 [262144, 512], P(('seq', 'table')), may hold values from -6 to 6
- owner: int32 [16, 4096, 1], P('table', 'seq'), may hold values from 0 to 127; in each aligned block of 512 rows (0 to 511, 512 to 1023, ..., all dimensions but the last counted through in order) at most 8 rows name the same one
- item_row: int32 [16, 4096], P('table', 'seq'), may hold values from 0 to 2047
- lengths: int32 [16], P('table'), may hold values from 1 to 4096, as said below
- gain_in: float32 [512], replicated, may hold values from 0.5 to 1.5
- gain_out: float32 [512], replicated, may hold values from 0.5 to 1.5
- w_in: bfloat16 [512, 2048], replicated, may hold values from -0.25 to 0.25
- w_out: bfloat16 [512, 512], replicated, may hold values from -0.25 to 0.25
- out_grad: bfloat16 [16, 4096, 512], P('table', 'seq'), may hold values from -6 to 6
Outputs:
- hidden_out: bfloat16 [16, 4096, 512], P('table', 'seq')
- table_grad: float32 [262144, 512], P(('seq', 'table'))
- w_in_grad: float32 [512, 2048], replicated
- w_out_grad: float32 [512, 512], replicated
The draws below stay inside these ranges and needn't reach their ends.
Inputs may be any that keep to these rules, and one draw needn't show every extreme that they name: Among the 512 events of one device (positions s*512 to (s+1)*512 - 1 of one user), no owner appears more than 8 times, and some device's block reaches 8. `lengths`: at least one history has all 4096 events live.
All inputs are finite; a program needn't handle non-finite values.
Results may differ from the reference program's by a relative error of at most 0.0083.
Values may be sent and summed in bfloat16 or wider, within the bound.
A program may use at most 128 MiB of HBM per device.

```python
import math
import jax
import jax.numpy as jnp
import numpy as np
from jax import lax

D = 512
HEADS = 4
HEAD = 128
TOK_DEV = 512
ROWS_DEV = 2048
EVENTS = 4096
USERS = 16
OWNERS = 128
ITEMS = 262144
CAP = 8
TOKENS = 65536


def draw_lengths(key, part):
    key = jax.random.fold_in(key, 11)
    first, second = jax.random.split(key)
    drawn = jax.random.randint(first, (USERS,), 1, EVENTS + 1)
    chosen = jax.random.randint(second, (), 0, USERS)
    return jnp.where(jnp.arange(USERS) == chosen, EVENTS, drawn).astype(jnp.int32)


def touch_ends(array, rng, smallest, largest):
    longest = array.shape.index(max(array.shape))
    spots = []
    for shift in (0, 1):
        where = [jax.random.randint(jax.random.fold_in(rng, axis), (), 0, length) for axis, length in enumerate(array.shape)]
        where[longest] = (where[longest] + shift) % array.shape[longest]
        spots.append(tuple(where))
    return array.at[spots[0]].set(smallest).at[spots[1]].set(largest)


def level_of(rng, extent, shards, low, top_value):
    level, own = 1.0, jax.random.fold_in(rng, 6)
    for dim, blocks in shards:
        draws = jnp.exp(jax.random.uniform(jax.random.fold_in(own, dim), (blocks,), jnp.float32, low / len(shards), top_value / len(shards)))
        level = level * jnp.repeat(draws, extent[dim] // blocks).reshape([-1 if axis == dim else 1 for axis in range(len(extent))])
    return level


def deal_out(own_key, own, number, rows, amount, top, reach, skew):
    sequence = jax.random.permutation(own_key, amount)
    heavy_load, usual = load_shares(amount, rows * top, reach, skew, True), load_shares(amount, rows * top, reach, skew, False)
    places = jnp.arange(amount)

    def named(sizes, rotation):
        used = int((sizes > 0).sum())
        fixed = max(1, used // 4)
        shifted = fixed + (places - fixed + rotation * (used - fixed)) % max(1, amount - fixed)
        return jnp.zeros((amount,), jnp.int32).at[sequence[jnp.where(places < fixed, places, shifted)]].set(jnp.asarray(sizes, jnp.int32))

    sizes = jnp.where(number % 4 == 0, named(heavy_load, number // 4), named(usual, number - number // 4 - 1))
    mixed = jax.random.permutation(jax.random.fold_in(own, 3), amount)
    giver, receiver = mixed[0:amount // 2 * 2:2], mixed[1:amount // 2 * 2:2]
    margin = jnp.minimum(sizes[giver] - 1, reach - sizes[receiver]) // 2
    margin = jnp.where((giver == sequence[0]) | (receiver == sequence[0]) | (sizes[receiver] == 0), 0, jnp.maximum(margin, 0))
    shifted = jax.random.randint(jax.random.fold_in(own, 4), (amount // 2,), 0, 1 << 20) % (margin + 1)
    sizes = sizes.at[giver].add(-shifted).at[receiver].add(shifted)
    members = jnp.searchsorted(jnp.cumsum(sizes), jnp.arange(rows * top), side="right").astype(jnp.int32)
    grid = members.reshape(top, rows).T
    grid = grid[jax.random.permutation(jax.random.fold_in(own, 1), rows)]
    rotation = jax.random.randint(jax.random.fold_in(own, 2), (rows, 1), 0, top)
    return jnp.take_along_axis(grid, (jnp.arange(top)[None, :] + rotation) % top, axis=1)


def load_shares(amount, total, reach, lean, full):
    weights = [(1 << 20) // math.isqrt(standing ** lean) + 1 for standing in range(1, amount + 1)]
    largest = reach if full else min(reach, max(-(-total // amount), total * weights[0] // sum(weights)))
    least = 1 if total - largest >= amount - 1 else 0
    counts, rest = [largest] + [least] * (amount - 1), total - largest - least * (amount - 1)
    while rest > 0:
        free = [i for i in range(1, amount) if counts[i] < largest] or [i for i in range(1, amount) if counts[i] < reach]
        whole, remaining = sum([weights[i] for i in free]), rest
        for i in free:
            more = min(reach - counts[i], max(1, remaining * weights[i] // whole), rest)
            counts[i] = counts[i] + more
            rest = rest - more
    return np.array(counts)


def normal_values(own_key, shape, deviation, reach, pieces=(), kind=jnp.bfloat16):
    values = deviation * jax.random.normal(own_key, shape, jnp.float32)
    if pieces:
        values = values * level_of(own_key, shape, pieces, -0.22, 0.18)
    return jnp.clip(values, -reach, reach).astype(kind)


def setup_inputs(seed: int = 0) -> dict:
    key_of = jax.random.split(jax.random.key(seed), 10)
    item_table = normal_values(key_of[0], (ITEMS, D), 1.0, 6.0, ((0, 128),))
    owner_keys = jax.random.split(jax.random.fold_in(key_of[1], 1), USERS * EVENTS // TOK_DEV)
    owner_turns = jax.random.permutation(jax.random.fold_in(key_of[1], 3), USERS * EVENTS // TOK_DEV)
    owner = jax.vmap(lambda own, number: deal_out(jax.random.fold_in(key_of[1], 2), own, number, TOK_DEV, OWNERS, 1, CAP, 1))(owner_keys, owner_turns).reshape((USERS, EVENTS, 1))
    item_row = touch_ends(jax.random.randint(key_of[2], (USERS, EVENTS), 0, ROWS_DEV), jax.random.fold_in(key_of[2], 1), 0, ROWS_DEV - 1).astype(jnp.int32)
    lengths = draw_lengths(jax.random.fold_in(key_of[9], 71), 0)
    gain_in = jnp.clip(1.0 + 0.1 * jax.random.normal(key_of[4], (D,), jnp.float32), 0.5, 1.5)
    gain_out = jnp.clip(1.0 + 0.1 * jax.random.normal(key_of[5], (D,), jnp.float32), 0.5, 1.5)
    w_in = normal_values(key_of[6], (D, 4 * D), D ** -0.5, 0.25)
    w_out = normal_values(key_of[7], (D, D), D ** -0.5, 0.25)
    out_grad = normal_values(key_of[8], (USERS, EVENTS, D), 1.0, 6.0, ((0, 16), (1, 8)))
    return {"item_table": item_table, "owner": owner, "item_row": item_row, "lengths": lengths, "gain_in": gain_in, "gain_out": gain_out, "w_in": w_in, "w_out": w_out, "out_grad": out_grad}


def layer_norm(rows, gain):
    mean = lax.optimization_barrier(jnp.mean(rows, -1, keepdims=True))
    centred = rows - mean
    variance = lax.optimization_barrier(jnp.mean(centred * centred, -1, keepdims=True))
    return centred * lax.rsqrt(variance + 1e-05) * gain

def slope(values):
    sigma = jax.nn.sigmoid(values)
    return sigma * (1.0 + values * (1.0 - sigma))

def split_heads(rows):
    return rows.reshape(rows.shape[0], HEADS, HEAD).astype(jnp.float32)

def scores_mask(queries, keys, query_pos, key_pos, length):
    scores = jnp.einsum('ihd,jhd->hij', split_heads(queries), split_heads(keys)) * HEAD ** (-0.5)
    allowed = (key_pos[None, :] <= query_pos[:, None]) & (key_pos[None, :] < length) & (query_pos[:, None] < length)
    return (scores, allowed.astype(jnp.float32)[None])

def attn_weights(scores, allowed):
    return (jax.nn.silu(scores) * allowed).astype(jnp.bfloat16)

def attend(queries, keys, values, query_pos, key_pos, length):
    scores, allowed = scores_mask(queries, keys, query_pos, key_pos, length)
    weights = attn_weights(scores, allowed)
    mixed = jnp.einsum('hij,jhd->ihd', weights.astype(jnp.float32), split_heads(values))
    return mixed.reshape(queries.shape[0], -1)

def query_grad(queries, keys, values, out_back, query_pos, key_pos, length):
    scores, allowed = scores_mask(queries, keys, query_pos, key_pos, length)
    pulled = jnp.einsum('ihd,jhd->hij', split_heads(out_back), split_heads(values))
    score_back = (pulled * slope(scores) * allowed).astype(jnp.bfloat16)
    result = jnp.einsum('hij,jhd->ihd', score_back.astype(jnp.float32), split_heads(keys)) * HEAD ** (-0.5)
    return result.reshape(queries.shape[0], -1)

def key_grads(queries, keys, values, out_back, query_pos, key_pos, length):
    scores, allowed = scores_mask(queries, keys, query_pos, key_pos, length)
    weights = attn_weights(scores, allowed)
    value_back = jnp.einsum('hij,ihd->jhd', weights.astype(jnp.float32), split_heads(out_back))
    pulled = jnp.einsum('ihd,jhd->hij', split_heads(out_back), split_heads(values))
    score_back = (pulled * slope(scores) * allowed).astype(jnp.bfloat16)
    key_back = jnp.einsum('hij,ihd->jhd', score_back.astype(jnp.float32), split_heads(queries)) * HEAD ** (-0.5)
    return (key_back.reshape(keys.shape[0], -1), value_back.reshape(keys.shape[0], -1))

def reference(item_table, owner, item_row, lengths, gain_in, gain_out, w_in, w_out, out_grad):
    idents = (owner[:, :, 0] * ROWS_DEV + item_row).astype(jnp.int32)
    size = 512 if EVENTS % 512 == 0 else EVENTS
    count = EVENTS // size
    positions = jnp.arange(EVENTS, dtype=jnp.int32)

    def one_user(inputs):
        ident_row, length, grad_row = inputs
        embed = jnp.take(item_table, ident_row, axis=0)
        x_rows = embed.astype(jnp.float32)
        live = (positions < length)[:, None]
        normed = layer_norm(x_rows, gain_in).astype(jnp.bfloat16)
        pre = jnp.dot(normed, w_in, preferred_element_type=jnp.float32)
        proj = jax.nn.silu(pre).astype(jnp.bfloat16)
        gate = proj[:, :D]
        values = proj[:, D:2 * D]
        queries = proj[:, 2 * D:3 * D]
        keys = proj[:, 3 * D:]

        def forward_block(block):
            start = (block * size).astype(jnp.int32)
            query_block = lax.dynamic_slice_in_dim(queries, start, size, 0)
            return attend(query_block, keys, values, start + jnp.arange(size, dtype=jnp.int32), positions, length)
        mixed = lax.map(forward_block, jnp.arange(count, dtype=jnp.int32)).reshape(EVENTS, D)

        def post(mixed_in, gate_in):
            return layer_norm(mixed_in, gain_out) * gate_in
        joined_full, pull_post = jax.vjp(post, mixed, gate.astype(jnp.float32))
        joined = joined_full.astype(jnp.bfloat16)
        output = jnp.dot(joined, w_out, preferred_element_type=jnp.float32) + x_rows
        hidden = (output * live.astype(jnp.float32)).astype(jnp.bfloat16)
        upstream = grad_row * live.astype(jnp.bfloat16)
        joined_grad = jnp.dot(upstream, w_out.T, preferred_element_type=jnp.float32)
        mixed_full, gate_back = pull_post(joined_grad)
        mixed_back = mixed_full.astype(jnp.bfloat16)

        def query_block_grad(block):
            start = (block * size).astype(jnp.int32)
            query_block = lax.dynamic_slice_in_dim(queries, start, size, 0)
            back_block = lax.dynamic_slice_in_dim(mixed_back, start, size, 0)
            return query_grad(query_block, keys, values, back_block, start + jnp.arange(size, dtype=jnp.int32), positions, length)
        query_back = lax.map(query_block_grad, jnp.arange(count, dtype=jnp.int32)).reshape(EVENTS, D)

        def key_block_grad(block):
            start = (block * size).astype(jnp.int32)
            key_block = lax.dynamic_slice_in_dim(keys, start, size, 0)
            value_block = lax.dynamic_slice_in_dim(values, start, size, 0)
            return key_grads(queries, key_block, value_block, mixed_back, positions, start + jnp.arange(size, dtype=jnp.int32), length)
        key_parts, value_parts = lax.map(key_block_grad, jnp.arange(count, dtype=jnp.int32))
        key_back = key_parts.reshape(EVENTS, D)
        value_back = value_parts.reshape(EVENTS, D)
        proj_back = jnp.concatenate([gate_back, value_back, query_back, key_back], axis=1)
        pre_back = (proj_back * slope(pre)).astype(jnp.bfloat16)
        normed_back = jnp.dot(pre_back, w_in.T, preferred_element_type=jnp.float32)
        _, pull_in = jax.vjp(lambda rows: layer_norm(rows, gain_in), x_rows)
        embed_grad = pull_in(normed_back)[0] + upstream.astype(jnp.float32)
        in_term = jnp.dot(normed.T, pre_back, preferred_element_type=jnp.float32)
        out_term = jnp.dot(joined.T, upstream, preferred_element_type=jnp.float32)
        return (hidden, embed_grad, in_term, out_term)
    hidden_out, embed_grads, in_terms, out_terms = lax.map(one_user, (idents, lengths, out_grad))
    table_grad = jnp.zeros((ITEMS, D), jnp.float32).at[idents.reshape(-1)].add(embed_grads.reshape(-1, D))
    factor = TOKENS ** (-0.5)
    w_in_grad = lax.optimization_barrier(jnp.sum(in_terms, axis=0)) * factor
    w_out_grad = lax.optimization_barrier(jnp.sum(out_terms, axis=0)) * factor
    return (hidden_out, table_grad, w_in_grad, w_out_grad)
```

```python
import functools

import jax
import jax.numpy as jnp
from jax import lax
from jax.experimental import pallas as pl
from jax.experimental.pallas import tpu as pltpu
from jax.sharding import PartitionSpec as P

HEADS = 4
HEAD = 128
TOK = 512
WIDTH = 512
TILE = 128
SCALE = HEAD ** (-0.5)
EPS = 1e-05
MESH = pl.DeviceIdType.MESH
BF = jnp.bfloat16
F32 = jnp.float32


def dot(a, b, ca=1, cb=0):
    return lax.dot_general(a, b, (((ca,), (cb,)), ((), ())), preferred_element_type=F32)


def landed(ref, sem):
    pltpu.make_async_copy(ref, ref, sem).wait()


def layer_kernel(
    factor,
    len_ref, x_ref, og_ref, gin_ref, gout_ref, w_in_ref, w_out_ref,
    hidden_ref, egrad_ref, interm_ref, outterm_ref,
    normed, normed_t, slope, gate, upstream, joined, jgrad, nback, pback,
    q_out, kv_out, q_in, kv_in, mix_out, mix_in, dm_out, dm_in,
    dq_acc, dkv_acc, part_out, part_in, dq_out, dkv_out, dq_in, dkv_in, m_acc,
    q_send, q_recv, kv_send, kv_recv, fwd_send, mix_send, mix_recv, dm_send, dm_recv,
    part_send, part_recv, dq_send, dq_recv, dkv_send, dkv_recv,
):
    s = lax.axis_index("seq")
    t = lax.axis_index("table")
    core = lax.rem(t, 2)
    base = t - core
    head = lax.rem(s, HEADS)
    user_core = s // HEADS
    sibling = base + 1 - core
    part_of_s = lax.rem((s + 1) // 2, 2)
    slot_of_s = s // 2

    barrier = pltpu.get_barrier_semaphore()
    me = s * 2 + core

    def greet(d, carry):
        other = lax.rem(me + d, 16)
        pl.semaphore_signal(
            barrier, inc=1, device_id=(other // 2, base + lax.rem(other, 2)), device_id_type=MESH
        )
        return carry

    lax.fori_loop(1, 16, greet, 0)
    pl.semaphore_wait(barrier, 15)

    def push(src, dst, send, recv, to_s, to_t):
        mine = jnp.logical_and(to_s == s, to_t == t)

        @pl.when(mine)
        def _():
            pltpu.make_async_copy(src, dst, recv).start()

        @pl.when(jnp.logical_not(mine))
        def _():
            pltpu.make_async_remote_copy(
                src_ref=src, dst_ref=dst, send_sem=send, recv_sem=recv,
                device_id=(to_s, to_t), device_id_type=MESH,
            ).start()

    def left(src, send, to_s, to_t):
        @pl.when(jnp.logical_not(jnp.logical_and(to_s == s, to_t == t)))
        def _():
            landed(src, send)

    def worker(h):
        return core * HEADS + h, base + part_of_s

    def mine_of(k):
        return 2 * k + lax.rem(k + core, 2)

    def other_of(k):
        return 2 * k + lax.rem(k + core + 1, 2)

    length = len_ref[0]

    def live_rows(start, count):
        pos = s * TOK + start + lax.broadcasted_iota(jnp.int32, (count, 1), 0)
        return (pos < length).astype(F32)

    def norm_tile(r, carry):
        rows = pl.ds(pl.multiple_of(r * TILE, TILE), TILE)
        x = x_ref[rows, :].astype(F32)
        mean = jnp.mean(x, -1, keepdims=True)
        cent = x - mean
        var = jnp.mean(cent * cent, -1, keepdims=True)
        normed[rows, :] = (cent * lax.rsqrt(var + EPS) * gin_ref[...]).astype(BF)
        return carry

    lax.fori_loop(0, TOK // TILE, norm_tile, 0)

    live = live_rows(0, TOK)

    def project(first, columns):
        pre = dot(normed[...], w_in_ref[:, pl.ds(first, columns)])
        half = 0.5 * pre
        th = jnp.tanh(half)
        slope[:, pl.ds(first, columns)] = 0.5 * (1.0 + th) * (1.0 + half - half * th)
        return half + half * th

    for h in range(HEADS):
        kv_out[h, :, :HEAD] = project(3 * WIDTH + h * HEAD, HEAD).astype(BF)
        kv_out[h, :, HEAD:] = (project(WIDTH + h * HEAD, HEAD) * live).astype(BF)
        to = worker(h)
        push(kv_out.at[h], kv_in.at[s], kv_send.at[h], kv_recv.at[s], *to)
        q_out[h] = project(2 * WIDTH + h * HEAD, HEAD).astype(BF)
        push(q_out.at[h], q_in.at[slot_of_s], q_send.at[h], q_recv.at[slot_of_s], *to)

    gate[:, :256] = project(0, 256).astype(BF)
    gate[:, 256:] = project(256, 256).astype(BF)
    upstream[...] = (og_ref[...].astype(F32) * live).astype(BF)
    jgrad[...] = dot(upstream[...], w_out_ref[...], 1, 1)
    normed_t[...] = normed[...].T
    dq_acc[...] = jnp.zeros_like(dq_acc)
    dkv_acc[...] = jnp.zeros_like(dkv_acc)

    def take(k):
        d = mine_of(k)
        landed(kv_in.at[d], kv_recv.at[d])
        pltpu.make_async_remote_copy(
            src_ref=kv_in.at[d], dst_ref=kv_in.at[d], send_sem=fwd_send.at[k], recv_sem=kv_recv.at[d],
            device_id=(s, sibling), device_id_type=MESH,
        ).start()

    row = lax.broadcasted_iota(jnp.int32, (TOK, TOK), 0)
    col = lax.broadcasted_iota(jnp.int32, (TOK, TOK), 1)

    def forward_pair(k, j, diagonal):
        half = dot(q_in[k], kv_in[j, :, :HEAD], 1, 1) * (0.5 * SCALE)
        w = half + half * jnp.tanh(half)
        if diagonal:
            w = jnp.where(col <= row, w, 0.0)
        return dot(w.astype(BF), kv_in[j, :, HEAD:])

    take(0)

    def forward(k, carry):
        i = mine_of(k)

        @pl.when(k < 3)
        def _():
            take(k + 1)

        landed(q_in.at[k], q_recv.at[k])
        o = other_of(k)
        landed(kv_in.at[o], kv_recv.at[o])
        m_acc[...] = forward_pair(k, i, True)

        def inner(j, c):
            m_acc[...] += forward_pair(k, j, False)
            return c

        lax.fori_loop(0, i, inner, 0)
        mix_out[k] = m_acc[...].astype(BF)
        push(mix_out.at[k], mix_in.at[head], mix_send.at[k], mix_recv.at[head], i, base + user_core)
        return carry

    lax.fori_loop(0, 4, forward, 0)

    for h in range(HEADS):
        landed(mix_in.at[h], mix_recv.at[h])

    def post_tile(r, carry):
        start = pl.multiple_of(r * TILE, TILE)
        rows = pl.ds(start, TILE)
        alive = live_rows(start, TILE)
        m = jnp.concatenate([mix_in[h, rows, :] for h in range(HEADS)], axis=1).astype(F32) * alive
        mean = jnp.mean(m, -1, keepdims=True)
        cent = m - mean
        var = jnp.mean(cent * cent, -1, keepdims=True)
        rstd = lax.rsqrt(var + EPS)
        n = cent * rstd
        ng = n * gout_ref[...]
        g = gate[rows, :].astype(F32)
        jg = jgrad[rows, :]
        joined[rows, :] = (ng * g).astype(BF)
        pback[rows, :WIDTH] = (jg * ng * slope[rows, :WIDTH]).astype(BF)
        dn = jg * g * gout_ref[...]
        dm = rstd * (dn - jnp.mean(dn, -1, keepdims=True) - n * jnp.mean(dn * n, -1, keepdims=True))
        dm = (dm * alive).astype(BF)
        for h in range(HEADS):
            dm_out[h, rows, :] = dm[:, h * HEAD : (h + 1) * HEAD]
        return carry

    lax.fori_loop(0, TOK // TILE, post_tile, 0)
    for h in range(HEADS):
        push(dm_out.at[h], dm_in.at[slot_of_s], dm_send.at[h], dm_recv.at[slot_of_s], *worker(h))

    hidden_ref[...] = ((dot(joined[...], w_out_ref[...]) + x_ref[...].astype(F32)) * live).astype(BF)
    outterm_ref[...] = dot(joined[...], upstream[...], 0, 0) * factor
    interm_ref[:, :WIDTH] = dot(normed_t[...], pback[:, :WIDTH]) * factor
    nback[...] = dot(pback[:, :WIDTH], w_in_ref[:, :WIDTH], 1, 1)

    for k in range(4):
        landed(dm_in.at[k], dm_recv.at[k])

    def backward_pair(k, j, diagonal):
        q, dm = q_in[k], dm_in[k]
        half = dot(kv_in[j, :, :HEAD], q, 1, 1) * (0.5 * SCALE)
        th = jnp.tanh(half)
        ht = half * th
        w = half + ht
        sb = dot(kv_in[j, :, HEAD:], dm, 1, 1) * ((0.5 + 0.5 * th) * (1.0 + half - ht))
        if diagonal:
            w = jnp.where(row <= col, w, 0.0)
            sb = jnp.where(row <= col, sb, 0.0)
        sb = sb.astype(BF)
        dkv_acc[j, :, HEAD:] += dot(w.astype(BF), dm)
        dkv_acc[j, :, :HEAD] += dot(sb, q)
        dq_acc[k] += dot(sb, kv_in[j, :, :HEAD], 0, 0)

    def finish(m):
        d = mine_of(m)
        landed(part_in.at[m], part_recv.at[m])
        total = dkv_acc[d] + part_in[m].astype(F32)
        dkv_out[m, :, :HEAD] = (total[:, :HEAD] * SCALE).astype(BF)
        dkv_out[m, :, HEAD:] = total[:, HEAD:].astype(BF)
        push(dkv_out.at[m], dkv_in.at[head], dkv_send.at[m], dkv_recv.at[head], d, base + user_core)

    def backward(m, carry):
        i = mine_of(m)

        def one(jj, c):
            j = 2 * m + jj

            @pl.when(i == j)
            def _():
                backward_pair(m, j, True)

            def inner(k, cc):
                backward_pair(k, j, False)
                return cc

            lax.fori_loop(jnp.where(i > j, m, m + 1), 4, inner, 0)
            return c

        lax.fori_loop(0, 2, one, 0)
        part_out[m] = dkv_acc[other_of(m)].astype(BF)
        pltpu.make_async_remote_copy(
            src_ref=part_out.at[m], dst_ref=part_in.at[m], send_sem=part_send.at[m], recv_sem=part_recv.at[m],
            device_id=(s, sibling), device_id_type=MESH,
        ).start()
        dq_out[m] = (dq_acc[m] * SCALE).astype(BF)
        push(dq_out.at[m], dq_in.at[head], dq_send.at[m], dq_recv.at[head], i, base + user_core)

        @pl.when(m > 0)
        def _():
            finish(m - 1)

        return carry

    lax.fori_loop(0, 4, backward, 0)
    finish(3)

    for h in range(HEADS):
        landed(dq_in.at[h], dq_recv.at[h])
        landed(dkv_in.at[h], dkv_recv.at[h])

    def back_tile(r, carry):
        start = pl.multiple_of(r * TILE, TILE)
        rows = pl.ds(start, TILE)
        alive = live_rows(start, TILE)
        for h in range(HEADS):
            for first, piece in (
                (WIDTH, dkv_in[h, rows, HEAD:].astype(F32) * alive),
                (2 * WIDTH, dq_in[h, rows, :].astype(F32)),
                (3 * WIDTH, dkv_in[h, rows, :HEAD].astype(F32)),
            ):
                c = first + h * HEAD
                pback[rows, c : c + HEAD] = (piece * slope[rows, c : c + HEAD]).astype(BF)
        nb = nback[rows, :] + dot(pback[rows, WIDTH:], w_in_ref[:, WIDTH:], 1, 1)
        x = x_ref[rows, :].astype(F32)
        mean = jnp.mean(x, -1, keepdims=True)
        cent = x - mean
        var = jnp.mean(cent * cent, -1, keepdims=True)
        rstd = lax.rsqrt(var + EPS)
        n = cent * rstd
        dn = nb * gin_ref[...]
        dx = rstd * (dn - jnp.mean(dn, -1, keepdims=True) - n * jnp.mean(dn * n, -1, keepdims=True))
        egrad_ref[rows, :] = (dx + upstream[rows, :].astype(F32)).astype(BF)
        return carry

    lax.fori_loop(0, TOK // TILE, back_tile, 0)

    def in_columns(c, carry):
        cols = pl.ds(pl.multiple_of(c * 256, 256), 256)
        interm_ref[:, cols] = dot(normed_t[...], pback[:, cols]) * factor
        return carry

    lax.fori_loop(2, 8, in_columns, 0)

    for h in range(HEADS):
        to = worker(h)
        left(kv_out.at[h], kv_send.at[h], *to)
        left(q_out.at[h], q_send.at[h], *to)
        left(dm_out.at[h], dm_send.at[h], *to)
        landed(kv_in.at[mine_of(h)], fwd_send.at[h])
        landed(part_out.at[h], part_send.at[h])
        back = (mine_of(h), base + user_core)
        left(mix_out.at[h], mix_send.at[h], *back)
        left(dq_out.at[h], dq_send.at[h], *back)
        left(dkv_out.at[h], dkv_send.at[h], *back)


def layer(length, embed, out_grad, gain_in, gain_out, w_in, w_out, factor):
    vm = pl.BlockSpec(memory_space=pltpu.VMEM)
    dma = pltpu.SemaphoreType.DMA

    def buf(*shape, dtype=BF):
        return pltpu.VMEM(shape, dtype)

    blocks = [
        buf(TOK, WIDTH), buf(WIDTH, TOK), buf(TOK, 4 * WIDTH, dtype=F32), buf(TOK, WIDTH), buf(TOK, WIDTH),
        buf(TOK, WIDTH), buf(TOK, WIDTH, dtype=F32), buf(TOK, WIDTH, dtype=F32), buf(TOK, 4 * WIDTH),
        buf(4, TOK, HEAD), buf(4, TOK, 2 * HEAD), buf(4, TOK, HEAD), buf(8, TOK, 2 * HEAD),
        buf(4, TOK, HEAD), buf(4, TOK, HEAD), buf(4, TOK, HEAD), buf(4, TOK, HEAD),
        buf(4, TOK, HEAD, dtype=F32), buf(8, TOK, 2 * HEAD, dtype=F32),
        buf(4, TOK, 2 * HEAD), buf(4, TOK, 2 * HEAD), buf(4, TOK, HEAD), buf(4, TOK, 2 * HEAD),
        buf(4, TOK, HEAD), buf(4, TOK, 2 * HEAD), buf(TOK, HEAD, dtype=F32),
    ]
    sems = [dma((n,)) for n in (4, 4, 4, 8, 4, 4, 4, 4, 4, 4, 4, 4, 4, 4, 4)]
    return pl.pallas_call(
        functools.partial(layer_kernel, factor),
        out_shape=(
            jax.ShapeDtypeStruct((TOK, WIDTH), BF),
            jax.ShapeDtypeStruct((TOK, WIDTH), BF),
            jax.ShapeDtypeStruct((WIDTH, 4 * WIDTH), F32),
            jax.ShapeDtypeStruct((WIDTH, WIDTH), F32),
        ),
        in_specs=[pl.BlockSpec(memory_space=pltpu.SMEM)] + [vm] * 6,
        out_specs=(vm,) * 4,
        scratch_shapes=blocks + sems,
        compiler_params=pltpu.CompilerParams(
            collective_id=0, has_side_effects=True, vmem_limit_bytes=56 * 1024 * 1024
        ),
        cost_estimate=pl.CostEstimate(flops=14 * 10**9, bytes_accessed=12 * 2**20, transcendentals=10**7),
    )(length, embed, out_grad, gain_in.reshape(1, -1), gain_out.reshape(1, -1), w_in, w_out)


def local(item_table, owner, item_row, lengths, gain_in, gain_out, w_in, w_out, out_grad):
    events_here = owner.shape[1]
    owners = lax.axis_size(("seq", "table"))
    slots = max(2, 2 * events_here // owners)
    width = w_out.shape[0]
    factor = (events_here * owners) ** (-0.5)
    target = owner[0, :, 0]
    wanted = item_row[0]
    chosen = (target[:, None] == jnp.arange(owners, dtype=jnp.int32)[None, :]).astype(jnp.int32)
    before = jnp.cumsum(chosen, axis=0) - chosen
    rank = jnp.sum(before * chosen, axis=1)
    slot = target * slots + rank
    request = jnp.full((owners * slots,), -1, jnp.int32).at[slot].set(wanted).reshape(owners, slots)
    asked = lax.all_to_all(request, ("seq", "table"), split_axis=0, concat_axis=0, tiled=True)
    found = jnp.take(item_table, jnp.maximum(asked, 0), axis=0)
    found = jnp.where((asked >= 0)[:, :, None], found, jnp.zeros_like(found))
    fetched = lax.all_to_all(found, ("seq", "table"), split_axis=0, concat_axis=0, tiled=True)
    embed = jnp.take(fetched.reshape(owners * slots, width), slot, axis=0)
    hidden, embed_grad, in_term, out_term = layer(
        lengths, embed, out_grad[0], gain_in, gain_out, w_in, w_out, factor
    )
    outgoing = jnp.zeros((owners * slots, width), jnp.bfloat16).at[slot].set(embed_grad).reshape(owners, slots, width)
    incoming = lax.all_to_all(outgoing, ("seq", "table"), split_axis=0, concat_axis=0, tiled=True)
    table_grad = (
        jnp.zeros((item_table.shape[0], width), jnp.float32)
        .at[jnp.maximum(asked, 0).reshape(-1)]
        .add(incoming.reshape(-1, width).astype(jnp.float32))
    )
    w_in_grad, w_out_grad = lax.psum((in_term, out_term), ("seq", "table"))
    return (hidden[None], table_grad, w_in_grad, w_out_grad)


def solution(mesh):
    placed = (
        P(("seq", "table"), None),
        P("table", "seq", None),
        P("table", "seq"),
        P("table"),
        P(),
        P(),
        P(),
        P(),
        P("table", "seq", None),
    )
    return jax.shard_map(
        local,
        mesh=mesh,
        in_specs=placed,
        out_specs=(P("table", "seq", None), P(("seq", "table"), None), P(), P()),
        check_vma=False,
    )
```

```python
import functools

import jax
import jax.numpy as jnp
from jax import lax
from jax.experimental import pallas as pl
from jax.experimental.pallas import tpu as pltpu
from jax.sharding import PartitionSpec as P

HEADS = 4
HEAD = 128
TOK = 512
WIDTH = 512
TILE = 128
SCALE = HEAD ** (-0.5)
EPS = 1e-05
MESH = pl.DeviceIdType.MESH
BF = jnp.bfloat16
F32 = jnp.float32


def dot(a, b, ca=1, cb=0):
    return lax.dot_general(a, b, (((ca,), (cb,)), ((), ())), preferred_element_type=F32)


def landed(ref, sem):
    pltpu.make_async_copy(ref, ref, sem).wait()


def layer_kernel(
    factor,
    len_ref, x_ref, og_ref, gin_ref, gout_ref, w_in_ref, w_out_ref,
    hidden_ref, egrad_ref, terms_ref,
    normed, normed_t, slope, gate, upstream, joined, jgrad, nback, pback,
    q_out, kv_out, q_in, kv_in, mix_out, mix_in, dm_out, dm_in,
    dq_acc, dkv_acc, part_out, part_in, dq_out, dkv_out, dq_in, dkv_in, m_acc,
    q_send, q_recv, kv_send, kv_recv, fwd_send, mix_send, mix_recv, dm_send, dm_recv,
    part_send, part_recv, dq_send, dq_recv, dkv_send, dkv_recv,
):
    s = lax.axis_index("seq")
    t = lax.axis_index("table")
    core = lax.rem(t, 2)
    base = t - core
    head = lax.rem(s, HEADS)
    user_core = s // HEADS
    sibling = base + 1 - core
    part_of_s = lax.rem((s + 1) // 2, 2)
    slot_of_s = s // 2

    barrier = pltpu.get_barrier_semaphore()
    me = s * 2 + core

    def greet(d, carry):
        other = lax.rem(me + d, 16)
        pl.semaphore_signal(
            barrier, inc=1, device_id=(other // 2, base + lax.rem(other, 2)), device_id_type=MESH
        )
        return carry

    lax.fori_loop(1, 16, greet, 0)
    pl.semaphore_wait(barrier, 15)

    def push(src, dst, send, recv, to_s, to_t):
        mine = jnp.logical_and(to_s == s, to_t == t)

        @pl.when(mine)
        def _():
            pltpu.make_async_copy(src, dst, recv).start()

        @pl.when(jnp.logical_not(mine))
        def _():
            pltpu.make_async_remote_copy(
                src_ref=src, dst_ref=dst, send_sem=send, recv_sem=recv,
                device_id=(to_s, to_t), device_id_type=MESH,
            ).start()

    def left(src, send, to_s, to_t):
        @pl.when(jnp.logical_not(jnp.logical_and(to_s == s, to_t == t)))
        def _():
            landed(src, send)

    def worker(h):
        return core * HEADS + h, base + part_of_s

    def mine_of(k):
        return 2 * k + lax.rem(k + core, 2)

    def other_of(k):
        return 2 * k + lax.rem(k + core + 1, 2)

    length = len_ref[0]

    def live_rows(start, count):
        pos = s * TOK + start + lax.broadcasted_iota(jnp.int32, (count, 1), 0)
        return (pos < length).astype(F32)

    def norm_tile(r, carry):
        rows = pl.ds(pl.multiple_of(r * TILE, TILE), TILE)
        x = x_ref[rows, :].astype(F32)
        mean = jnp.mean(x, -1, keepdims=True)
        cent = x - mean
        var = jnp.mean(cent * cent, -1, keepdims=True)
        normed[rows, :] = (cent * lax.rsqrt(var + EPS) * gin_ref[...]).astype(BF)
        return carry

    lax.fori_loop(0, TOK // TILE, norm_tile, 0)

    live = live_rows(0, TOK)

    def project(first, columns):
        pre = dot(normed[...], w_in_ref[:, pl.ds(first, columns)])
        half = 0.5 * pre
        th = jnp.tanh(half)
        slope[:, pl.ds(first, columns)] = 0.5 * (1.0 + th) * (1.0 + half - half * th)
        return half + half * th

    for h in range(HEADS):
        kv_out[h, :, :HEAD] = project(3 * WIDTH + h * HEAD, HEAD).astype(BF)
        kv_out[h, :, HEAD:] = (project(WIDTH + h * HEAD, HEAD) * live).astype(BF)
        to = worker(h)
        push(kv_out.at[h], kv_in.at[s], kv_send.at[h], kv_recv.at[s], *to)
        q_out[h] = project(2 * WIDTH + h * HEAD, HEAD).astype(BF)
        push(q_out.at[h], q_in.at[slot_of_s], q_send.at[h], q_recv.at[slot_of_s], *to)

    gate[:, :256] = project(0, 256).astype(BF)
    gate[:, 256:] = project(256, 256).astype(BF)
    upstream[...] = (og_ref[...].astype(F32) * live).astype(BF)
    jgrad[...] = dot(upstream[...], w_out_ref[...], 1, 1)
    normed_t[...] = normed[...].T
    dq_acc[...] = jnp.zeros_like(dq_acc)
    dkv_acc[...] = jnp.zeros_like(dkv_acc)

    def take(k):
        d = mine_of(k)
        landed(kv_in.at[d], kv_recv.at[d])
        pltpu.make_async_remote_copy(
            src_ref=kv_in.at[d], dst_ref=kv_in.at[d], send_sem=fwd_send.at[k], recv_sem=kv_recv.at[d],
            device_id=(s, sibling), device_id_type=MESH,
        ).start()

    row = lax.broadcasted_iota(jnp.int32, (TOK, TOK), 0)
    col = lax.broadcasted_iota(jnp.int32, (TOK, TOK), 1)

    def forward_pair(k, j, diagonal):
        half = dot(q_in[k], kv_in[j, :, :HEAD], 1, 1) * (0.5 * SCALE)
        w = half + half * jnp.tanh(half)
        if diagonal:
            w = jnp.where(col <= row, w, 0.0)
        return dot(w.astype(BF), kv_in[j, :, HEAD:])

    take(0)

    def forward(k, carry):
        i = mine_of(k)

        @pl.when(k < 3)
        def _():
            take(k + 1)

        landed(q_in.at[k], q_recv.at[k])
        o = other_of(k)
        landed(kv_in.at[o], kv_recv.at[o])
        m_acc[...] = forward_pair(k, i, True)

        def inner(j, c):
            m_acc[...] += forward_pair(k, j, False)
            return c

        lax.fori_loop(0, i, inner, 0)
        m = m_acc[...]
        shift = jnp.mean(m, -1, keepdims=True).astype(BF).astype(F32)
        mix_out[k, :TOK, :] = (m - shift).astype(BF)
        wide = jnp.broadcast_to(shift, (TOK, HEAD))
        lines = jnp.zeros((16, HEAD), F32)
        line = lax.broadcasted_iota(jnp.int32, (16, HEAD), 0)
        for b in range(TOK // HEAD):
            lines += jnp.where(line == b, wide[b * HEAD : (b + 1) * HEAD].T[:16], 0.0)
        mix_out[k, TOK:, :] = lines.astype(BF)
        push(mix_out.at[k], mix_in.at[head], mix_send.at[k], mix_recv.at[head], i, base + user_core)
        return carry

    lax.fori_loop(0, 4, forward, 0)

    for h in range(HEADS):
        landed(mix_in.at[h], mix_recv.at[h])

    def post_tile(r, carry):
        start = pl.multiple_of(r * TILE, TILE)
        rows = pl.ds(start, TILE)
        alive = live_rows(start, TILE)
        pick = (lax.broadcasted_iota(jnp.int32, (16, HEAD), 0) == r).astype(F32).astype(BF)
        m = jnp.concatenate(
            [mix_in[h, rows, :].astype(F32) + dot(mix_in[h, TOK:, :], pick, 0, 0) for h in range(HEADS)], axis=1
        ) * alive
        mean = jnp.mean(m, -1, keepdims=True)
        cent = m - mean
        var = jnp.mean(cent * cent, -1, keepdims=True)
        rstd = lax.rsqrt(var + EPS)
        n = cent * rstd
        ng = n * gout_ref[...]
        g = gate[rows, :].astype(F32)
        jg = jgrad[rows, :]
        joined[rows, :] = (ng * g).astype(BF)
        pback[rows, :WIDTH] = (jg * ng * slope[rows, :WIDTH]).astype(BF)
        dn = jg * g * gout_ref[...]
        dm = rstd * (dn - jnp.mean(dn, -1, keepdims=True) - n * jnp.mean(dn * n, -1, keepdims=True))
        dm = (dm * alive).astype(BF)
        for h in range(HEADS):
            dm_out[h, rows, :] = dm[:, h * HEAD : (h + 1) * HEAD]
        return carry

    lax.fori_loop(0, TOK // TILE, post_tile, 0)
    for h in range(HEADS):
        push(dm_out.at[h], dm_in.at[slot_of_s], dm_send.at[h], dm_recv.at[slot_of_s], *worker(h))

    hidden_ref[...] = ((dot(joined[...], w_out_ref[...]) + x_ref[...].astype(F32)) * live).astype(BF)
    terms_ref[4] = (dot(joined[...], upstream[...], 0, 0) * factor).astype(BF)
    terms_ref[0] = (dot(normed_t[...], pback[:, :WIDTH]) * factor).astype(BF)
    nback[...] = dot(pback[:, :WIDTH], w_in_ref[:, :WIDTH], 1, 1)

    for k in range(4):
        landed(dm_in.at[k], dm_recv.at[k])

    def backward_pair(k, j, diagonal):
        q, dm = q_in[k], dm_in[k]
        half = dot(kv_in[j, :, :HEAD], q, 1, 1) * (0.5 * SCALE)
        th = jnp.tanh(half)
        ht = half * th
        w = half + ht
        sb = dot(kv_in[j, :, HEAD:], dm, 1, 1) * ((0.5 + 0.5 * th) * (1.0 + half - ht))
        if diagonal:
            w = jnp.where(row <= col, w, 0.0)
            sb = jnp.where(row <= col, sb, 0.0)
        sb = sb.astype(BF)
        dkv_acc[j, :, HEAD:] += dot(w.astype(BF), dm)
        dkv_acc[j, :, :HEAD] += dot(sb, q)
        dq_acc[k] += dot(sb, kv_in[j, :, :HEAD], 0, 0)

    def finish(m):
        d = mine_of(m)
        landed(part_in.at[m], part_recv.at[m])
        total = dkv_acc[d] + part_in[m].astype(F32)
        dkv_out[m, :, :HEAD] = (total[:, :HEAD] * SCALE).astype(BF)
        dkv_out[m, :, HEAD:] = total[:, HEAD:].astype(BF)
        push(dkv_out.at[m], dkv_in.at[head], dkv_send.at[m], dkv_recv.at[head], d, base + user_core)

    def backward(m, carry):
        i = mine_of(m)

        def one(jj, c):
            j = 2 * m + jj

            @pl.when(i == j)
            def _():
                backward_pair(m, j, True)

            def inner(k, cc):
                backward_pair(k, j, False)
                return cc

            lax.fori_loop(jnp.where(i > j, m, m + 1), 4, inner, 0)
            return c

        lax.fori_loop(0, 2, one, 0)
        part_out[m] = dkv_acc[other_of(m)].astype(BF)
        pltpu.make_async_remote_copy(
            src_ref=part_out.at[m], dst_ref=part_in.at[m], send_sem=part_send.at[m], recv_sem=part_recv.at[m],
            device_id=(s, sibling), device_id_type=MESH,
        ).start()
        dq_out[m] = (dq_acc[m] * SCALE).astype(BF)
        push(dq_out.at[m], dq_in.at[head], dq_send.at[m], dq_recv.at[head], i, base + user_core)

        @pl.when(m > 0)
        def _():
            finish(m - 1)

        return carry

    lax.fori_loop(0, 4, backward, 0)
    finish(3)

    for h in range(HEADS):
        landed(dq_in.at[h], dq_recv.at[h])
        landed(dkv_in.at[h], dkv_recv.at[h])

    def back_tile(r, carry):
        start = pl.multiple_of(r * TILE, TILE)
        rows = pl.ds(start, TILE)
        alive = live_rows(start, TILE)
        for h in range(HEADS):
            for first, piece in (
                (WIDTH, dkv_in[h, rows, HEAD:].astype(F32) * alive),
                (2 * WIDTH, dq_in[h, rows, :].astype(F32)),
                (3 * WIDTH, dkv_in[h, rows, :HEAD].astype(F32)),
            ):
                c = first + h * HEAD
                pback[rows, c : c + HEAD] = (piece * slope[rows, c : c + HEAD]).astype(BF)
        nb = nback[rows, :] + dot(pback[rows, WIDTH:], w_in_ref[:, WIDTH:], 1, 1)
        x = x_ref[rows, :].astype(F32)
        mean = jnp.mean(x, -1, keepdims=True)
        cent = x - mean
        var = jnp.mean(cent * cent, -1, keepdims=True)
        rstd = lax.rsqrt(var + EPS)
        n = cent * rstd
        dn = nb * gin_ref[...]
        dx = rstd * (dn - jnp.mean(dn, -1, keepdims=True) - n * jnp.mean(dn * n, -1, keepdims=True))
        egrad_ref[rows, :] = (dx + upstream[rows, :].astype(F32)).astype(BF)
        return carry

    lax.fori_loop(0, TOK // TILE, back_tile, 0)

    def in_columns(c, carry):
        cols = pl.ds(pl.multiple_of(c * WIDTH, WIDTH), WIDTH)
        terms_ref[c] = (dot(normed_t[...], pback[:, cols]) * factor).astype(BF)
        return carry

    lax.fori_loop(1, 4, in_columns, 0)

    for h in range(HEADS):
        to = worker(h)
        left(kv_out.at[h], kv_send.at[h], *to)
        left(q_out.at[h], q_send.at[h], *to)
        left(dm_out.at[h], dm_send.at[h], *to)
        landed(kv_in.at[mine_of(h)], fwd_send.at[h])
        landed(part_out.at[h], part_send.at[h])
        back = (mine_of(h), base + user_core)
        left(mix_out.at[h], mix_send.at[h], *back)
        left(dq_out.at[h], dq_send.at[h], *back)
        left(dkv_out.at[h], dkv_send.at[h], *back)


def layer(length, embed, out_grad, gain_in, gain_out, w_in, w_out, factor):
    vm = pl.BlockSpec(memory_space=pltpu.VMEM)
    dma = pltpu.SemaphoreType.DMA

    def buf(*shape, dtype=BF):
        return pltpu.VMEM(shape, dtype)

    blocks = [
        buf(TOK, WIDTH), buf(WIDTH, TOK), buf(TOK, 4 * WIDTH, dtype=F32), buf(TOK, WIDTH), buf(TOK, WIDTH),
        buf(TOK, WIDTH), buf(TOK, WIDTH, dtype=F32), buf(TOK, WIDTH, dtype=F32), buf(TOK, 4 * WIDTH),
        buf(4, TOK, HEAD), buf(4, TOK, 2 * HEAD), buf(4, TOK, HEAD), buf(8, TOK, 2 * HEAD),
        buf(4, TOK + 16, HEAD), buf(4, TOK + 16, HEAD), buf(4, TOK, HEAD), buf(4, TOK, HEAD),
        buf(4, TOK, HEAD, dtype=F32), buf(8, TOK, 2 * HEAD, dtype=F32),
        buf(4, TOK, 2 * HEAD), buf(4, TOK, 2 * HEAD), buf(4, TOK, HEAD), buf(4, TOK, 2 * HEAD),
        buf(4, TOK, HEAD), buf(4, TOK, 2 * HEAD), buf(TOK, HEAD, dtype=F32),
    ]
    sems = [dma((n,)) for n in (4, 4, 4, 8, 4, 4, 4, 4, 4, 4, 4, 4, 4, 4, 4)]
    return pl.pallas_call(
        functools.partial(layer_kernel, factor),
        out_shape=(
            jax.ShapeDtypeStruct((TOK, WIDTH), BF),
            jax.ShapeDtypeStruct((TOK, WIDTH), BF),
            jax.ShapeDtypeStruct((5, WIDTH, WIDTH), BF),
        ),
        in_specs=[pl.BlockSpec(memory_space=pltpu.SMEM)] + [vm] * 6,
        out_specs=(vm,) * 3,
        scratch_shapes=blocks + sems,
        compiler_params=pltpu.CompilerParams(
            collective_id=0, has_side_effects=True, vmem_limit_bytes=56 * 1024 * 1024
        ),
        cost_estimate=pl.CostEstimate(flops=14 * 10**9, bytes_accessed=12 * 2**20, transcendentals=10**7),
    )(length, embed, out_grad, gain_in.reshape(1, -1), gain_out.reshape(1, -1), w_in, w_out)


OWNERS = 128
SLOTS = 8
ROWS = 2048


def greet_all(s, t):
    barrier = pltpu.get_barrier_semaphore()
    me = s * 16 + t

    def greet(d, carry):
        other = lax.rem(me + d, OWNERS)
        pl.semaphore_signal(
            barrier, inc=1, device_id=(other // 16, lax.rem(other, 16)), device_id_type=MESH
        )
        return carry

    lax.fori_loop(1, OWNERS, greet, 0)
    pl.semaphore_wait(barrier, OWNERS - 1)


def send_rows(src, dst, send, recv, s, t, to_s, to_t, take, place):
    mine = jnp.logical_and(to_s == s, to_t == t)

    @pl.when(mine)
    def _():
        pltpu.make_async_copy(src.at[take], dst.at[place], recv).start()

    @pl.when(jnp.logical_not(mine))
    def _():
        pltpu.make_async_remote_copy(
            src_ref=src.at[take], dst_ref=dst.at[place], send_sem=send, recv_sem=recv,
            device_id=(to_s, to_t), device_id_type=MESH,
        ).start()


def sixteen(index):
    return pl.ds(pl.multiple_of(index * 16, 16), 16)


def spread(src, dst, send, recv, s, t, to_s):
    def one(p, carry):
        to_t = lax.rem(t + p, 16)
        send_rows(src, dst, send, recv, s, t, to_s, to_t, sixteen(to_s * 16 + to_t), sixteen(s * 16 + t))
        return carry

    lax.fori_loop(0, 16, one, 0)


def front_kernel(
    owner_ref, row_ref, table_ref, embed_ref, slot_ref, asked_ref,
    req_out, req_in, asked_col, found, fetched, req_send, req_recv, row_send, row_recv,
):
    s = lax.axis_index("seq")
    t = lax.axis_index("table")
    me = s * 16 + t
    greet_all(s, t)

    target = owner_ref[...]
    lane = lax.broadcasted_iota(jnp.int32, (TOK, OWNERS), 1)
    chosen_mask = lane == target
    chosen = jnp.where(chosen_mask, 1.0, 0.0).astype(BF)
    below = jnp.where(
        lax.broadcasted_iota(jnp.int32, (TOK, TOK), 1) < lax.broadcasted_iota(jnp.int32, (TOK, TOK), 0), 1.0, 0.0
    ).astype(BF)
    before = dot(below, chosen)
    rank = jnp.sum(jnp.where(chosen_mask, before, 0.0), axis=1, keepdims=True).astype(jnp.int32)
    value = row_ref[...] + 1
    high = (value >> 7).astype(F32)
    low = (value & 127).astype(F32)
    message = jnp.where(lane == rank, high, 0.0) + jnp.where(lane == rank + SLOTS, low, 0.0)
    req_out[:, 0, :] = dot(chosen, message.astype(BF), 0, 0)

    def ask(p, carry):
        other = lax.rem(me + p, OWNERS)
        send_rows(
            req_out, req_in, req_send, req_recv, s, t, other // 16, lax.rem(other, 16), other, me
        )
        return carry

    lax.fori_loop(0, OWNERS, ask, 0)

    place = target * 16 + rank
    slot_ref[...] = jnp.broadcast_to(place.astype(F32), (TOK, 128)).T[:8]

    landed(req_in, req_recv)
    number = lax.broadcasted_iota(jnp.int32, (OWNERS * SLOTS, OWNERS), 0)
    lane_s = lax.broadcasted_iota(jnp.int32, (OWNERS * SLOTS, OWNERS), 1)
    expand = jnp.where((number >> 3) == lane_s, 1.0, 0.0).astype(BF)
    values = dot(expand, req_in[:, 0, :].astype(BF))
    own = number & 7
    asked = (
        jnp.sum(
            jnp.where(lane_s == own, values * 128.0, 0.0) + jnp.where(lane_s == own + SLOTS, values, 0.0),
            axis=1,
            keepdims=True,
        )
        - 1.0
    )
    wide = jnp.broadcast_to(asked, (OWNERS * SLOTS, 128))
    asked_col[...] = wide
    asked_ref[...] = wide.T[:8]

    def gather(p, carry):
        q = lax.rem(s + p, 8)
        column = asked_col[pl.ds(pl.multiple_of(q * 128, 128), 128), :][:, :1].astype(jnp.int32)
        hit = lax.broadcasted_iota(jnp.int32, (128, ROWS), 1) == column
        rows = dot(jnp.where(hit, 1.0, 0.0).astype(BF), table_ref[...])
        both = jnp.concatenate(
            [rows[:, :256].reshape(16, SLOTS, 256), rows[:, 256:].reshape(16, SLOTS, 256)], axis=1
        )
        found[pl.ds(pl.multiple_of(q * 256, 256), 256), :] = both.reshape(256, 256).astype(BF)
        spread(found, fetched, row_send, row_recv, s, t, q)
        return carry

    lax.fori_loop(0, 8, gather, 0)
    landed(fetched, row_recv)
    for r in range(TOK // TILE):
        rows = slice(r * TILE, (r + 1) * TILE)
        at = lax.broadcasted_iota(jnp.int32, (TILE, ROWS), 1)
        first = jnp.where(at == place[rows], 1.0, 0.0).astype(BF)
        second = jnp.where(at == place[rows] + SLOTS, 1.0, 0.0).astype(BF)
        embed_ref[rows, :256] = dot(first, fetched[...]).astype(BF)
        embed_ref[rows, 256:] = dot(second, fetched[...]).astype(BF)
    landed(req_out.at[pl.ds(0, OWNERS - 1)], req_send)
    landed(found.at[pl.ds(0, (OWNERS - 1) * 16)], row_send)


def front(owner, item_row, item_table):
    vm = pl.BlockSpec(memory_space=pltpu.VMEM)
    dma = pltpu.SemaphoreType.DMA
    return pl.pallas_call(
        front_kernel,
        out_shape=(
            jax.ShapeDtypeStruct((TOK, WIDTH), BF),
            jax.ShapeDtypeStruct((8, TOK), F32),
            jax.ShapeDtypeStruct((8, OWNERS * SLOTS), F32),
        ),
        in_specs=[vm] * 3,
        out_specs=(vm,) * 3,
        scratch_shapes=[
            pltpu.VMEM((OWNERS, 1, 128), F32), pltpu.VMEM((OWNERS, 1, 128), F32),
            pltpu.VMEM((OWNERS * SLOTS, 128), F32),
            pltpu.VMEM((ROWS, 256), BF), pltpu.VMEM((ROWS, 256), BF),
            dma, dma, dma, dma,
        ],
        compiler_params=pltpu.CompilerParams(
            collective_id=1, has_side_effects=True, vmem_limit_bytes=48 * 1024 * 1024
        ),
    )(owner, item_row, item_table)


ORDERS = ("xyz", "yzx", "zxy", "xzy", "yxz")


def tail_kernel(
    egrad_ref, slot_ref, terms_ref, incoming_ref, sums_ref,
    outgoing, r0, a1, r1, a2, r2, a3, r3,
    row_send, row_recv, s0, v0, s1, v1, s2, v2, s3, v3, s4, v4, s5, v5, s6, v6, s7, v7,
):
    s = lax.axis_index("seq")
    t = lax.axis_index("table")
    core = lax.rem(t, 2)
    x, z = lax.rem(s, 4), t // 4
    y = lax.rem(t // 2, 2) * 2 + s // 4
    sibling = t + 1 - 2 * core
    greet_all(s, t)

    place = {"x": x, "y": y, "z": z}

    def partner(axis, d):
        other = lax.rem(place[axis] + d, 4)
        if axis == "x":
            return other, s - x + other, t
        if axis == "y":
            return other, lax.rem(other, 2) * 4 + x, z * 4 + (other // 2) * 2 + core
        return other, s, other * 4 + lax.rem(t, 4)

    def ship(src, dst, send, recv, to_s, to_t):
        pltpu.make_async_remote_copy(
            src_ref=src, dst_ref=dst, send_sem=send, recv_sem=recv,
            device_id=(to_s, to_t), device_id_type=MESH,
        ).start()

    units = range(len(ORDERS))
    half = pl.ds(pl.multiple_of(core * 256, 256), 256)
    other_half = pl.ds(pl.multiple_of(256 - core * 256, 256), 256)
    for u in units:
        ship(terms_ref.at[u, other_half], r0.at[u], s0.at[u], v0.at[u], s, sibling)

    slot = slot_ref[...][:1].astype(jnp.int32)

    def scatter(p, carry):
        q = lax.rem(s + p, 8)
        at = lax.broadcasted_iota(jnp.int32, (256, TOK), 0) + q * 256
        first = jnp.where(at == slot, 1.0, 0.0).astype(BF)
        second = jnp.where(at == slot + SLOTS, 1.0, 0.0).astype(BF)
        outgoing[pl.ds(pl.multiple_of(q * 256, 256), 256), :] = (
            dot(first, egrad_ref[:, :256]) + dot(second, egrad_ref[:, 256:])
        ).astype(BF)
        spread(outgoing, incoming_ref, row_send, row_recv, s, t, q)
        return carry

    lax.fori_loop(0, 8, scatter, 0)

    def block(axis, size):
        return pl.ds(pl.multiple_of(place[axis] * size, size), size)

    def block_of(index, size):
        return pl.ds(pl.multiple_of(index * size, size), size)

    for u in units:
        landed(r0.at[u], v0.at[u])
        a1[u] = (terms_ref[u, half, :].astype(F32) + r0[u].astype(F32)).astype(BF)
        for d in range(1, 4):
            other, to_s, to_t = partner(ORDERS[u][0], d)
            ship(a1.at[u, block_of(other, 64)], r1.at[u, d - 1], s1.at[u, d - 1], v1.at[u, d - 1], to_s, to_t)
    for u in units:
        total = a1[u, block(ORDERS[u][0], 64), :].astype(F32)
        for d in range(1, 4):
            landed(r1.at[u, d - 1], v1.at[u, d - 1])
            total += r1[u, d - 1].astype(F32)
        a2[u] = total.astype(BF)
        for d in range(1, 4):
            other, to_s, to_t = partner(ORDERS[u][1], d)
            ship(a2.at[u, block_of(other, 16)], r2.at[u, d - 1], s2.at[u, d - 1], v2.at[u, d - 1], to_s, to_t)
    for u in units:
        total = a2[u, block(ORDERS[u][1], 16), :].astype(F32)
        for d in range(1, 4):
            landed(r2.at[u, d - 1], v2.at[u, d - 1])
            total += r2[u, d - 1].astype(F32)
        a3[u] = total.astype(BF)
        for d in range(1, 4):
            other, to_s, to_t = partner(ORDERS[u][2], d)
            ship(
                a3.at[u, :, block_of(other, 128)], r3.at[u, d - 1], s3.at[u, d - 1], v3.at[u, d - 1], to_s, to_t
            )

    def spot(u, first, second, third):
        return sums_ref.at[u, pl.ds(pl.multiple_of(core * 256 + first * 64 + second * 16, 16), 16), block_of(third, 128)]

    def lines(u, first, second):
        return sums_ref.at[u, pl.ds(pl.multiple_of(core * 256 + first * 64 + second * 16, 16), 16)]

    def quarter(u, first):
        return sums_ref.at[u, pl.ds(pl.multiple_of(core * 256 + first * 64, 64), 64)]

    def before(axis, d):
        return lax.rem(place[axis] + 4 - d, 4)

    for u in units:
        one, two, three = ORDERS[u]
        total = a3[u, :, block(three, 128)].astype(F32)
        for d in range(1, 4):
            landed(r3.at[u, d - 1], v3.at[u, d - 1])
            total += r3[u, d - 1].astype(F32)
        mine = spot(u, place[one], place[two], place[three])
        mine[...] = total.astype(BF)
        for d in range(1, 4):
            _, to_s, to_t = partner(three, d)
            ship(mine, mine, s4.at[u, d - 1], v4.at[u, d - 1], to_s, to_t)
    for u in units:
        one, two, three = ORDERS[u]
        for d in range(1, 4):
            landed(spot(u, place[one], place[two], before(three, d)), v4.at[u, d - 1])
        mine = lines(u, place[one], place[two])
        for d in range(1, 4):
            _, to_s, to_t = partner(two, d)
            ship(mine, mine, s5.at[u, d - 1], v5.at[u, d - 1], to_s, to_t)
    for u in units:
        one, two, three = ORDERS[u]
        for d in range(1, 4):
            landed(lines(u, place[one], before(two, d)), v5.at[u, d - 1])
        mine = quarter(u, place[one])
        for d in range(1, 4):
            _, to_s, to_t = partner(one, d)
            ship(mine, mine, s6.at[u, d - 1], v6.at[u, d - 1], to_s, to_t)
    for u in units:
        one, two, three = ORDERS[u]
        for d in range(1, 4):
            landed(quarter(u, before(one, d)), v6.at[u, d - 1])
        ship(sums_ref.at[u, half], sums_ref.at[u, half], s7.at[u], v7.at[u], s, sibling)
    for u in units:
        landed(sums_ref.at[u, other_half], v7.at[u])

    landed(incoming_ref, row_recv)
    landed(outgoing.at[pl.ds(0, (OWNERS - 1) * 16)], row_send)
    for u in units:
        one, two, three = ORDERS[u]
        landed(terms_ref.at[u, other_half], s0.at[u])
        landed(sums_ref.at[u, half], s7.at[u])
        for d in range(3):
            landed(r1.at[u, d], s1.at[u, d])
            landed(r2.at[u, d], s2.at[u, d])
            landed(r3.at[u, d], s3.at[u, d])
            landed(spot(u, place[one], place[two], place[three]), s4.at[u, d])
            landed(lines(u, place[one], place[two]), s5.at[u, d])
            landed(quarter(u, place[one]), s6.at[u, d])


def tail(embed_grad, slots, terms):
    vm = pl.BlockSpec(memory_space=pltpu.VMEM)
    dma = pltpu.SemaphoreType.DMA
    n = len(ORDERS)
    one, three = dma((n,)), dma((n, 3))

    def buf(*shape):
        return pltpu.VMEM(shape, BF)

    return pl.pallas_call(
        tail_kernel,
        out_shape=(
            jax.ShapeDtypeStruct((ROWS, 256), BF),
            jax.ShapeDtypeStruct((n, WIDTH, WIDTH), BF),
        ),
        in_specs=[vm] * 3,
        out_specs=(vm,) * 2,
        scratch_shapes=[
            buf(ROWS, 256), buf(n, 256, WIDTH), buf(n, 256, WIDTH), buf(n, 3, 64, WIDTH), buf(n, 64, WIDTH),
            buf(n, 3, 16, WIDTH), buf(n, 16, WIDTH), buf(n, 3, 16, 128),
            dma, dma, one, one, three, three, three, three, three, three,
            three, three, three, three, three, three, one, one,
        ],
        compiler_params=pltpu.CompilerParams(
            collective_id=2, has_side_effects=True, vmem_limit_bytes=48 * 1024 * 1024
        ),
    )(embed_grad, slots, terms)


def table_kernel(incoming_ref, asked_ref, out_ref, rows):
    @pl.when(pl.program_id(0) == 0)
    def _():
        for q in range(8):
            both = incoming_ref[q * 256 : (q + 1) * 256, :].astype(F32).reshape(16, 16, 256)
            part = slice(q * 128, (q + 1) * 128)
            rows[part, :256] = both[:, :SLOTS].reshape(128, 256).astype(BF)
            rows[part, 256:] = both[:, SLOTS:].reshape(128, 256).astype(BF)

    at = lax.broadcasted_iota(jnp.int32, (256, OWNERS * SLOTS), 0) + pl.program_id(0) * 256
    hit = at == asked_ref[...][:1].astype(jnp.int32)
    out_ref[...] = dot(jnp.where(hit, 1.0, 0.0).astype(BF), rows[...])


def table_sum(incoming, asked):
    return pl.pallas_call(
        table_kernel,
        grid=(8,),
        out_shape=jax.ShapeDtypeStruct((ROWS, WIDTH), F32),
        in_specs=[
            pl.BlockSpec((ROWS, 256), lambda i: (0, 0)),
            pl.BlockSpec((8, OWNERS * SLOTS), lambda i: (0, 0)),
        ],
        out_specs=pl.BlockSpec((256, WIDTH), lambda i: (i, 0)),
        scratch_shapes=[pltpu.VMEM((OWNERS * SLOTS, WIDTH), BF)],
        compiler_params=pltpu.CompilerParams(vmem_limit_bytes=32 * 1024 * 1024),
    )(incoming, asked)


def local(item_table, owner, item_row, lengths, gain_in, gain_out, w_in, w_out, out_grad):
    factor = (TOK * OWNERS) ** (-0.5)
    embed, slots, asked = front(owner[0], item_row.reshape(TOK, 1), item_table)
    hidden, embed_grad, terms = layer(
        lengths, embed, out_grad[0], gain_in, gain_out, w_in, w_out, factor
    )
    incoming, sums = tail(embed_grad, slots, terms)
    table_grad = table_sum(incoming, asked)
    w_in_grad = jnp.concatenate([sums[u] for u in range(4)], axis=1).astype(F32)
    return (hidden[None], table_grad, w_in_grad, sums[4].astype(F32))


def solution(mesh):
    placed = (
        P(("seq", "table"), None),
        P("table", "seq", None),
        P("table", "seq"),
        P("table"),
        P(),
        P(),
        P(),
        P(),
        P("table", "seq", None),
    )
    return jax.shard_map(
        local,
        mesh=mesh,
        in_specs=placed,
        out_specs=(P("table", "seq", None), P(("seq", "table"), None), P(), P()),
        check_vma=False,
    )
```

```python
import functools

import jax
import jax.numpy as jnp
from jax import lax
from jax.experimental import pallas as pl
from jax.experimental.pallas import tpu as pltpu
from jax.sharding import PartitionSpec as P

HEADS = 4
HEAD = 128
TOK = 512
WIDTH = 512
TILE = 128
SCALE = HEAD ** (-0.5)
EPS = 1e-05
MESH = pl.DeviceIdType.MESH
BF = jnp.bfloat16
F32 = jnp.float32


def dot(a, b, ca=1, cb=0):
    return lax.dot_general(a, b, (((ca,), (cb,)), ((), ())), preferred_element_type=F32)


def landed(ref, sem):
    pltpu.make_async_copy(ref, ref, sem).wait()


OWNERS = 128
SLOTS = 8
ROWS = 2048


def greet_all(s, t):
    barrier = pltpu.get_barrier_semaphore()
    me = s * 16 + t

    def greet(d, carry):
        other = lax.rem(me + d, OWNERS)
        pl.semaphore_signal(
            barrier, inc=1, device_id=(other // 16, lax.rem(other, 16)), device_id_type=MESH
        )
        return carry

    lax.fori_loop(1, OWNERS, greet, 0)
    return barrier


def send_rows(src, dst, send, recv, s, t, to_s, to_t, take, place):
    mine = jnp.logical_and(to_s == s, to_t == t)

    @pl.when(mine)
    def _():
        pltpu.make_async_copy(src.at[take], dst.at[place], recv).start()

    @pl.when(jnp.logical_not(mine))
    def _():
        pltpu.make_async_remote_copy(
            src_ref=src.at[take], dst_ref=dst.at[place], send_sem=send, recv_sem=recv,
            device_id=(to_s, to_t), device_id_type=MESH,
        ).start()


def sixteen(index):
    return pl.ds(pl.multiple_of(index * 16, 16), 16)


def spread(src, dst, send, recv, s, t, to_s):
    def one(p, carry):
        to_t = lax.rem(t + p, 16)
        send_rows(src, dst, send, recv, s, t, to_s, to_t, sixteen(to_s * 16 + to_t), sixteen(s * 16 + t))
        return carry

    lax.fori_loop(0, 16, one, 0)


ORDERS = ("zxy", "xyz", "yzx", "zxy", "zyx")
EARLY = (0, 4)
LATE = (1, 2, 3)


def step_kernel(
    factor,
    len_ref, owner_ref, row_ref, table_ref, og_ref, gin_ref, gout_ref, w_in_ref, w_out_ref,
    hidden_ref, incoming_ref, sums_ref, asked_ref,
    x_ref, egrad, terms, normed, normed_t, slope, gate, upstream, joined, jgrad, nback, pback,
    q_out, kv_out, q_in, kv_in, mix_out, mix_in, dm_out, dm_in,
    dq_acc, dkv_acc, part_out, part_in, dq_out, dkv_out, dq_in, dkv_in, m_acc,
    req_out, req_in, asked_col, found, fetched, spot_col, pick_one, pick_two, put_one, put_two,
    r0, a1, r1, a2, r2, a3, r3,
    q_send, q_recv, kv_send, kv_recv, fwd_send, mix_send, mix_recv, dm_send, dm_recv,
    part_send, part_recv, dq_send, dq_recv, dkv_send, dkv_recv,
    req_send, req_recv, row_send, row_recv, back_send, back_recv,
    s0, v0, s1, v1, s2, v2, s3, v3, s4, v4, s5, v5, s6, v6, s7, v7,
):
    s = lax.axis_index("seq")
    t = lax.axis_index("table")
    me = s * 16 + t
    core = lax.rem(t, 2)
    base = t - core
    head = lax.rem(s, HEADS)
    user_core = s // HEADS
    sibling = base + 1 - core
    part_of_s = lax.rem((s + 1) // 2, 2)
    slot_of_s = s // 2
    cx, cz = lax.rem(s, 4), t // 4
    cy = lax.rem(t // 2, 2) * 2 + s // 4
    barrier = greet_all(s, t)

    def push(src, dst, send, recv, to_s, to_t):
        mine = jnp.logical_and(to_s == s, to_t == t)

        @pl.when(mine)
        def _():
            pltpu.make_async_copy(src, dst, recv).start()

        @pl.when(jnp.logical_not(mine))
        def _():
            pltpu.make_async_remote_copy(
                src_ref=src, dst_ref=dst, send_sem=send, recv_sem=recv,
                device_id=(to_s, to_t), device_id_type=MESH,
            ).start()

    def left(src, send, to_s, to_t):
        @pl.when(jnp.logical_not(jnp.logical_and(to_s == s, to_t == t)))
        def _():
            landed(src, send)

    def worker(h):
        return core * HEADS + h, base + part_of_s

    def mine_of(k):
        return 2 * k + lax.rem(k + core, 2)

    def other_of(k):
        return 2 * k + lax.rem(k + core + 1, 2)

    length = len_ref[0]

    def live_rows(start, count):
        pos = s * TOK + start + lax.broadcasted_iota(jnp.int32, (count, 1), 0)
        return (pos < length).astype(F32)

    place = {"x": cx, "y": cy, "z": cz}

    def partner(axis, d):
        other = lax.rem(place[axis] + d, 4)
        if axis == "x":
            return other, s - cx + other, t
        if axis == "y":
            return other, lax.rem(other, 2) * 4 + cx, cz * 4 + (other // 2) * 2 + core
        return other, s, other * 4 + lax.rem(t, 4)

    def ship(src, dst, send, recv, to_s, to_t):
        pltpu.make_async_remote_copy(
            src_ref=src, dst_ref=dst, send_sem=send, recv_sem=recv,
            device_id=(to_s, to_t), device_id_type=MESH,
        ).start()

    half = pl.ds(pl.multiple_of(core * 256, 256), 256)
    other_half = pl.ds(pl.multiple_of(256 - core * 256, 256), 256)

    def block_of(index, size):
        return pl.ds(pl.multiple_of(index * size, size), size)

    def block(axis, size):
        return block_of(place[axis], size)

    def spot(u, first, second, third):
        return sums_ref.at[u, block_of(core * 16 + first * 4 + second, 16), block_of(third, 128)]

    def lines(u, first, second):
        return sums_ref.at[u, block_of(core * 16 + first * 4 + second, 16)]

    def quarter(u, first):
        return sums_ref.at[u, block_of(core * 4 + first, 64)]

    def before_me(axis, d):
        return lax.rem(place[axis] + 4 - d, 4)

    def step(u, n):
        one, two, three = ORDERS[u]
        if n == 0:
            ship(terms.at[u, other_half], r0.at[u], s0.at[u], v0.at[u], s, sibling)
        elif n == 1:
            landed(r0.at[u], v0.at[u])
            a1[u] = (terms[u, half, :].astype(F32) + r0[u].astype(F32)).astype(BF)
            for d in range(1, 4):
                other, to_s, to_t = partner(one, d)
                ship(a1.at[u, block_of(other, 64)], r1.at[u, d - 1], s1.at[u, d - 1], v1.at[u, d - 1], to_s, to_t)
        elif n == 2:
            total = a1[u, block(one, 64), :].astype(F32)
            for d in range(1, 4):
                landed(r1.at[u, d - 1], v1.at[u, d - 1])
                total += r1[u, d - 1].astype(F32)
            a2[u] = total.astype(BF)
            for d in range(1, 4):
                other, to_s, to_t = partner(two, d)
                ship(a2.at[u, block_of(other, 16)], r2.at[u, d - 1], s2.at[u, d - 1], v2.at[u, d - 1], to_s, to_t)
        elif n == 3:
            total = a2[u, block(two, 16), :].astype(F32)
            for d in range(1, 4):
                landed(r2.at[u, d - 1], v2.at[u, d - 1])
                total += r2[u, d - 1].astype(F32)
            a3[u] = total.astype(BF)
            for d in range(1, 4):
                other, to_s, to_t = partner(three, d)
                ship(
                    a3.at[u, :, block_of(other, 128)], r3.at[u, d - 1], s3.at[u, d - 1], v3.at[u, d - 1], to_s, to_t
                )
        elif n == 4:
            total = a3[u, :, block(three, 128)].astype(F32)
            for d in range(1, 4):
                landed(r3.at[u, d - 1], v3.at[u, d - 1])
                total += r3[u, d - 1].astype(F32)
            mine = spot(u, place[one], place[two], place[three])
            mine[...] = total.astype(BF)
            for d in range(1, 4):
                _, to_s, to_t = partner(three, d)
                ship(mine, mine, s4.at[u, d - 1], v4.at[u, d - 1], to_s, to_t)
        elif n == 5:
            for d in range(1, 4):
                landed(spot(u, place[one], place[two], before_me(three, d)), v4.at[u, d - 1])
            mine = lines(u, place[one], place[two])
            for d in range(1, 4):
                _, to_s, to_t = partner(two, d)
                ship(mine, mine, s5.at[u, d - 1], v5.at[u, d - 1], to_s, to_t)
        elif n == 6:
            for d in range(1, 4):
                landed(lines(u, place[one], before_me(two, d)), v5.at[u, d - 1])
            mine = quarter(u, place[one])
            for d in range(1, 4):
                _, to_s, to_t = partner(one, d)
                ship(mine, mine, s6.at[u, d - 1], v6.at[u, d - 1], to_s, to_t)
        elif n == 7:
            for d in range(1, 4):
                landed(quarter(u, before_me(one, d)), v6.at[u, d - 1])
            ship(sums_ref.at[u, half], sums_ref.at[u, half], s7.at[u], v7.at[u], s, sibling)
        else:
            landed(sums_ref.at[u, other_half], v7.at[u])

    target = owner_ref[...]
    lane = lax.broadcasted_iota(jnp.int32, (TOK, OWNERS), 1)
    chosen_mask = lane == target
    chosen = jnp.where(chosen_mask, 1.0, 0.0).astype(BF)
    below = jnp.where(
        lax.broadcasted_iota(jnp.int32, (TOK, TOK), 1) < lax.broadcasted_iota(jnp.int32, (TOK, TOK), 0), 1.0, 0.0
    ).astype(BF)
    before = dot(below, chosen)
    rank = jnp.sum(jnp.where(chosen_mask, before, 0.0), axis=1, keepdims=True).astype(jnp.int32)
    value = row_ref[...] + 1
    high = (value >> 7).astype(F32)
    low = (value & 127).astype(F32)
    message = jnp.where(lane == rank, high, 0.0) + jnp.where(lane == rank + SLOTS, low, 0.0)
    req_out[:, 0, :] = dot(chosen, message.astype(BF), 0, 0)

    pl.semaphore_wait(barrier, OWNERS - 1)

    def ask(p, carry):
        other = lax.rem(me + p, OWNERS)
        send_rows(
            req_out, req_in, req_send, req_recv, s, t, other // 16, lax.rem(other, 16), other, me
        )
        return carry

    lax.fori_loop(0, OWNERS, ask, 0)

    spot_of = target * 16 + rank
    slot_row = jnp.broadcast_to(spot_of.astype(F32), (TOK, 128)).T[:1].astype(jnp.int32)
    live = live_rows(0, TOK)
    upstream[...] = (og_ref[...].astype(F32) * live).astype(BF)
    jgrad[...] = dot(upstream[...], w_out_ref[...], 1, 1)
    number = lax.broadcasted_iota(jnp.int32, (OWNERS * SLOTS, OWNERS), 0)
    lane_s = lax.broadcasted_iota(jnp.int32, (OWNERS * SLOTS, OWNERS), 1)
    expand = jnp.where((number >> 3) == lane_s, 1.0, 0.0).astype(BF)
    landed(req_in, req_recv)
    values = dot(expand, req_in[:, 0, :].astype(BF))
    own = number & 7
    asked = (
        jnp.sum(
            jnp.where(lane_s == own, values * 128.0, 0.0) + jnp.where(lane_s == own + SLOTS, values, 0.0),
            axis=1,
            keepdims=True,
        )
        - 1.0
    )
    wide = jnp.broadcast_to(asked, (OWNERS * SLOTS, 128))
    asked_col[...] = wide
    asked_ref[...] = wide.T[:8]

    def gather(p, carry):
        q = lax.rem(s + p, 8)
        column = asked_col[pl.ds(pl.multiple_of(q * 128, 128), 128), :][:, :1].astype(jnp.int32)
        hit = lax.broadcasted_iota(jnp.int32, (128, ROWS), 1) == column
        rows = dot(jnp.where(hit, 1.0, 0.0).astype(BF), table_ref[...])
        both = jnp.concatenate(
            [rows[:, :256].reshape(16, SLOTS, 256), rows[:, 256:].reshape(16, SLOTS, 256)], axis=1
        )
        found[pl.ds(pl.multiple_of(q * 256, 256), 256), :] = both.reshape(256, 256).astype(BF)
        spread(found, fetched, row_send, row_recv, s, t, q)
        return carry

    lax.fori_loop(0, 8, gather, 0)
    def pick_tile(r, carry):
        rows = pl.ds(pl.multiple_of(r * TILE, TILE), TILE)
        at = lax.broadcasted_iota(jnp.int32, (TILE, ROWS), 1)
        spots = spot_col[rows, :][:, :1]
        pick_one[rows, :] = jnp.where(at == spots, 1.0, 0.0).astype(BF)
        pick_two[rows, :] = jnp.where(at == spots + SLOTS, 1.0, 0.0).astype(BF)
        return carry

    spot_col[...] = jnp.broadcast_to(spot_of, (TOK, 128))
    lax.fori_loop(0, TOK // TILE, pick_tile, 0)
    dq_acc[...] = jnp.zeros_like(dq_acc)
    dkv_acc[...] = jnp.zeros_like(dkv_acc)
    landed(fetched, row_recv)

    def norm_tile(r, carry):
        rows = pl.ds(pl.multiple_of(r * TILE, TILE), TILE)
        x_ref[rows, :256] = dot(pick_one[rows, :], fetched[...]).astype(BF)
        x_ref[rows, 256:] = dot(pick_two[rows, :], fetched[...]).astype(BF)
        x = x_ref[rows, :].astype(F32)
        mean = jnp.mean(x, -1, keepdims=True)
        cent = x - mean
        var = jnp.mean(cent * cent, -1, keepdims=True)
        normed[rows, :] = (cent * lax.rsqrt(var + EPS) * gin_ref[...]).astype(BF)
        return carry

    lax.fori_loop(0, TOK // TILE, norm_tile, 0)

    def project(first, columns):
        pre = dot(normed[...], w_in_ref[:, pl.ds(first, columns)])
        half = 0.5 * pre
        th = jnp.tanh(half)
        slope[:, pl.ds(first, columns)] = 0.5 * (1.0 + th) * (1.0 + half - half * th)
        return half + half * th

    for h in range(HEADS):
        kv_out[h, :, :HEAD] = project(3 * WIDTH + h * HEAD, HEAD).astype(BF)
        kv_out[h, :, HEAD:] = (project(WIDTH + h * HEAD, HEAD) * live).astype(BF)
        to = worker(h)
        push(kv_out.at[h], kv_in.at[s], kv_send.at[h], kv_recv.at[s], *to)
        q_out[h] = project(2 * WIDTH + h * HEAD, HEAD).astype(BF)
        push(q_out.at[h], q_in.at[slot_of_s], q_send.at[h], q_recv.at[slot_of_s], *to)

    gate[:, :256] = project(0, 256).astype(BF)
    gate[:, 256:] = project(256, 256).astype(BF)
    normed_t[...] = normed[...].T

    def scatter_tile(q, carry):
        rows = pl.ds(pl.multiple_of(q * 256, 256), 256)
        at = lax.broadcasted_iota(jnp.int32, (256, TOK), 0) + q * 256
        put_one[rows, :] = jnp.where(at == slot_row, 1.0, 0.0).astype(BF)
        put_two[rows, :] = jnp.where(at == slot_row + SLOTS, 1.0, 0.0).astype(BF)
        return carry

    lax.fori_loop(0, 8, scatter_tile, 0)

    def take(k):
        d = mine_of(k)
        landed(kv_in.at[d], kv_recv.at[d])
        pltpu.make_async_remote_copy(
            src_ref=kv_in.at[d], dst_ref=kv_in.at[d], send_sem=fwd_send.at[k], recv_sem=kv_recv.at[d],
            device_id=(s, sibling), device_id_type=MESH,
        ).start()

    row = lax.broadcasted_iota(jnp.int32, (TOK, TOK), 0)
    col = lax.broadcasted_iota(jnp.int32, (TOK, TOK), 1)

    def forward_pair(k, j, diagonal):
        half = dot(q_in[k], kv_in[j, :, :HEAD], 1, 1) * (0.5 * SCALE)
        w = half + half * jnp.tanh(half)
        if diagonal:
            w = jnp.where(col <= row, w, 0.0)
        return dot(w.astype(BF), kv_in[j, :, HEAD:])

    take(0)

    def forward(k, carry):
        i = mine_of(k)

        @pl.when(k < 3)
        def _():
            take(k + 1)

        landed(q_in.at[k], q_recv.at[k])
        o = other_of(k)
        landed(kv_in.at[o], kv_recv.at[o])
        m_acc[...] = forward_pair(k, i, True)

        def inner(j, c):
            m_acc[...] += forward_pair(k, j, False)
            return c

        lax.fori_loop(0, i, inner, 0)
        m = m_acc[...]
        shift = jnp.mean(m, -1, keepdims=True).astype(BF).astype(F32)
        mix_out[k, :TOK, :] = (m - shift).astype(BF)
        wide = jnp.broadcast_to(shift, (TOK, HEAD))
        lines = jnp.zeros((16, HEAD), F32)
        line = lax.broadcasted_iota(jnp.int32, (16, HEAD), 0)
        for b in range(TOK // HEAD):
            lines += jnp.where(line == b, wide[b * HEAD : (b + 1) * HEAD].T[:16], 0.0)
        mix_out[k, TOK:, :] = lines.astype(BF)
        push(mix_out.at[k], mix_in.at[head], mix_send.at[k], mix_recv.at[head], i, base + user_core)
        return carry

    lax.fori_loop(0, 4, forward, 0)

    for h in range(HEADS):
        landed(mix_in.at[h], mix_recv.at[h])

    def post_tile(r, carry):
        start = pl.multiple_of(r * TILE, TILE)
        rows = pl.ds(start, TILE)
        alive = live_rows(start, TILE)
        pick = (lax.broadcasted_iota(jnp.int32, (16, HEAD), 0) == r).astype(F32).astype(BF)
        m = jnp.concatenate(
            [mix_in[h, rows, :].astype(F32) + dot(mix_in[h, TOK:, :], pick, 0, 0) for h in range(HEADS)], axis=1
        ) * alive
        mean = jnp.mean(m, -1, keepdims=True)
        cent = m - mean
        var = jnp.mean(cent * cent, -1, keepdims=True)
        rstd = lax.rsqrt(var + EPS)
        n = cent * rstd
        ng = n * gout_ref[...]
        g = gate[rows, :].astype(F32)
        jg = jgrad[rows, :]
        joined[rows, :] = (ng * g).astype(BF)
        pback[rows, :WIDTH] = (jg * ng * slope[rows, :WIDTH]).astype(BF)
        dn = jg * g * gout_ref[...]
        dm = rstd * (dn - jnp.mean(dn, -1, keepdims=True) - n * jnp.mean(dn * n, -1, keepdims=True))
        dm = (dm * alive).astype(BF)
        for h in range(HEADS):
            dm_out[h, rows, :] = dm[:, h * HEAD : (h + 1) * HEAD]
        return carry

    lax.fori_loop(0, TOK // TILE, post_tile, 0)
    for h in range(HEADS):
        push(dm_out.at[h], dm_in.at[slot_of_s], dm_send.at[h], dm_recv.at[slot_of_s], *worker(h))

    terms[4] = (dot(joined[...], upstream[...], 0, 0) * factor).astype(BF)
    terms[0] = (dot(normed_t[...], pback[:, :WIDTH]) * factor).astype(BF)
    for u in EARLY:
        step(u, 0)
    hidden_ref[...] = ((dot(joined[...], w_out_ref[...]) + x_ref[...].astype(F32)) * live).astype(BF)
    nback[...] = dot(pback[:, :WIDTH], w_in_ref[:, :WIDTH], 1, 1)

    for k in range(4):
        landed(dm_in.at[k], dm_recv.at[k])

    def backward_pair(k, j, diagonal):
        q, dm = q_in[k], dm_in[k]
        half = dot(kv_in[j, :, :HEAD], q, 1, 1) * (0.5 * SCALE)
        th = jnp.tanh(half)
        ht = half * th
        w = half + ht
        sb = dot(kv_in[j, :, HEAD:], dm, 1, 1) * ((0.5 + 0.5 * th) * (1.0 + half - ht))
        if diagonal:
            w = jnp.where(row <= col, w, 0.0)
            sb = jnp.where(row <= col, sb, 0.0)
        sb = sb.astype(BF)
        dkv_acc[j, :, HEAD:] += dot(w.astype(BF), dm)
        dkv_acc[j, :, :HEAD] += dot(sb, q)
        dq_acc[k] += dot(sb, kv_in[j, :, :HEAD], 0, 0)

    def finish(m):
        d = mine_of(m)
        landed(part_in.at[m], part_recv.at[m])
        total = dkv_acc[d] + part_in[m].astype(F32)
        dkv_out[m, :, :HEAD] = (total[:, :HEAD] * SCALE).astype(BF)
        dkv_out[m, :, HEAD:] = total[:, HEAD:].astype(BF)
        push(dkv_out.at[m], dkv_in.at[head], dkv_send.at[m], dkv_recv.at[head], d, base + user_core)

    def backward(m, carry):
        i = mine_of(m)

        def one(jj, c):
            j = 2 * m + jj

            @pl.when(i == j)
            def _():
                backward_pair(m, j, True)

            def inner(k, cc):
                backward_pair(k, j, False)
                return cc

            lax.fori_loop(jnp.where(i > j, m, m + 1), 4, inner, 0)
            for n in range(8):

                @pl.when(j == n)
                def _():
                    for u in EARLY:
                        step(u, n + 1)

            return c

        lax.fori_loop(0, 2, one, 0)
        part_out[m] = dkv_acc[other_of(m)].astype(BF)
        pltpu.make_async_remote_copy(
            src_ref=part_out.at[m], dst_ref=part_in.at[m], send_sem=part_send.at[m], recv_sem=part_recv.at[m],
            device_id=(s, sibling), device_id_type=MESH,
        ).start()
        dq_out[m] = (dq_acc[m] * SCALE).astype(BF)
        push(dq_out.at[m], dq_in.at[head], dq_send.at[m], dq_recv.at[head], i, base + user_core)

        @pl.when(m > 0)
        def _():
            finish(m - 1)

        return carry

    lax.fori_loop(0, 4, backward, 0)
    finish(3)

    for h in range(HEADS):
        landed(dq_in.at[h], dq_recv.at[h])
        landed(dkv_in.at[h], dkv_recv.at[h])

    def gate_tile(r, carry):
        start = pl.multiple_of(r * TILE, TILE)
        rows = pl.ds(start, TILE)
        alive = live_rows(start, TILE)
        for h in range(HEADS):
            for first, piece in (
                (WIDTH, dkv_in[h, rows, HEAD:].astype(F32) * alive),
                (2 * WIDTH, dq_in[h, rows, :].astype(F32)),
                (3 * WIDTH, dkv_in[h, rows, :HEAD].astype(F32)),
            ):
                c = first + h * HEAD
                pback[rows, c : c + HEAD] = (piece * slope[rows, c : c + HEAD]).astype(BF)
        return carry

    lax.fori_loop(0, TOK // TILE, gate_tile, 0)
    for u in LATE:
        terms[u] = (dot(normed_t[...], pback[:, u * WIDTH : (u + 1) * WIDTH]) * factor).astype(BF)
        step(u, 0)

    def back_tile(r, carry):
        rows = pl.ds(pl.multiple_of(r * TILE, TILE), TILE)
        nb = nback[rows, :] + dot(pback[rows, WIDTH:], w_in_ref[:, WIDTH:], 1, 1)
        x = x_ref[rows, :].astype(F32)
        mean = jnp.mean(x, -1, keepdims=True)
        cent = x - mean
        var = jnp.mean(cent * cent, -1, keepdims=True)
        rstd = lax.rsqrt(var + EPS)
        n = cent * rstd
        dn = nb * gin_ref[...]
        dx = rstd * (dn - jnp.mean(dn, -1, keepdims=True) - n * jnp.mean(dn * n, -1, keepdims=True))
        egrad[rows, :] = (dx + upstream[rows, :].astype(F32)).astype(BF)
        return carry

    lax.fori_loop(0, TOK // TILE, back_tile, 0)
    for u in LATE:
        step(u, 1)

    landed(found.at[pl.ds(0, (OWNERS - 1) * 16)], row_send)

    def scatter(p, carry):
        q = lax.rem(s + p, 8)
        rows = pl.ds(pl.multiple_of(q * 256, 256), 256)
        found[rows, :] = (dot(put_one[rows, :], egrad[:, :256]) + dot(put_two[rows, :], egrad[:, 256:])).astype(BF)
        spread(found, incoming_ref, back_send, back_recv, s, t, q)
        return carry

    for n in range(4):
        lax.fori_loop(2 * n, 2 * n + 2, scatter, 0)
        if n < 3:
            for u in LATE:
                step(u, n + 2)
    for n in range(5, 9):
        for u in LATE:
            step(u, n)
    landed(incoming_ref, back_recv)
    landed(found.at[pl.ds(0, (OWNERS - 1) * 16)], back_send)
    landed(req_out.at[pl.ds(0, OWNERS - 1)], req_send)

    for h in range(HEADS):
        to = worker(h)
        left(kv_out.at[h], kv_send.at[h], *to)
        left(q_out.at[h], q_send.at[h], *to)
        left(dm_out.at[h], dm_send.at[h], *to)
        landed(kv_in.at[mine_of(h)], fwd_send.at[h])
        landed(part_out.at[h], part_send.at[h])
        back = (mine_of(h), base + user_core)
        left(mix_out.at[h], mix_send.at[h], *back)
        left(dq_out.at[h], dq_send.at[h], *back)
        left(dkv_out.at[h], dkv_send.at[h], *back)


    for u in range(len(ORDERS)):
        one, two, three = ORDERS[u]
        landed(terms.at[u, other_half], s0.at[u])
        landed(sums_ref.at[u, half], s7.at[u])
        for d in range(3):
            landed(r1.at[u, d], s1.at[u, d])
            landed(r2.at[u, d], s2.at[u, d])
            landed(r3.at[u, d], s3.at[u, d])
            landed(spot(u, place[one], place[two], place[three]), s4.at[u, d])
            landed(lines(u, place[one], place[two]), s5.at[u, d])
            landed(quarter(u, place[one]), s6.at[u, d])


def layer_step(length, owner, item_row, item_table, out_grad, gain_in, gain_out, w_in, w_out, factor):
    vm = pl.BlockSpec(memory_space=pltpu.VMEM)
    dma = pltpu.SemaphoreType.DMA
    n = len(ORDERS)

    def buf(*shape, dtype=BF):
        return pltpu.VMEM(shape, dtype)

    square = buf(TOK, WIDTH)
    wide = buf(TOK, WIDTH, dtype=F32)
    heads, pairs, carried = buf(4, TOK, HEAD), buf(4, TOK, 2 * HEAD), buf(4, TOK + 16, HEAD)
    message = buf(OWNERS, 1, 128, dtype=F32)
    blocks = [
        square, square, buf(n, WIDTH, WIDTH), square, square, buf(TOK, 4 * WIDTH, dtype=F32), square, square,
        square, wide, wide, buf(TOK, 4 * WIDTH),
        heads, pairs, heads, buf(8, TOK, 2 * HEAD), carried, carried, heads, heads,
        buf(4, TOK, HEAD, dtype=F32), buf(8, TOK, 2 * HEAD, dtype=F32),
        pairs, pairs, heads, pairs, heads, pairs, buf(TOK, HEAD, dtype=F32),
        message, message, buf(OWNERS * SLOTS, 128, dtype=F32), buf(ROWS, 256), buf(ROWS, 256),
        buf(TOK, 128, dtype=jnp.int32), buf(TOK, ROWS), buf(TOK, ROWS), buf(ROWS, TOK), buf(ROWS, TOK),
        buf(n, 256, WIDTH), buf(n, 256, WIDTH), buf(n, 3, 64, WIDTH), buf(n, 64, WIDTH),
        buf(n, 3, 16, WIDTH), buf(n, 16, WIDTH), buf(n, 3, 16, 128),
    ]
    one, three = dma((n,)), dma((n, 3))
    sems = [dma((c,)) for c in (4, 4, 4, 8, 4, 4, 4, 4, 4, 4, 4, 4, 4, 4, 4)]
    sems += [dma] * 6 + [one] * 2 + [three] * 12 + [one] * 2
    return pl.pallas_call(
        functools.partial(step_kernel, factor),
        out_shape=(
            jax.ShapeDtypeStruct((TOK, WIDTH), BF),
            jax.ShapeDtypeStruct((ROWS, 256), BF),
            jax.ShapeDtypeStruct((n, WIDTH, WIDTH), BF),
            jax.ShapeDtypeStruct((8, OWNERS * SLOTS), F32),
        ),
        in_specs=[pl.BlockSpec(memory_space=pltpu.SMEM)] + [vm] * 8,
        out_specs=(vm,) * 4,
        scratch_shapes=blocks + sems,
        compiler_params=pltpu.CompilerParams(
            collective_id=0, has_side_effects=True, vmem_limit_bytes=62 * 1024 * 1024
        ),
    )(length, owner, item_row, item_table, out_grad, gain_in.reshape(1, -1), gain_out.reshape(1, -1), w_in, w_out)


def finish_kernel(incoming_ref, asked_ref, sums_ref, out_ref, w_in_ref, w_out_ref, rows):
    @pl.when(pl.program_id(0) == 0)
    def _():
        for q in range(8):
            both = incoming_ref[q * 256 : (q + 1) * 256, :].astype(F32).reshape(16, 16, 256)
            part = slice(q * 128, (q + 1) * 128)
            rows[part, :256] = both[:, :SLOTS].reshape(128, 256).astype(BF)
            rows[part, 256:] = both[:, SLOTS:].reshape(128, 256).astype(BF)

    at = lax.broadcasted_iota(jnp.int32, (256, OWNERS * SLOTS), 0) + pl.program_id(0) * 256
    hit = at == asked_ref[...][:1].astype(jnp.int32)
    out_ref[...] = dot(jnp.where(hit, 1.0, 0.0).astype(BF), rows[...])
    for u in range(4):
        w_in_ref[:, u * WIDTH : (u + 1) * WIDTH] = sums_ref[u].astype(F32)
    w_out_ref[...] = sums_ref[4].astype(F32)


def finish(incoming, asked, sums):
    n = len(ORDERS)
    return pl.pallas_call(
        finish_kernel,
        grid=(8,),
        out_shape=(
            jax.ShapeDtypeStruct((ROWS, WIDTH), F32),
            jax.ShapeDtypeStruct((WIDTH, 4 * WIDTH), F32),
            jax.ShapeDtypeStruct((WIDTH, WIDTH), F32),
        ),
        in_specs=[
            pl.BlockSpec((ROWS, 256), lambda i: (0, 0)),
            pl.BlockSpec((8, OWNERS * SLOTS), lambda i: (0, 0)),
            pl.BlockSpec((n, 64, WIDTH), lambda i: (0, i, 0)),
        ],
        out_specs=(
            pl.BlockSpec((256, WIDTH), lambda i: (i, 0)),
            pl.BlockSpec((64, 4 * WIDTH), lambda i: (i, 0)),
            pl.BlockSpec((64, WIDTH), lambda i: (i, 0)),
        ),
        scratch_shapes=[pltpu.VMEM((OWNERS * SLOTS, WIDTH), BF)],
        compiler_params=pltpu.CompilerParams(vmem_limit_bytes=32 * 1024 * 1024),
    )(incoming, asked, sums)


def local(item_table, owner, item_row, lengths, gain_in, gain_out, w_in, w_out, out_grad):
    factor = (TOK * OWNERS) ** (-0.5)
    hidden, incoming, sums, asked = layer_step(
        lengths, owner[0], item_row.reshape(TOK, 1), item_table, out_grad[0], gain_in, gain_out, w_in, w_out, factor
    )
    table_grad, w_in_grad, w_out_grad = finish(incoming, asked, sums)
    return (hidden[None], table_grad, w_in_grad, w_out_grad)


def solution(mesh):
    placed = (
        P(("seq", "table"), None),
        P("table", "seq", None),
        P("table", "seq"),
        P("table"),
        P(),
        P(),
        P(),
        P(),
        P("table", "seq", None),
    )
    return jax.shard_map(
        local,
        mesh=mesh,
        in_specs=placed,
        out_specs=(P("table", "seq", None), P(("seq", "table"), None), P(), P()),
        check_vma=False,
    )
```

```python
import functools

import jax
import jax.numpy as jnp
from jax import lax
from jax.experimental import pallas as pl
from jax.experimental.pallas import tpu as pltpu
from jax.sharding import PartitionSpec as P

HEADS = 4
HEAD = 128
TOK = 512
WIDTH = 512
TILE = 128
SCALE = HEAD ** (-0.5)
EPS = 1e-05
MESH = pl.DeviceIdType.MESH
BF = jnp.bfloat16
F32 = jnp.float32


def dot(a, b, ca=1, cb=0):
    return lax.dot_general(a, b, (((ca,), (cb,)), ((), ())), preferred_element_type=F32)


def landed(ref, sem):
    pltpu.make_async_copy(ref, ref, sem).wait()


OWNERS = 128
SLOTS = 8
ROWS = 2048


def greet_all(s, t):
    barrier = pltpu.get_barrier_semaphore()
    me = s * 16 + t

    def greet(d, carry):
        other = lax.rem(me + d, OWNERS)
        pl.semaphore_signal(
            barrier, inc=1, device_id=(other // 16, lax.rem(other, 16)), device_id_type=MESH
        )
        return carry

    lax.fori_loop(1, OWNERS, greet, 0)
    return barrier


def send_rows(src, dst, send, recv, s, t, to_s, to_t, take, place):
    mine = jnp.logical_and(to_s == s, to_t == t)

    @pl.when(mine)
    def _():
        pltpu.make_async_copy(src.at[take], dst.at[place], recv).start()

    @pl.when(jnp.logical_not(mine))
    def _():
        pltpu.make_async_remote_copy(
            src_ref=src.at[take], dst_ref=dst.at[place], send_sem=send, recv_sem=recv,
            device_id=(to_s, to_t), device_id_type=MESH,
        ).start()


def sixteen(index):
    return pl.ds(pl.multiple_of(index * 16, 16), 16)


def spread(src, dst, send, recv, s, t, to_s):
    def one(p, carry):
        to_t = lax.rem(t + p, 16)
        send_rows(src, dst, send, recv, s, t, to_s, to_t, sixteen(to_s * 16 + to_t), sixteen(s * 16 + t))
        return carry

    lax.fori_loop(0, 16, one, 0)


ORDERS = ("zxy", "xyz", "yzx", "zxy", "zyx")
EARLY = (0, 4)
LATE = (1, 2, 3)


def step_kernel(
    factor,
    len_ref, owner_ref, row_ref, table_hbm, og_hbm, gin_ref, gout_ref, w_in_hbm, w_out_hbm,
    hidden_ref, incoming_ref, sums_ref, asked_ref,
    table_ref, og_ref, w_in_ref, w_out_ref, x_ref, egrad, terms, normed, normed_t, slope, gate, upstream, joined, jgrad, nback, pback,
    q_out, kv_out, q_in, kv_in, mix_out, mix_in, dm_out, dm_in,
    dq_acc, dkv_acc, part_out, part_in, dq_out, dkv_out, dq_in, dkv_in, m_acc,
    req_out, req_in, asked_col, found, fetched, spot_col, pick_one, pick_two, put_one, put_two,
    r0, a1, r1, a2, r2, a3, r3,
    q_send, q_recv, kv_send, kv_recv, fwd_send, mix_send, mix_recv, dm_send, dm_recv,
    part_send, part_recv, dq_send, dq_recv, dkv_send, dkv_recv,
    load_sem, req_send, req_recv, row_send, row_recv, back_send, back_recv,
    s0, v0, s1, v1, s2, v2, s3, v3, s4, v4, s5, v5, s6, v6, s7, v7,
):
    s = lax.axis_index("seq")
    t = lax.axis_index("table")
    me = s * 16 + t
    core = lax.rem(t, 2)
    base = t - core
    head = lax.rem(s, HEADS)
    user_core = lax.rem(lax.rem(s, HEADS) + s // HEADS, 2)
    upward = user_core == 1
    sibling = base + 1 - core
    part_of_s = lax.rem((s + 1) // 2, 2)
    slot_of_s = s // 2
    cx, cz = lax.rem(s, 4), t // 4
    cy = lax.rem(t // 2, 2) * 2 + s // 4
    barrier = greet_all(s, t)

    def push(src, dst, send, recv, to_s, to_t):
        mine = jnp.logical_and(to_s == s, to_t == t)

        @pl.when(mine)
        def _():
            pltpu.make_async_copy(src, dst, recv).start()

        @pl.when(jnp.logical_not(mine))
        def _():
            pltpu.make_async_remote_copy(
                src_ref=src, dst_ref=dst, send_sem=send, recv_sem=recv,
                device_id=(to_s, to_t), device_id_type=MESH,
            ).start()

    def left(src, send, to_s, to_t):
        @pl.when(jnp.logical_not(jnp.logical_and(to_s == s, to_t == t)))
        def _():
            landed(src, send)

    def worker(h):
        return lax.rem(core + h, 2) * HEADS + h, base + part_of_s

    def mine_of(k):
        return 2 * k + lax.rem(k + core, 2)

    def other_of(k):
        return 2 * k + lax.rem(k + core + 1, 2)

    length = len_ref[0]

    def live_rows(start, count):
        pos = s * TOK + start + lax.broadcasted_iota(jnp.int32, (count, 1), 0)
        return (pos < length).astype(F32)

    place = {"x": cx, "y": cy, "z": cz}

    def partner(axis, d):
        other = lax.rem(place[axis] + d, 4)
        if axis == "x":
            return other, s - cx + other, t
        if axis == "y":
            return other, lax.rem(other, 2) * 4 + cx, cz * 4 + (other // 2) * 2 + core
        return other, s, other * 4 + lax.rem(t, 4)

    def ship(src, dst, send, recv, to_s, to_t):
        pltpu.make_async_remote_copy(
            src_ref=src, dst_ref=dst, send_sem=send, recv_sem=recv,
            device_id=(to_s, to_t), device_id_type=MESH,
        ).start()

    half = pl.ds(pl.multiple_of(core * 256, 256), 256)
    other_half = pl.ds(pl.multiple_of(256 - core * 256, 256), 256)

    def block_of(index, size):
        return pl.ds(pl.multiple_of(index * size, size), size)

    def block(axis, size):
        return block_of(place[axis], size)

    def spot(u, first, second, third):
        return sums_ref.at[u, block_of(core * 16 + first * 4 + second, 16), block_of(third, 128)]

    def lines(u, first, second):
        return sums_ref.at[u, block_of(core * 16 + first * 4 + second, 16)]

    def quarter(u, first):
        return sums_ref.at[u, block_of(core * 4 + first, 64)]

    def before_me(axis, d):
        return lax.rem(place[axis] + 4 - d, 4)

    def step(u, n):
        one, two, three = ORDERS[u]
        if n == 0:
            ship(terms.at[u, other_half], r0.at[u], s0.at[u], v0.at[u], s, sibling)
        elif n == 1:
            landed(r0.at[u], v0.at[u])
            a1[u] = (terms[u, half, :].astype(F32) + r0[u].astype(F32)).astype(BF)
            for d in range(1, 4):
                other, to_s, to_t = partner(one, d)
                ship(a1.at[u, block_of(other, 64)], r1.at[u, d - 1], s1.at[u, d - 1], v1.at[u, d - 1], to_s, to_t)
        elif n == 2:
            total = a1[u, block(one, 64), :].astype(F32)
            for d in range(1, 4):
                landed(r1.at[u, d - 1], v1.at[u, d - 1])
                total += r1[u, d - 1].astype(F32)
            a2[u] = total.astype(BF)
            for d in range(1, 4):
                other, to_s, to_t = partner(two, d)
                ship(a2.at[u, block_of(other, 16)], r2.at[u, d - 1], s2.at[u, d - 1], v2.at[u, d - 1], to_s, to_t)
        elif n == 3:
            total = a2[u, block(two, 16), :].astype(F32)
            for d in range(1, 4):
                landed(r2.at[u, d - 1], v2.at[u, d - 1])
                total += r2[u, d - 1].astype(F32)
            a3[u] = total.astype(BF)
            for d in range(1, 4):
                other, to_s, to_t = partner(three, d)
                ship(
                    a3.at[u, :, block_of(other, 128)], r3.at[u, d - 1], s3.at[u, d - 1], v3.at[u, d - 1], to_s, to_t
                )
        elif n == 4:
            total = a3[u, :, block(three, 128)].astype(F32)
            for d in range(1, 4):
                landed(r3.at[u, d - 1], v3.at[u, d - 1])
                total += r3[u, d - 1].astype(F32)
            mine = spot(u, place[one], place[two], place[three])
            mine[...] = total.astype(BF)
            for d in range(1, 4):
                _, to_s, to_t = partner(three, d)
                ship(mine, mine, s4.at[u, d - 1], v4.at[u, d - 1], to_s, to_t)
        elif n == 5:
            for d in range(1, 4):
                landed(spot(u, place[one], place[two], before_me(three, d)), v4.at[u, d - 1])
            mine = lines(u, place[one], place[two])
            for d in range(1, 4):
                _, to_s, to_t = partner(two, d)
                ship(mine, mine, s5.at[u, d - 1], v5.at[u, d - 1], to_s, to_t)
        elif n == 6:
            for d in range(1, 4):
                landed(lines(u, place[one], before_me(two, d)), v5.at[u, d - 1])
            mine = quarter(u, place[one])
            for d in range(1, 4):
                _, to_s, to_t = partner(one, d)
                ship(mine, mine, s6.at[u, d - 1], v6.at[u, d - 1], to_s, to_t)
        elif n == 7:
            for d in range(1, 4):
                landed(quarter(u, before_me(one, d)), v6.at[u, d - 1])
            ship(sums_ref.at[u, half], sums_ref.at[u, half], s7.at[u], v7.at[u], s, sibling)
        else:
            landed(sums_ref.at[u, other_half], v7.at[u])

    copies = [
        pltpu.make_async_copy(src, dst, load_sem.at[n])
        for n, (src, dst) in enumerate(
            ((table_hbm, table_ref), (og_hbm, og_ref), (w_out_hbm, w_out_ref), (w_in_hbm, w_in_ref))
        )
    ]
    for copy in copies:
        copy.start()

    target = owner_ref[...]
    line_e = lax.broadcasted_iota(jnp.int32, (OWNERS, TOK), 0)
    chosen_mask = line_e == target
    chosen = jnp.where(chosen_mask, 1.0, 0.0).astype(BF)
    above = jnp.where(
        lax.broadcasted_iota(jnp.int32, (TOK, TOK), 0) < lax.broadcasted_iota(jnp.int32, (TOK, TOK), 1), 1.0, 0.0
    ).astype(BF)
    before = dot(chosen, above)
    rank = jnp.sum(jnp.where(chosen_mask, before, 0.0), axis=0, keepdims=True).astype(jnp.int32)
    value = row_ref[...] + 1
    high = (value >> 7).astype(F32)
    low = (value & 127).astype(F32)
    message = jnp.where(line_e == rank, high, 0.0) + jnp.where(line_e == rank + SLOTS, low, 0.0)
    req_out[:, 0, :] = dot(chosen, message.astype(BF), 1, 1)
    pl.semaphore_wait(barrier, OWNERS - 1)

    def ask(p, carry):
        other = lax.rem(me + p, OWNERS)
        send_rows(
            req_out, req_in, req_send, req_recv, s, t, other // 16, lax.rem(other, 16), other, me
        )
        return carry

    lax.fori_loop(0, OWNERS, ask, 0)

    slot_row = target * 16 + rank
    spot_col[...] = jnp.broadcast_to(slot_row.astype(F32), (128, TOK)).T.astype(jnp.int32)
    live = live_rows(0, TOK)
    copies[1].wait()
    copies[2].wait()
    upstream[...] = (og_ref[...].astype(F32) * live).astype(BF)
    jgrad[...] = dot(upstream[...], w_out_ref[...], 1, 1)
    number = lax.broadcasted_iota(jnp.int32, (OWNERS * SLOTS, OWNERS), 0)
    lane_s = lax.broadcasted_iota(jnp.int32, (OWNERS * SLOTS, OWNERS), 1)
    expand = jnp.where((number >> 3) == lane_s, 1.0, 0.0).astype(BF)
    landed(req_in, req_recv)
    values = dot(expand, req_in[:, 0, :].astype(BF))
    own = number & 7
    asked = (
        jnp.sum(
            jnp.where(lane_s == own, values * 128.0, 0.0) + jnp.where(lane_s == own + SLOTS, values, 0.0),
            axis=1,
            keepdims=True,
        )
        - 1.0
    )
    wide = jnp.broadcast_to(asked, (OWNERS * SLOTS, 128))
    asked_col[...] = wide
    asked_ref[...] = wide.T[:8]

    copies[0].wait()

    def gather(p, carry):
        q = lax.rem(s + p, 8)
        column = asked_col[pl.ds(pl.multiple_of(q * 128, 128), 128), :][:, :1].astype(jnp.int32)
        hit = lax.broadcasted_iota(jnp.int32, (128, ROWS), 1) == column
        rows = dot(jnp.where(hit, 1.0, 0.0).astype(BF), table_ref[...])
        both = jnp.concatenate(
            [rows[:, :256].reshape(16, SLOTS, 256), rows[:, 256:].reshape(16, SLOTS, 256)], axis=1
        )
        found[pl.ds(pl.multiple_of(q * 256, 256), 256), :] = both.reshape(256, 256).astype(BF)
        spread(found, fetched, row_send, row_recv, s, t, q)
        return carry

    lax.fori_loop(0, 8, gather, 0)
    def pick_tile(r, carry):
        rows = pl.ds(pl.multiple_of(r * TILE, TILE), TILE)
        at = lax.broadcasted_iota(jnp.int32, (TILE, ROWS), 1)
        spots = spot_col[rows, :][:, :1]
        pick_one[rows, :] = jnp.where(at == spots, 1.0, 0.0).astype(BF)
        pick_two[rows, :] = jnp.where(at == spots + SLOTS, 1.0, 0.0).astype(BF)
        return carry

    lax.fori_loop(0, TOK // TILE, pick_tile, 0)
    dq_acc[...] = jnp.zeros_like(dq_acc)
    dkv_acc[...] = jnp.zeros_like(dkv_acc)
    copies[3].wait()
    landed(fetched, row_recv)

    def norm_tile(r, carry):
        rows = pl.ds(pl.multiple_of(r * TILE, TILE), TILE)
        x_ref[rows, :256] = dot(pick_one[rows, :], fetched[...]).astype(BF)
        x_ref[rows, 256:] = dot(pick_two[rows, :], fetched[...]).astype(BF)
        x = x_ref[rows, :].astype(F32)
        mean = jnp.mean(x, -1, keepdims=True)
        cent = x - mean
        var = jnp.mean(cent * cent, -1, keepdims=True)
        normed[rows, :] = (cent * lax.rsqrt(var + EPS) * gin_ref[...]).astype(BF)
        return carry

    lax.fori_loop(0, TOK // TILE, norm_tile, 0)

    def project(first, columns):
        pre = dot(normed[...], w_in_ref[:, pl.ds(first, columns)])
        half = 0.5 * pre
        th = jnp.tanh(half)
        slope[:, pl.ds(first, columns)] = 0.5 * (1.0 + th) * (1.0 + half - half * th)
        return half + half * th

    for h in range(HEADS):
        kv_out[h, :, :HEAD] = project(3 * WIDTH + h * HEAD, HEAD).astype(BF)
        kv_out[h, :, HEAD:] = (project(WIDTH + h * HEAD, HEAD) * live).astype(BF)
        to = worker(h)
        push(kv_out.at[h], kv_in.at[s], kv_send.at[h], kv_recv.at[s], *to)
        q_out[h] = project(2 * WIDTH + h * HEAD, HEAD).astype(BF)
        push(q_out.at[h], q_in.at[slot_of_s], q_send.at[h], q_recv.at[slot_of_s], *to)

    gate[:, :256] = project(0, 256).astype(BF)
    gate[:, 256:] = project(256, 256).astype(BF)
    normed_t[...] = normed[...].T

    def scatter_tile(q, carry):
        rows = pl.ds(pl.multiple_of(q * 256, 256), 256)
        at = lax.broadcasted_iota(jnp.int32, (256, TOK), 0) + q * 256
        put_one[rows, :] = jnp.where(at == slot_row, 1.0, 0.0).astype(BF)
        put_two[rows, :] = jnp.where(at == slot_row + SLOTS, 1.0, 0.0).astype(BF)
        return carry

    lax.fori_loop(0, 8, scatter_tile, 0)

    def take(k):
        d = mine_of(k)
        landed(kv_in.at[d], kv_recv.at[d])
        pltpu.make_async_remote_copy(
            src_ref=kv_in.at[d], dst_ref=kv_in.at[d], send_sem=fwd_send.at[k], recv_sem=kv_recv.at[d],
            device_id=(s, sibling), device_id_type=MESH,
        ).start()

    row = lax.broadcasted_iota(jnp.int32, (TOK, TOK), 0)
    col = lax.broadcasted_iota(jnp.int32, (TOK, TOK), 1)

    def forward_pair(k, j, diagonal):
        half = dot(q_in[k], kv_in[j, :, :HEAD], 1, 1) * (0.5 * SCALE)
        w = half + half * jnp.tanh(half)
        if diagonal:
            w = jnp.where(col <= row, w, 0.0)
        return dot(w.astype(BF), kv_in[j, :, HEAD:])

    take(0)

    def forward(k, carry):
        i = mine_of(k)

        @pl.when(k < 3)
        def _():
            take(k + 1)

        landed(q_in.at[k], q_recv.at[k])
        o = other_of(k)
        landed(kv_in.at[o], kv_recv.at[o])
        m_acc[...] = forward_pair(k, i, True)

        def inner(j, c):
            m_acc[...] += forward_pair(k, j, False)
            return c

        lax.fori_loop(0, i, inner, 0)
        m = m_acc[...]
        shift = jnp.mean(m, -1, keepdims=True).astype(BF).astype(F32)
        mix_out[k, :TOK, :] = (m - shift).astype(BF)
        wide = jnp.broadcast_to(shift, (TOK, HEAD))
        lines = jnp.zeros((16, HEAD), F32)
        line = lax.broadcasted_iota(jnp.int32, (16, HEAD), 0)
        for b in range(TOK // HEAD):
            lines += jnp.where(line == b, wide[b * HEAD : (b + 1) * HEAD].T[:16], 0.0)
        mix_out[k, TOK:, :] = lines.astype(BF)
        push(mix_out.at[k], mix_in.at[head], mix_send.at[k], mix_recv.at[head], i, base + user_core)
        return carry

    lax.fori_loop(0, 4, forward, 0)

    for h in range(HEADS):
        landed(mix_in.at[h], mix_recv.at[h])

    def post_tile(r, carry):
        start = pl.multiple_of(r * TILE, TILE)
        rows = pl.ds(start, TILE)
        alive = live_rows(start, TILE)
        pick = (lax.broadcasted_iota(jnp.int32, (16, HEAD), 0) == r).astype(F32).astype(BF)
        m = jnp.concatenate(
            [mix_in[h, rows, :].astype(F32) + dot(mix_in[h, TOK:, :], pick, 0, 0) for h in range(HEADS)], axis=1
        ) * alive
        mean = jnp.mean(m, -1, keepdims=True)
        cent = m - mean
        var = jnp.mean(cent * cent, -1, keepdims=True)
        rstd = lax.rsqrt(var + EPS)
        n = cent * rstd
        ng = n * gout_ref[...]
        g = gate[rows, :].astype(F32)
        jg = jgrad[rows, :]
        joined[rows, :] = (ng * g).astype(BF)
        pback[rows, :WIDTH] = (jg * ng * slope[rows, :WIDTH]).astype(BF)
        dn = jg * g * gout_ref[...]
        dm = rstd * (dn - jnp.mean(dn, -1, keepdims=True) - n * jnp.mean(dn * n, -1, keepdims=True))
        dm = (dm * alive).astype(BF)
        for h in range(HEADS):
            dm_out[h, rows, :] = dm[:, h * HEAD : (h + 1) * HEAD]
        return carry

    lax.fori_loop(0, TOK // TILE, post_tile, 0)
    for h in range(HEADS):
        push(dm_out.at[h], dm_in.at[slot_of_s], dm_send.at[h], dm_recv.at[slot_of_s], *worker(h))

    terms[4] = (dot(joined[...], upstream[...], 0, 0) * factor).astype(BF)
    terms[0] = (dot(normed_t[...], pback[:, :WIDTH]) * factor).astype(BF)
    for u in EARLY:
        step(u, 0)
    hidden_ref[...] = ((dot(joined[...], w_out_ref[...]) + x_ref[...].astype(F32)) * live).astype(BF)
    nback[...] = dot(pback[:, :WIDTH], w_in_ref[:, :WIDTH], 1, 1)

    for k in range(4):
        landed(dm_in.at[k], dm_recv.at[k])

    def backward_pair(k, j, diagonal):
        q, dm = q_in[k], dm_in[k]
        half = dot(kv_in[j, :, :HEAD], q, 1, 1) * (0.5 * SCALE)
        th = jnp.tanh(half)
        ht = half * th
        w = half + ht
        sb = dot(kv_in[j, :, HEAD:], dm, 1, 1) * ((0.5 + 0.5 * th) * (1.0 + half - ht))
        if diagonal:
            w = jnp.where(row <= col, w, 0.0)
            sb = jnp.where(row <= col, sb, 0.0)
        sb = sb.astype(BF)
        dkv_acc[j, :, HEAD:] += dot(w.astype(BF), dm)
        dkv_acc[j, :, :HEAD] += dot(sb, q)
        dq_acc[k] += dot(sb, kv_in[j, :, :HEAD], 0, 0)

    def send_back(out, into, send, recv, k):
        push(out.at[k], into.at[head], send.at[k], recv.at[head], mine_of(k), base + user_core)

    def finish_query(k):
        dq_out[k] = (dq_acc[k] * SCALE).astype(BF)
        send_back(dq_out, dq_in, dq_send, dq_recv, k)

    def finish_key(j):
        m = j // 2

        @pl.when(mine_of(m) == j)
        def _():
            landed(part_in.at[m], part_recv.at[m])
            total = dkv_acc[j] + part_in[m].astype(F32)
            dkv_out[m, :, :HEAD] = (total[:, :HEAD] * SCALE).astype(BF)
            dkv_out[m, :, HEAD:] = total[:, HEAD:].astype(BF)
            send_back(dkv_out, dkv_in, dkv_send, dkv_recv, m)

    def key_block(n):
        return jnp.where(upward, n, 7 - n)

    def backward(n, carry):
        j = key_block(n)
        m = j // 2
        i = mine_of(m)

        @pl.when(i == j)
        def _():
            backward_pair(m, j, True)

        def inner(k, c):
            backward_pair(k, j, False)
            return c

        lax.fori_loop(jnp.where(i > j, m, m + 1), 4, inner, 0)

        @pl.when(i != j)
        def _():
            part_out[m] = dkv_acc[j].astype(BF)
            pltpu.make_async_remote_copy(
                src_ref=part_out.at[m], dst_ref=part_in.at[m], send_sem=part_send.at[m], recv_sem=part_recv.at[m],
                device_id=(s, sibling), device_id_type=MESH,
            ).start()

        @pl.when(jnp.logical_and(i == j, upward))
        def _():
            finish_query(m)

        @pl.when(n > 0)
        def _():
            finish_key(key_block(n - 1))

        for e in range(4):

            @pl.when(n == jnp.where(upward, e, e + 3))
            def _():
                for u in EARLY:
                    step(u, e + 1)

        return carry

    lax.fori_loop(0, 8, backward, 0)

    @pl.when(jnp.logical_not(upward))
    def _():
        for k in range(4):
            finish_query(k)

    finish_key(key_block(7))
    for u in EARLY:
        step(u, 5)

    for h in range(HEADS):
        landed(dq_in.at[h], dq_recv.at[h])
        landed(dkv_in.at[h], dkv_recv.at[h])

    def gate_tile(r, carry):
        start = pl.multiple_of(r * TILE, TILE)
        rows = pl.ds(start, TILE)
        alive = live_rows(start, TILE)
        for h in range(HEADS):
            for first, piece in (
                (WIDTH, dkv_in[h, rows, HEAD:].astype(F32) * alive),
                (2 * WIDTH, dq_in[h, rows, :].astype(F32)),
                (3 * WIDTH, dkv_in[h, rows, :HEAD].astype(F32)),
            ):
                c = first + h * HEAD
                pback[rows, c : c + HEAD] = (piece * slope[rows, c : c + HEAD]).astype(BF)
        return carry

    lax.fori_loop(0, TOK // TILE, gate_tile, 0)
    for u in LATE:
        terms[u] = (dot(normed_t[...], pback[:, u * WIDTH : (u + 1) * WIDTH]) * factor).astype(BF)
        step(u, 0)
    for u in EARLY:
        step(u, 6)

    def back_tile(r, carry):
        rows = pl.ds(pl.multiple_of(r * TILE, TILE), TILE)
        nb = nback[rows, :] + dot(pback[rows, WIDTH:], w_in_ref[:, WIDTH:], 1, 1)
        x = x_ref[rows, :].astype(F32)
        mean = jnp.mean(x, -1, keepdims=True)
        cent = x - mean
        var = jnp.mean(cent * cent, -1, keepdims=True)
        rstd = lax.rsqrt(var + EPS)
        n = cent * rstd
        dn = nb * gin_ref[...]
        dx = rstd * (dn - jnp.mean(dn, -1, keepdims=True) - n * jnp.mean(dn * n, -1, keepdims=True))
        egrad[rows, :] = (dx + upstream[rows, :].astype(F32)).astype(BF)
        return carry

    lax.fori_loop(0, TOK // TILE, back_tile, 0)
    for u in LATE:
        step(u, 1)
    for u in EARLY:
        step(u, 7)

    landed(found.at[pl.ds(0, (OWNERS - 1) * 16)], row_send)

    def scatter(p, carry):
        q = lax.rem(s + p, 8)
        rows = pl.ds(pl.multiple_of(q * 256, 256), 256)
        found[rows, :] = (dot(put_one[rows, :], egrad[:, :256]) + dot(put_two[rows, :], egrad[:, 256:])).astype(BF)
        spread(found, incoming_ref, back_send, back_recv, s, t, q)
        return carry

    for n in range(4):
        lax.fori_loop(2 * n, 2 * n + 2, scatter, 0)
        if n < 3:
            for u in LATE:
                step(u, n + 2)
        if n == 1:
            for u in EARLY:
                step(u, 8)
    for n in range(5, 9):
        for u in LATE:
            step(u, n)
    landed(incoming_ref, back_recv)
    landed(found.at[pl.ds(0, (OWNERS - 1) * 16)], back_send)
    landed(req_out.at[pl.ds(0, OWNERS - 1)], req_send)

    for h in range(HEADS):
        to = worker(h)
        left(kv_out.at[h], kv_send.at[h], *to)
        left(q_out.at[h], q_send.at[h], *to)
        left(dm_out.at[h], dm_send.at[h], *to)
        landed(kv_in.at[mine_of(h)], fwd_send.at[h])
        landed(part_out.at[h], part_send.at[h])
        back = (mine_of(h), base + user_core)
        left(mix_out.at[h], mix_send.at[h], *back)
        left(dq_out.at[h], dq_send.at[h], *back)
        left(dkv_out.at[h], dkv_send.at[h], *back)


    for u in range(len(ORDERS)):
        one, two, three = ORDERS[u]
        landed(terms.at[u, other_half], s0.at[u])
        landed(sums_ref.at[u, half], s7.at[u])
        for d in range(3):
            landed(r1.at[u, d], s1.at[u, d])
            landed(r2.at[u, d], s2.at[u, d])
            landed(r3.at[u, d], s3.at[u, d])
            landed(spot(u, place[one], place[two], place[three]), s4.at[u, d])
            landed(lines(u, place[one], place[two]), s5.at[u, d])
            landed(quarter(u, place[one]), s6.at[u, d])


def layer_step(length, owner, item_row, item_table, out_grad, gain_in, gain_out, w_in, w_out, factor):
    vm, far = pl.BlockSpec(memory_space=pltpu.VMEM), pl.BlockSpec(memory_space=pl.ANY)
    dma = pltpu.SemaphoreType.DMA
    n = len(ORDERS)

    def buf(*shape, dtype=BF):
        return pltpu.VMEM(shape, dtype)

    square = buf(TOK, WIDTH)
    wide = buf(TOK, WIDTH, dtype=F32)
    heads, pairs, carried = buf(4, TOK, HEAD), buf(4, TOK, 2 * HEAD), buf(4, TOK + 16, HEAD)
    message = buf(OWNERS, 1, 128, dtype=F32)
    blocks = [
        buf(ROWS, WIDTH), square, buf(WIDTH, 4 * WIDTH), square,
        square, square, buf(n, WIDTH, WIDTH), square, square, buf(TOK, 4 * WIDTH, dtype=F32), square, square,
        square, wide, wide, buf(TOK, 4 * WIDTH),
        heads, pairs, heads, buf(8, TOK, 2 * HEAD), carried, carried, heads, heads,
        buf(4, TOK, HEAD, dtype=F32), buf(8, TOK, 2 * HEAD, dtype=F32),
        pairs, pairs, heads, pairs, heads, pairs, buf(TOK, HEAD, dtype=F32),
        message, message, buf(OWNERS * SLOTS, 128, dtype=F32), buf(ROWS, 256), buf(ROWS, 256),
        buf(TOK, 128, dtype=jnp.int32), buf(TOK, ROWS), buf(TOK, ROWS), buf(ROWS, TOK), buf(ROWS, TOK),
        buf(n, 256, WIDTH), buf(n, 256, WIDTH), buf(n, 3, 64, WIDTH), buf(n, 64, WIDTH),
        buf(n, 3, 16, WIDTH), buf(n, 16, WIDTH), buf(n, 3, 16, 128),
    ]
    one, three = dma((n,)), dma((n, 3))
    sems = [dma((c,)) for c in (4, 4, 4, 8, 4, 4, 4, 4, 4, 4, 4, 4, 4, 4, 4)]
    sems += [dma((4,))] + [dma] * 6 + [one] * 2 + [three] * 12 + [one] * 2
    return pl.pallas_call(
        functools.partial(step_kernel, factor),
        out_shape=(
            jax.ShapeDtypeStruct((TOK, WIDTH), BF),
            jax.ShapeDtypeStruct((ROWS, 256), BF),
            jax.ShapeDtypeStruct((n, WIDTH, WIDTH), BF),
            jax.ShapeDtypeStruct((8, OWNERS * SLOTS), F32),
        ),
        in_specs=[pl.BlockSpec(memory_space=pltpu.SMEM), vm, vm, far, far, vm, vm, far, far],
        out_specs=(vm,) * 4,
        scratch_shapes=blocks + sems,
        compiler_params=pltpu.CompilerParams(
            collective_id=0, has_side_effects=True, vmem_limit_bytes=62 * 1024 * 1024
        ),
    )(length, owner, item_row, item_table, out_grad, gain_in.reshape(1, -1), gain_out.reshape(1, -1), w_in, w_out)


def finish_kernel(incoming_ref, asked_ref, sums_ref, out_ref, w_in_ref, w_out_ref, rows):
    @pl.when(pl.program_id(0) == 0)
    def _():
        for q in range(8):
            both = incoming_ref[q * 256 : (q + 1) * 256, :].astype(F32).reshape(16, 16, 256)
            part = slice(q * 128, (q + 1) * 128)
            rows[part, :256] = both[:, :SLOTS].reshape(128, 256).astype(BF)
            rows[part, 256:] = both[:, SLOTS:].reshape(128, 256).astype(BF)

    at = lax.broadcasted_iota(jnp.int32, (256, OWNERS * SLOTS), 0) + pl.program_id(0) * 256
    hit = at == asked_ref[...][:1].astype(jnp.int32)
    out_ref[...] = dot(jnp.where(hit, 1.0, 0.0).astype(BF), rows[...])
    for u in range(4):
        w_in_ref[:, u * WIDTH : (u + 1) * WIDTH] = sums_ref[u].astype(F32)
    w_out_ref[...] = sums_ref[4].astype(F32)


def finish(incoming, asked, sums):
    n = len(ORDERS)
    return pl.pallas_call(
        finish_kernel,
        grid=(8,),
        out_shape=(
            jax.ShapeDtypeStruct((ROWS, WIDTH), F32),
            jax.ShapeDtypeStruct((WIDTH, 4 * WIDTH), F32),
            jax.ShapeDtypeStruct((WIDTH, WIDTH), F32),
        ),
        in_specs=[
            pl.BlockSpec((ROWS, 256), lambda i: (0, 0)),
            pl.BlockSpec((8, OWNERS * SLOTS), lambda i: (0, 0)),
            pl.BlockSpec((n, 64, WIDTH), lambda i: (0, i, 0)),
        ],
        out_specs=(
            pl.BlockSpec((256, WIDTH), lambda i: (i, 0)),
            pl.BlockSpec((64, 4 * WIDTH), lambda i: (i, 0)),
            pl.BlockSpec((64, WIDTH), lambda i: (i, 0)),
        ),
        scratch_shapes=[pltpu.VMEM((OWNERS * SLOTS, WIDTH), BF)],
        compiler_params=pltpu.CompilerParams(vmem_limit_bytes=60 * 1024 * 1024),
    )(incoming, asked, sums)


def local(item_table, owner, item_row, lengths, gain_in, gain_out, w_in, w_out, out_grad):
    factor = (TOK * OWNERS) ** (-0.5)
    hidden, incoming, sums, asked = layer_step(
        lengths, owner.reshape(1, TOK), item_row, item_table, out_grad[0], gain_in, gain_out, w_in, w_out, factor
    )
    table_grad, w_in_grad, w_out_grad = finish(incoming, asked, sums)
    return (hidden[None], table_grad, w_in_grad, w_out_grad)


def solution(mesh):
    placed = (
        P(("seq", "table"), None),
        P("table", "seq", None),
        P("table", "seq"),
        P("table"),
        P(),
        P(),
        P(),
        P(),
        P("table", "seq", None),
    )
    return jax.shard_map(
        local,
        mesh=mesh,
        in_specs=placed,
        out_specs=(P("table", "seq", None), P(("seq", "table"), None), P(), P()),
        check_vma=False,
    )
```

```python
import functools

import jax
import jax.numpy as jnp
from jax import lax
from jax.experimental import pallas as pl
from jax.experimental.pallas import tpu as pltpu
from jax.sharding import PartitionSpec as P

HEADS = 4
HEAD = 128
TOK = 512
WIDTH = 512
TILE = 128
SCALE = HEAD ** (-0.5)
EPS = 1e-05
MESH = pl.DeviceIdType.MESH
BF = jnp.bfloat16
F32 = jnp.float32


def dot(a, b, ca=1, cb=0):
    return lax.dot_general(a, b, (((ca,), (cb,)), ((), ())), preferred_element_type=F32)


def landed(ref, sem):
    pltpu.make_async_copy(ref, ref, sem).wait()


OWNERS = 128
SLOTS = 8
ROWS = 2048


def greet_all(s, t):
    barrier = pltpu.get_barrier_semaphore()
    me = s * 16 + t

    def greet(d, carry):
        other = lax.rem(me + d, OWNERS)
        pl.semaphore_signal(
            barrier, inc=1, device_id=(other // 16, lax.rem(other, 16)), device_id_type=MESH
        )
        return carry

    lax.fori_loop(1, OWNERS, greet, 0)
    return barrier


def send_rows(src, dst, send, recv, s, t, to_s, to_t, take, place):
    mine = jnp.logical_and(to_s == s, to_t == t)

    @pl.when(mine)
    def _():
        pltpu.make_async_copy(src.at[take], dst.at[place], recv).start()

    @pl.when(jnp.logical_not(mine))
    def _():
        pltpu.make_async_remote_copy(
            src_ref=src.at[take], dst_ref=dst.at[place], send_sem=send, recv_sem=recv,
            device_id=(to_s, to_t), device_id_type=MESH,
        ).start()


def sixteen(index):
    return pl.ds(pl.multiple_of(index * 16, 16), 16)


def spread(src, dst, send, recv, s, t, to_s):
    def one(p, carry):
        to_t = lax.rem(t + p, 16)
        send_rows(src, dst, send, recv, s, t, to_s, to_t, sixteen(to_s * 16 + to_t), sixteen(s * 16 + t))
        return carry

    lax.fori_loop(0, 16, one, 0)


ORDERS = ("zxy", "xyz", "yzx", "zxy", "zyx")
EARLY = (0, 4)
LATE = (1, 2, 3)


def step_kernel(
    factor,
    len_ref, owner_ref, row_ref, table_hbm, og_hbm, gin_ref, gout_ref, w_in_hbm, w_out_hbm,
    hidden_ref, incoming_ref, sums_ref, asked_ref,
    table_ref, og_ref, w_in_ref, w_out_ref, x_ref, egrad, terms, normed, normed_t, slope, gate, upstream, joined, jgrad, nback, pback,
    q_out, kv_out, q_in, kv_in, mix_out, mix_in, dm_out, dm_in,
    dq_acc, dkv_acc, part_out, part_in, dq_out, dkv_out, dq_in, dkv_in, m_acc,
    req_out, req_in, asked_col, found, fetched, spot_col, pick_one, pick_two, put_one, put_two,
    r0, a1, r1, a2, r2, a3, r3,
    q_send, q_recv, kv_send, kv_recv, fwd_send, mix_send, mix_recv, dm_send, dm_recv,
    part_send, part_recv, dq_send, dq_recv, dkv_send, dkv_recv,
    load_sem, req_send, req_recv, row_send, row_recv, back_send, back_recv,
    s0, v0, s1, v1, s2, v2, s3, v3, s4, v4, s5, v5, s6, v6, s7, v7,
):
    s = lax.axis_index("seq")
    t = lax.axis_index("table")
    me = s * 16 + t
    core = lax.rem(t, 2)
    base = t - core
    head = lax.rem(s, HEADS)
    user_core = lax.rem(lax.rem(s, HEADS) + s // HEADS, 2)
    upward = user_core == 1
    sibling = base + 1 - core
    part_of_s = lax.rem((s + 1) // 2, 2)
    slot_of_s = s // 2
    cx, cz = lax.rem(s, 4), t // 4
    cy = lax.rem(t // 2, 2) * 2 + s // 4
    barrier = greet_all(s, t)

    def push(src, dst, send, recv, to_s, to_t):
        mine = jnp.logical_and(to_s == s, to_t == t)

        @pl.when(mine)
        def _():
            pltpu.make_async_copy(src, dst, recv).start()

        @pl.when(jnp.logical_not(mine))
        def _():
            pltpu.make_async_remote_copy(
                src_ref=src, dst_ref=dst, send_sem=send, recv_sem=recv,
                device_id=(to_s, to_t), device_id_type=MESH,
            ).start()

    def left(src, send, to_s, to_t):
        @pl.when(jnp.logical_not(jnp.logical_and(to_s == s, to_t == t)))
        def _():
            landed(src, send)

    def worker(h):
        return lax.rem(core + h, 2) * HEADS + h, base + part_of_s

    def mine_of(k):
        return 2 * k + lax.rem(k + core, 2)

    def other_of(k):
        return 2 * k + lax.rem(k + core + 1, 2)

    length = len_ref[0]

    def live_rows(start, count):
        pos = s * TOK + start + lax.broadcasted_iota(jnp.int32, (count, 1), 0)
        return (pos < length).astype(F32)

    place = {"x": cx, "y": cy, "z": cz}

    def partner(axis, d):
        other = lax.rem(place[axis] + d, 4)
        if axis == "x":
            return other, s - cx + other, t
        if axis == "y":
            return other, lax.rem(other, 2) * 4 + cx, cz * 4 + (other // 2) * 2 + core
        return other, s, other * 4 + lax.rem(t, 4)

    def ship(src, dst, send, recv, to_s, to_t):
        pltpu.make_async_remote_copy(
            src_ref=src, dst_ref=dst, send_sem=send, recv_sem=recv,
            device_id=(to_s, to_t), device_id_type=MESH,
        ).start()

    half = pl.ds(pl.multiple_of(core * 256, 256), 256)
    other_half = pl.ds(pl.multiple_of(256 - core * 256, 256), 256)

    def block_of(index, size):
        return pl.ds(pl.multiple_of(index * size, size), size)

    def block(axis, size):
        return block_of(place[axis], size)

    def spot(u, first, second, third):
        return sums_ref.at[u, block_of(core * 16 + first * 4 + second, 16), block_of(third, 128)]

    def lines(u, first, second):
        return sums_ref.at[u, block_of(core * 16 + first * 4 + second, 16)]

    def quarter(u, first):
        return sums_ref.at[u, block_of(core * 4 + first, 64)]

    def before_me(axis, d):
        return lax.rem(place[axis] + 4 - d, 4)

    def step(u, n):
        one, two, three = ORDERS[u]
        if n == 0:
            ship(terms.at[u, other_half], r0.at[u], s0.at[u], v0.at[u], s, sibling)
        elif n == 1:
            landed(r0.at[u], v0.at[u])
            a1[u] = (terms[u, half, :].astype(F32) + r0[u].astype(F32)).astype(BF)
            for d in range(1, 4):
                other, to_s, to_t = partner(one, d)
                ship(a1.at[u, block_of(other, 64)], r1.at[u, d - 1], s1.at[u, d - 1], v1.at[u, d - 1], to_s, to_t)
        elif n == 2:
            total = a1[u, block(one, 64), :].astype(F32)
            for d in range(1, 4):
                landed(r1.at[u, d - 1], v1.at[u, d - 1])
                total += r1[u, d - 1].astype(F32)
            a2[u] = total.astype(BF)
            for d in range(1, 4):
                other, to_s, to_t = partner(two, d)
                ship(a2.at[u, block_of(other, 16)], r2.at[u, d - 1], s2.at[u, d - 1], v2.at[u, d - 1], to_s, to_t)
        elif n == 3:
            total = a2[u, block(two, 16), :].astype(F32)
            for d in range(1, 4):
                landed(r2.at[u, d - 1], v2.at[u, d - 1])
                total += r2[u, d - 1].astype(F32)
            a3[u] = total.astype(BF)
            for d in range(1, 4):
                other, to_s, to_t = partner(three, d)
                ship(
                    a3.at[u, :, block_of(other, 128)], r3.at[u, d - 1], s3.at[u, d - 1], v3.at[u, d - 1], to_s, to_t
                )
        elif n == 4:
            total = a3[u, :, block(three, 128)].astype(F32)
            for d in range(1, 4):
                landed(r3.at[u, d - 1], v3.at[u, d - 1])
                total += r3[u, d - 1].astype(F32)
            mine = spot(u, place[one], place[two], place[three])
            mine[...] = total.astype(BF)
            for d in range(1, 4):
                _, to_s, to_t = partner(three, d)
                ship(mine, mine, s4.at[u, d - 1], v4.at[u, d - 1], to_s, to_t)
        elif n == 5:
            for d in range(1, 4):
                landed(spot(u, place[one], place[two], before_me(three, d)), v4.at[u, d - 1])
            mine = lines(u, place[one], place[two])
            for d in range(1, 4):
                _, to_s, to_t = partner(two, d)
                ship(mine, mine, s5.at[u, d - 1], v5.at[u, d - 1], to_s, to_t)
        elif n == 6:
            for d in range(1, 4):
                landed(lines(u, place[one], before_me(two, d)), v5.at[u, d - 1])
            mine = quarter(u, place[one])
            for d in range(1, 4):
                _, to_s, to_t = partner(one, d)
                ship(mine, mine, s6.at[u, d - 1], v6.at[u, d - 1], to_s, to_t)
        elif n == 7:
            for d in range(1, 4):
                landed(quarter(u, before_me(one, d)), v6.at[u, d - 1])
            ship(sums_ref.at[u, half], sums_ref.at[u, half], s7.at[u], v7.at[u], s, sibling)
        else:
            landed(sums_ref.at[u, other_half], v7.at[u])

    copies = [
        pltpu.make_async_copy(src, dst, load_sem.at[n])
        for n, (src, dst) in enumerate(
            ((table_hbm, table_ref), (og_hbm, og_ref), (w_out_hbm, w_out_ref), (w_in_hbm, w_in_ref))
        )
    ]
    for copy in copies:
        copy.start()

    target = owner_ref[...]
    line_e = lax.broadcasted_iota(jnp.int32, (OWNERS, TOK), 0)
    chosen_mask = line_e == target
    chosen = jnp.where(chosen_mask, 1.0, 0.0).astype(BF)
    above = jnp.where(
        lax.broadcasted_iota(jnp.int32, (TOK, TOK), 0) < lax.broadcasted_iota(jnp.int32, (TOK, TOK), 1), 1.0, 0.0
    ).astype(BF)
    before = dot(chosen, above)
    rank = jnp.sum(jnp.where(chosen_mask, before, 0.0), axis=0, keepdims=True).astype(jnp.int32)
    value = row_ref[...] + 1
    high = (value >> 7).astype(F32)
    low = (value & 127).astype(F32)
    message = jnp.where(line_e == rank, high, 0.0) + jnp.where(line_e == rank + SLOTS, low, 0.0)
    req_out[:, 0, :] = dot(chosen, message.astype(BF), 1, 1)
    pl.semaphore_wait(barrier, OWNERS - 1)

    def ask(p, carry):
        other = lax.rem(me + p, OWNERS)
        send_rows(
            req_out, req_in, req_send, req_recv, s, t, other // 16, lax.rem(other, 16), other, me
        )
        return carry

    lax.fori_loop(0, OWNERS, ask, 0)

    slot_row = target * 16 + rank
    spot_col[...] = jnp.broadcast_to(slot_row.astype(F32), (128, TOK)).T.astype(jnp.int32)
    live = live_rows(0, TOK)
    copies[1].wait()
    copies[2].wait()
    upstream[...] = (og_ref[...].astype(F32) * live).astype(BF)
    jgrad[...] = dot(upstream[...], w_out_ref[...], 1, 1)
    number = lax.broadcasted_iota(jnp.int32, (OWNERS * SLOTS, OWNERS), 0)
    lane_s = lax.broadcasted_iota(jnp.int32, (OWNERS * SLOTS, OWNERS), 1)
    expand = jnp.where((number >> 3) == lane_s, 1.0, 0.0).astype(BF)
    landed(req_in, req_recv)
    values = dot(expand, req_in[:, 0, :].astype(BF))
    own = number & 7
    asked = (
        jnp.sum(
            jnp.where(lane_s == own, values * 128.0, 0.0) + jnp.where(lane_s == own + SLOTS, values, 0.0),
            axis=1,
            keepdims=True,
        )
        - 1.0
    )
    wide = jnp.broadcast_to(asked, (OWNERS * SLOTS, 128))
    asked_col[...] = wide
    asked_ref[...] = wide.T[:8]

    copies[0].wait()

    def gather(p, carry):
        q = lax.rem(s + p, 8)
        column = asked_col[pl.ds(pl.multiple_of(q * 128, 128), 128), :][:, :1].astype(jnp.int32)
        hit = lax.broadcasted_iota(jnp.int32, (128, ROWS), 1) == column
        rows = dot(jnp.where(hit, 1.0, 0.0).astype(BF), table_ref[...])
        both = jnp.concatenate(
            [rows[:, :256].reshape(16, SLOTS, 256), rows[:, 256:].reshape(16, SLOTS, 256)], axis=1
        )
        found[pl.ds(pl.multiple_of(q * 256, 256), 256), :] = both.reshape(256, 256).astype(BF)
        spread(found, fetched, row_send, row_recv, s, t, q)
        return carry

    lax.fori_loop(0, 8, gather, 0)
    def pick_tile(r, carry):
        rows = pl.ds(pl.multiple_of(r * TILE, TILE), TILE)
        at = lax.broadcasted_iota(jnp.int32, (TILE, ROWS), 1)
        spots = spot_col[rows, :][:, :1]
        pick_one[rows, :] = jnp.where(at == spots, 1.0, 0.0).astype(BF)
        pick_two[rows, :] = jnp.where(at == spots + SLOTS, 1.0, 0.0).astype(BF)
        return carry

    lax.fori_loop(0, TOK // TILE, pick_tile, 0)
    dq_acc[...] = jnp.zeros_like(dq_acc)
    dkv_acc[...] = jnp.zeros_like(dkv_acc)
    copies[3].wait()
    landed(fetched, row_recv)

    def norm_tile(r, carry):
        rows = pl.ds(pl.multiple_of(r * TILE, TILE), TILE)
        x_ref[rows, :256] = dot(pick_one[rows, :], fetched[...]).astype(BF)
        x_ref[rows, 256:] = dot(pick_two[rows, :], fetched[...]).astype(BF)
        x = x_ref[rows, :].astype(F32)
        mean = jnp.mean(x, -1, keepdims=True)
        cent = x - mean
        var = jnp.mean(cent * cent, -1, keepdims=True)
        normed[rows, :] = (cent * lax.rsqrt(var + EPS) * gin_ref[...]).astype(BF)
        return carry

    lax.fori_loop(0, TOK // TILE, norm_tile, 0)

    def project(first, columns):
        pre = dot(normed[...], w_in_ref[:, pl.ds(first, columns)])
        half = 0.5 * pre
        th = jnp.tanh(half)
        slope[:, pl.ds(first, columns)] = 0.5 * (1.0 + th) * (1.0 + half - half * th)
        return half + half * th

    for h in range(HEADS):
        kv_out[h, :, :HEAD] = project(3 * WIDTH + h * HEAD, HEAD).astype(BF)
        kv_out[h, :, HEAD:] = (project(WIDTH + h * HEAD, HEAD) * live).astype(BF)
        to = worker(h)
        push(kv_out.at[h], kv_in.at[s], kv_send.at[h], kv_recv.at[s], *to)
        q_out[h] = project(2 * WIDTH + h * HEAD, HEAD).astype(BF)
        push(q_out.at[h], q_in.at[slot_of_s], q_send.at[h], q_recv.at[slot_of_s], *to)

    gate[:, :256] = project(0, 256).astype(BF)
    gate[:, 256:] = project(256, 256).astype(BF)
    normed_t[...] = normed[...].T

    def scatter_tile(q, carry):
        rows = pl.ds(pl.multiple_of(q * 256, 256), 256)
        at = lax.broadcasted_iota(jnp.int32, (256, TOK), 0) + q * 256
        put_one[rows, :] = jnp.where(at == slot_row, 1.0, 0.0).astype(BF)
        put_two[rows, :] = jnp.where(at == slot_row + SLOTS, 1.0, 0.0).astype(BF)
        return carry

    lax.fori_loop(0, 8, scatter_tile, 0)

    def take(k):
        d = mine_of(k)
        landed(kv_in.at[d], kv_recv.at[d])
        pltpu.make_async_remote_copy(
            src_ref=kv_in.at[d], dst_ref=kv_in.at[d], send_sem=fwd_send.at[k], recv_sem=kv_recv.at[d],
            device_id=(s, sibling), device_id_type=MESH,
        ).start()

    row = lax.broadcasted_iota(jnp.int32, (TOK, TOK), 0)
    col = lax.broadcasted_iota(jnp.int32, (TOK, TOK), 1)

    def forward_pair(k, j, diagonal):
        half = dot(q_in[k], kv_in[j, :, :HEAD], 1, 1) * (0.5 * SCALE)
        w = half + half * jnp.tanh(half)
        if diagonal:
            w = jnp.where(col <= row, w, 0.0)
        return dot(w.astype(BF), kv_in[j, :, HEAD:])

    take(0)

    def forward(k, carry):
        i = mine_of(k)

        @pl.when(k < 3)
        def _():
            take(k + 1)

        landed(q_in.at[k], q_recv.at[k])
        o = other_of(k)
        landed(kv_in.at[o], kv_recv.at[o])
        m_acc[...] = forward_pair(k, i, True)

        def inner(j, c):
            m_acc[...] += forward_pair(k, j, False)
            return c

        lax.fori_loop(0, i, inner, 0)
        m = m_acc[...]
        shift = jnp.mean(m, -1, keepdims=True).astype(BF).astype(F32)
        mix_out[k, :TOK, :] = (m - shift).astype(BF)
        wide = jnp.broadcast_to(shift, (TOK, HEAD))
        lines = jnp.zeros((16, HEAD), F32)
        line = lax.broadcasted_iota(jnp.int32, (16, HEAD), 0)
        for b in range(TOK // HEAD):
            lines += jnp.where(line == b, wide[b * HEAD : (b + 1) * HEAD].T[:16], 0.0)
        mix_out[k, TOK:, :] = lines.astype(BF)
        push(mix_out.at[k], mix_in.at[head], mix_send.at[k], mix_recv.at[head], i, base + user_core)
        return carry

    lax.fori_loop(0, 4, forward, 0)

    for h in range(HEADS):
        landed(mix_in.at[h], mix_recv.at[h])

    def post_tile(r, carry):
        start = pl.multiple_of(r * TILE, TILE)
        rows = pl.ds(start, TILE)
        alive = live_rows(start, TILE)
        pick = (lax.broadcasted_iota(jnp.int32, (16, HEAD), 0) == r).astype(F32).astype(BF)
        m = jnp.concatenate(
            [mix_in[h, rows, :].astype(F32) + dot(mix_in[h, TOK:, :], pick, 0, 0) for h in range(HEADS)], axis=1
        ) * alive
        mean = jnp.mean(m, -1, keepdims=True)
        cent = m - mean
        var = jnp.mean(cent * cent, -1, keepdims=True)
        rstd = lax.rsqrt(var + EPS)
        n = cent * rstd
        ng = n * gout_ref[...]
        g = gate[rows, :].astype(F32)
        jg = jgrad[rows, :]
        joined[rows, :] = (ng * g).astype(BF)
        pback[rows, :WIDTH] = (jg * ng * slope[rows, :WIDTH]).astype(BF)
        dn = jg * g * gout_ref[...]
        dm = rstd * (dn - jnp.mean(dn, -1, keepdims=True) - n * jnp.mean(dn * n, -1, keepdims=True))
        dm = (dm * alive).astype(BF)
        for h in range(HEADS):
            dm_out[h, rows, :] = dm[:, h * HEAD : (h + 1) * HEAD]
        return carry

    lax.fori_loop(0, TOK // TILE, post_tile, 0)
    for h in range(HEADS):
        push(dm_out.at[h], dm_in.at[slot_of_s], dm_send.at[h], dm_recv.at[slot_of_s], *worker(h))

    terms[4] = (dot(joined[...], upstream[...], 0, 0) * factor).astype(BF)
    terms[0] = (dot(normed_t[...], pback[:, :WIDTH]) * factor).astype(BF)
    for u in EARLY:
        step(u, 0)
    hidden_ref[...] = ((dot(joined[...], w_out_ref[...]) + x_ref[...].astype(F32)) * live).astype(BF)
    nback[...] = dot(pback[:, :WIDTH], w_in_ref[:, :WIDTH], 1, 1)
    for u in EARLY:
        step(u, 1)

    for k in range(4):
        landed(dm_in.at[k], dm_recv.at[k])

    def backward_pair(k, j, diagonal):
        q, dm = q_in[k], dm_in[k]
        half = dot(kv_in[j, :, :HEAD], q, 1, 1) * (0.5 * SCALE)
        th = jnp.tanh(half)
        ht = half * th
        w = half + ht
        sb = dot(kv_in[j, :, HEAD:], dm, 1, 1) * ((0.5 + 0.5 * th) * (1.0 + half - ht))
        if diagonal:
            w = jnp.where(row <= col, w, 0.0)
            sb = jnp.where(row <= col, sb, 0.0)
        sb = sb.astype(BF)
        dkv_acc[j, :, HEAD:] += dot(w.astype(BF), dm)
        dkv_acc[j, :, :HEAD] += dot(sb, q)
        dq_acc[k] += dot(sb, kv_in[j, :, :HEAD], 0, 0)

    def send_back(out, into, send, recv, k):
        push(out.at[k], into.at[head], send.at[k], recv.at[head], mine_of(k), base + user_core)

    def finish_query(k):
        dq_out[k] = (dq_acc[k] * SCALE).astype(BF)
        send_back(dq_out, dq_in, dq_send, dq_recv, k)

    def finish_key(j):
        m = j // 2

        @pl.when(mine_of(m) == j)
        def _():
            landed(part_in.at[m], part_recv.at[m])
            total = dkv_acc[j] + part_in[m].astype(F32)
            dkv_out[m, :, :HEAD] = (total[:, :HEAD] * SCALE).astype(BF)
            dkv_out[m, :, HEAD:] = total[:, HEAD:].astype(BF)
            send_back(dkv_out, dkv_in, dkv_send, dkv_recv, m)

    def key_block(n):
        return jnp.where(upward, n, 7 - n)

    def backward(n, carry):
        j = key_block(n)
        m = j // 2
        i = mine_of(m)

        @pl.when(i == j)
        def _():
            backward_pair(m, j, True)

        def inner(k, c):
            backward_pair(k, j, False)
            return c

        lax.fori_loop(jnp.where(i > j, m, m + 1), 4, inner, 0)

        @pl.when(i != j)
        def _():
            part_out[m] = dkv_acc[j].astype(BF)
            pltpu.make_async_remote_copy(
                src_ref=part_out.at[m], dst_ref=part_in.at[m], send_sem=part_send.at[m], recv_sem=part_recv.at[m],
                device_id=(s, sibling), device_id_type=MESH,
            ).start()

        @pl.when(jnp.logical_and(i == j, upward))
        def _():
            finish_query(m)

        @pl.when(n > 0)
        def _():
            finish_key(key_block(n - 1))

        return carry

    lax.fori_loop(0, 8, backward, 0)

    @pl.when(jnp.logical_not(upward))
    def _():
        for k in range(4):
            finish_query(k)

    finish_key(key_block(7))
    for u in EARLY:
        step(u, 2)

    for h in range(HEADS):
        landed(dq_in.at[h], dq_recv.at[h])
        landed(dkv_in.at[h], dkv_recv.at[h])

    def gate_tile(r, carry):
        start = pl.multiple_of(r * TILE, TILE)
        rows = pl.ds(start, TILE)
        alive = live_rows(start, TILE)
        for h in range(HEADS):
            for first, piece in (
                (WIDTH, dkv_in[h, rows, HEAD:].astype(F32) * alive),
                (2 * WIDTH, dq_in[h, rows, :].astype(F32)),
                (3 * WIDTH, dkv_in[h, rows, :HEAD].astype(F32)),
            ):
                c = first + h * HEAD
                pback[rows, c : c + HEAD] = (piece * slope[rows, c : c + HEAD]).astype(BF)
        return carry

    lax.fori_loop(0, TOK // TILE, gate_tile, 0)
    for u in LATE:
        terms[u] = (dot(normed_t[...], pback[:, u * WIDTH : (u + 1) * WIDTH]) * factor).astype(BF)
        step(u, 0)
    for u in EARLY:
        step(u, 3)

    def back_tile(r, carry):
        rows = pl.ds(pl.multiple_of(r * TILE, TILE), TILE)
        nb = nback[rows, :] + dot(pback[rows, WIDTH:], w_in_ref[:, WIDTH:], 1, 1)
        x = x_ref[rows, :].astype(F32)
        mean = jnp.mean(x, -1, keepdims=True)
        cent = x - mean
        var = jnp.mean(cent * cent, -1, keepdims=True)
        rstd = lax.rsqrt(var + EPS)
        n = cent * rstd
        dn = nb * gin_ref[...]
        dx = rstd * (dn - jnp.mean(dn, -1, keepdims=True) - n * jnp.mean(dn * n, -1, keepdims=True))
        egrad[rows, :] = (dx + upstream[rows, :].astype(F32)).astype(BF)
        return carry

    lax.fori_loop(0, TOK // TILE, back_tile, 0)
    for u in LATE:
        step(u, 1)
    for u in EARLY:
        step(u, 4)

    landed(found.at[pl.ds(0, (OWNERS - 1) * 16)], row_send)

    def scatter(p, carry):
        q = lax.rem(s + p, 8)
        rows = pl.ds(pl.multiple_of(q * 256, 256), 256)
        found[rows, :] = (dot(put_one[rows, :], egrad[:, :256]) + dot(put_two[rows, :], egrad[:, 256:])).astype(BF)
        spread(found, incoming_ref, back_send, back_recv, s, t, q)
        return carry

    for n in range(4):
        lax.fori_loop(2 * n, 2 * n + 2, scatter, 0)
        if n < 3:
            for u in LATE:
                step(u, n + 2)
            for u in EARLY:
                step(u, n + 5)
    for n in range(5, 9):
        for u in LATE:
            step(u, n)
        if n == 5:
            for u in EARLY:
                step(u, 8)
    landed(incoming_ref, back_recv)
    landed(found.at[pl.ds(0, (OWNERS - 1) * 16)], back_send)
    landed(req_out.at[pl.ds(0, OWNERS - 1)], req_send)

    for h in range(HEADS):
        to = worker(h)
        left(kv_out.at[h], kv_send.at[h], *to)
        left(q_out.at[h], q_send.at[h], *to)
        left(dm_out.at[h], dm_send.at[h], *to)
        landed(kv_in.at[mine_of(h)], fwd_send.at[h])
        landed(part_out.at[h], part_send.at[h])
        back = (mine_of(h), base + user_core)
        left(mix_out.at[h], mix_send.at[h], *back)
        left(dq_out.at[h], dq_send.at[h], *back)
        left(dkv_out.at[h], dkv_send.at[h], *back)


    for u in range(len(ORDERS)):
        one, two, three = ORDERS[u]
        landed(terms.at[u, other_half], s0.at[u])
        landed(sums_ref.at[u, half], s7.at[u])
        for d in range(3):
            landed(r1.at[u, d], s1.at[u, d])
            landed(r2.at[u, d], s2.at[u, d])
            landed(r3.at[u, d], s3.at[u, d])
            landed(spot(u, place[one], place[two], place[three]), s4.at[u, d])
            landed(lines(u, place[one], place[two]), s5.at[u, d])
            landed(quarter(u, place[one]), s6.at[u, d])


def layer_step(length, owner, item_row, item_table, out_grad, gain_in, gain_out, w_in, w_out, factor):
    vm, far = pl.BlockSpec(memory_space=pltpu.VMEM), pl.BlockSpec(memory_space=pl.ANY)
    dma = pltpu.SemaphoreType.DMA
    n = len(ORDERS)

    def buf(*shape, dtype=BF):
        return pltpu.VMEM(shape, dtype)

    square = buf(TOK, WIDTH)
    wide = buf(TOK, WIDTH, dtype=F32)
    heads, pairs, carried = buf(4, TOK, HEAD), buf(4, TOK, 2 * HEAD), buf(4, TOK + 16, HEAD)
    message = buf(OWNERS, 1, 128, dtype=F32)
    blocks = [
        buf(ROWS, WIDTH), square, buf(WIDTH, 4 * WIDTH), square,
        square, square, buf(n, WIDTH, WIDTH), square, square, buf(TOK, 4 * WIDTH, dtype=F32), square, square,
        square, wide, wide, buf(TOK, 4 * WIDTH),
        heads, pairs, heads, buf(8, TOK, 2 * HEAD), carried, carried, heads, heads,
        buf(4, TOK, HEAD, dtype=F32), buf(8, TOK, 2 * HEAD, dtype=F32),
        pairs, pairs, heads, pairs, heads, pairs, buf(TOK, HEAD, dtype=F32),
        message, message, buf(OWNERS * SLOTS, 128, dtype=F32), buf(ROWS, 256), buf(ROWS, 256),
        buf(TOK, 128, dtype=jnp.int32), buf(TOK, ROWS), buf(TOK, ROWS), buf(ROWS, TOK), buf(ROWS, TOK),
        buf(n, 256, WIDTH), buf(n, 256, WIDTH), buf(n, 3, 64, WIDTH), buf(n, 64, WIDTH),
        buf(n, 3, 16, WIDTH), buf(n, 16, WIDTH), buf(n, 3, 16, 128),
    ]
    one, three = dma((n,)), dma((n, 3))
    sems = [dma((c,)) for c in (4, 4, 4, 8, 4, 4, 4, 4, 4, 4, 4, 4, 4, 4, 4)]
    sems += [dma((4,))] + [dma] * 6 + [one] * 2 + [three] * 12 + [one] * 2
    return pl.pallas_call(
        functools.partial(step_kernel, factor),
        out_shape=(
            jax.ShapeDtypeStruct((TOK, WIDTH), BF),
            jax.ShapeDtypeStruct((ROWS, 256), BF),
            jax.ShapeDtypeStruct((n, WIDTH, WIDTH), BF),
            jax.ShapeDtypeStruct((8, OWNERS * SLOTS), F32),
        ),
        in_specs=[pl.BlockSpec(memory_space=pltpu.SMEM), vm, vm, far, far, vm, vm, far, far],
        out_specs=(vm,) * 4,
        scratch_shapes=blocks + sems,
        compiler_params=pltpu.CompilerParams(
            collective_id=0, has_side_effects=True, vmem_limit_bytes=62 * 1024 * 1024
        ),
    )(length, owner, item_row, item_table, out_grad, gain_in.reshape(1, -1), gain_out.reshape(1, -1), w_in, w_out)


def finish_kernel(incoming_ref, asked_ref, sums_ref, out_ref, w_in_ref, w_out_ref, rows):
    @pl.when(pl.program_id(0) == 0)
    def _():
        for q in range(8):
            both = incoming_ref[q * 256 : (q + 1) * 256, :].astype(F32).reshape(16, 16, 256)
            part = slice(q * 128, (q + 1) * 128)
            rows[part, :256] = both[:, :SLOTS].reshape(128, 256).astype(BF)
            rows[part, 256:] = both[:, SLOTS:].reshape(128, 256).astype(BF)

    at = lax.broadcasted_iota(jnp.int32, (256, OWNERS * SLOTS), 0) + pl.program_id(0) * 256
    hit = at == asked_ref[...][:1].astype(jnp.int32)
    out_ref[...] = dot(jnp.where(hit, 1.0, 0.0).astype(BF), rows[...])
    for u in range(4):
        w_in_ref[:, u * WIDTH : (u + 1) * WIDTH] = sums_ref[u].astype(F32)
    w_out_ref[...] = sums_ref[4].astype(F32)


def finish(incoming, asked, sums):
    n = len(ORDERS)
    return pl.pallas_call(
        finish_kernel,
        grid=(8,),
        out_shape=(
            jax.ShapeDtypeStruct((ROWS, WIDTH), F32),
            jax.ShapeDtypeStruct((WIDTH, 4 * WIDTH), F32),
            jax.ShapeDtypeStruct((WIDTH, WIDTH), F32),
        ),
        in_specs=[
            pl.BlockSpec((ROWS, 256), lambda i: (0, 0)),
            pl.BlockSpec((8, OWNERS * SLOTS), lambda i: (0, 0)),
            pl.BlockSpec((n, 64, WIDTH), lambda i: (0, i, 0)),
        ],
        out_specs=(
            pl.BlockSpec((256, WIDTH), lambda i: (i, 0)),
            pl.BlockSpec((64, 4 * WIDTH), lambda i: (i, 0)),
            pl.BlockSpec((64, WIDTH), lambda i: (i, 0)),
        ),
        scratch_shapes=[pltpu.VMEM((OWNERS * SLOTS, WIDTH), BF)],
        compiler_params=pltpu.CompilerParams(vmem_limit_bytes=60 * 1024 * 1024),
    )(incoming, asked, sums)


def local(item_table, owner, item_row, lengths, gain_in, gain_out, w_in, w_out, out_grad):
    factor = (TOK * OWNERS) ** (-0.5)
    hidden, incoming, sums, asked = layer_step(
        lengths, owner.reshape(1, TOK), item_row, item_table, out_grad[0], gain_in, gain_out, w_in, w_out, factor
    )
    table_grad, w_in_grad, w_out_grad = finish(incoming, asked, sums)
    return (hidden[None], table_grad, w_in_grad, w_out_grad)


def solution(mesh):
    placed = (
        P(("seq", "table"), None),
        P("table", "seq", None),
        P("table", "seq"),
        P("table"),
        P(),
        P(),
        P(),
        P(),
        P("table", "seq", None),
    )
    return jax.shard_map(
        local,
        mesh=mesh,
        in_specs=placed,
        out_specs=(P("table", "seq", None), P(("seq", "table"), None), P(), P()),
        check_vma=False,
    )
```

```python
import functools

import jax
import jax.numpy as jnp
from jax import lax
from jax.experimental import pallas as pl
from jax.experimental.pallas import tpu as pltpu
from jax.sharding import PartitionSpec as P

HEADS = 4
HEAD = 128
TOK = 512
WIDTH = 512
TILE = 128
SCALE = HEAD ** (-0.5)
EPS = 1e-05
MESH = pl.DeviceIdType.MESH
BF = jnp.bfloat16
F32 = jnp.float32


def dot(a, b, ca=1, cb=0):
    return lax.dot_general(a, b, (((ca,), (cb,)), ((), ())), preferred_element_type=F32)


def landed(ref, sem):
    pltpu.make_async_copy(ref, ref, sem).wait()


OWNERS = 128
SLOTS = 8
ROWS = 2048


def greet_all(s, t):
    barrier = pltpu.get_barrier_semaphore()
    me = s * 16 + t

    def greet(d, carry):
        other = lax.rem(me + d, OWNERS)
        pl.semaphore_signal(
            barrier, inc=1, device_id=(other // 16, lax.rem(other, 16)), device_id_type=MESH
        )
        return carry

    lax.fori_loop(1, OWNERS, greet, 0)
    return barrier


def send_rows(src, dst, send, recv, s, t, to_s, to_t, take, place):
    mine = jnp.logical_and(to_s == s, to_t == t)

    @pl.when(mine)
    def _():
        pltpu.make_async_copy(src.at[take], dst.at[place], recv).start()

    @pl.when(jnp.logical_not(mine))
    def _():
        pltpu.make_async_remote_copy(
            src_ref=src.at[take], dst_ref=dst.at[place], send_sem=send, recv_sem=recv,
            device_id=(to_s, to_t), device_id_type=MESH,
        ).start()


def sixteen(index):
    return pl.ds(pl.multiple_of(index * 16, 16), 16)


def spread(src, dst, send, recv, s, t, to_s, part):
    send_rows(src, dst, send, recv, s, t, to_s, t, part(to_s * 16 + t), part(s * 16 + t))
    for p in range(1, 16):
        to_t = lax.rem(t + p, 16)
        pltpu.make_async_remote_copy(
            src_ref=src.at[part(to_s * 16 + to_t)], dst_ref=dst.at[part(s * 16 + t)], send_sem=send, recv_sem=recv,
            device_id=(to_s, to_t), device_id_type=MESH,
        ).start()


ORDERS = ("zxy", "xyz", "yzx", "zxy", "zyx")
EARLY = (0, 4)
LATE = (1, 2, 3)


def step_kernel(
    factor,
    len_ref, owner_ref, row_ref, table_hbm, og_hbm, gin_ref, gout_ref, w_in_hbm, w_out_hbm,
    hidden_ref, incoming_ref, sums_ref, asked_ref,
    table_ref, og_ref, w_in_ref, w_out_ref, x_ref, egrad, terms, normed, normed_t, slope, gate, upstream, joined, jgrad, nback, pback,
    q_out, kv_out, q_in, kv_in, mix_out, mix_in, dm_out, dm_in,
    dq_acc, dkv_acc, part_out, part_in, dq_out, dkv_out, dq_in, dkv_in, m_acc,
    req_out, req_in, asked_col, found, fetched, spot_col, pick_one, pick_two, put_one, put_two,
    r0, a1, r1, a2, r2, a3, r3,
    q_send, q_recv, kv_send, kv_recv, fwd_send, mix_send, mix_recv, dm_send, dm_recv,
    part_send, part_recv, dq_send, dq_recv, dkv_send, dkv_recv,
    load_sem, req_send, req_recv, row_send, row_recv, back_send, back_recv,
    s0, v0, s1, v1, s2, v2, s3, v3, s4, v4, s5, v5, s6, v6, s7, v7,
):
    s = lax.axis_index("seq")
    t = lax.axis_index("table")
    me = s * 16 + t
    core = lax.rem(t, 2)
    base = t - core
    head = lax.rem(s, HEADS)
    user_core = lax.rem(lax.rem(s, HEADS) + s // HEADS, 2)
    upward = user_core == 1
    sibling = base + 1 - core
    part_of_s = lax.rem((s + 1) // 2, 2)
    slot_of_s = s // 2
    cx, cz = lax.rem(s, 4), t // 4
    cy = lax.rem(t // 2, 2) * 2 + s // 4
    barrier = greet_all(s, t)

    def push(src, dst, send, recv, to_s, to_t):
        mine = jnp.logical_and(to_s == s, to_t == t)

        @pl.when(mine)
        def _():
            pltpu.make_async_copy(src, dst, recv).start()

        @pl.when(jnp.logical_not(mine))
        def _():
            pltpu.make_async_remote_copy(
                src_ref=src, dst_ref=dst, send_sem=send, recv_sem=recv,
                device_id=(to_s, to_t), device_id_type=MESH,
            ).start()

    def left(src, send, to_s, to_t):
        @pl.when(jnp.logical_not(jnp.logical_and(to_s == s, to_t == t)))
        def _():
            landed(src, send)

    def worker(h):
        return lax.rem(core + h, 2) * HEADS + h, base + part_of_s

    def mine_of(k):
        return 2 * k + lax.rem(k + core, 2)

    def other_of(k):
        return 2 * k + lax.rem(k + core + 1, 2)

    length = len_ref[0]

    def live_rows(start, count):
        pos = s * TOK + start + lax.broadcasted_iota(jnp.int32, (count, 1), 0)
        return (pos < length).astype(F32)

    place = {"x": cx, "y": cy, "z": cz}

    def partner(axis, d):
        other = lax.rem(place[axis] + d, 4)
        if axis == "x":
            return other, s - cx + other, t
        if axis == "y":
            return other, lax.rem(other, 2) * 4 + cx, cz * 4 + (other // 2) * 2 + core
        return other, s, other * 4 + lax.rem(t, 4)

    def ship(src, dst, send, recv, to_s, to_t):
        pltpu.make_async_remote_copy(
            src_ref=src, dst_ref=dst, send_sem=send, recv_sem=recv,
            device_id=(to_s, to_t), device_id_type=MESH,
        ).start()

    half = pl.ds(pl.multiple_of(core * 256, 256), 256)
    other_half = pl.ds(pl.multiple_of(256 - core * 256, 256), 256)

    def block_of(index, size):
        return pl.ds(pl.multiple_of(index * size, size), size)

    def block(axis, size):
        return block_of(place[axis], size)

    def spot(u, first, second, third):
        return sums_ref.at[u, block_of(core * 16 + first * 4 + second, 16), block_of(third, 128)]

    def lines(u, first, second):
        return sums_ref.at[u, block_of(core * 16 + first * 4 + second, 16)]

    def quarter(u, first):
        return sums_ref.at[u, block_of(core * 4 + first, 64)]

    def before_me(axis, d):
        return lax.rem(place[axis] + 4 - d, 4)

    def step(u, n):
        one, two, three = ORDERS[u]
        if n == 0:
            ship(terms.at[u, other_half], r0.at[u], s0.at[u], v0.at[u], s, sibling)
        elif n == 1:
            landed(r0.at[u], v0.at[u])
            a1[u] = (terms[u, half, :].astype(F32) + r0[u].astype(F32)).astype(BF)
            for d in range(1, 4):
                other, to_s, to_t = partner(one, d)
                ship(a1.at[u, block_of(other, 64)], r1.at[u, d - 1], s1.at[u, d - 1], v1.at[u, d - 1], to_s, to_t)
        elif n == 2:
            total = a1[u, block(one, 64), :].astype(F32)
            for d in range(1, 4):
                landed(r1.at[u, d - 1], v1.at[u, d - 1])
                total += r1[u, d - 1].astype(F32)
            a2[u] = total.astype(BF)
            for d in range(1, 4):
                other, to_s, to_t = partner(two, d)
                ship(a2.at[u, block_of(other, 16)], r2.at[u, d - 1], s2.at[u, d - 1], v2.at[u, d - 1], to_s, to_t)
        elif n == 3:
            total = a2[u, block(two, 16), :].astype(F32)
            for d in range(1, 4):
                landed(r2.at[u, d - 1], v2.at[u, d - 1])
                total += r2[u, d - 1].astype(F32)
            a3[u] = total.astype(BF)
            for d in range(1, 4):
                other, to_s, to_t = partner(three, d)
                ship(
                    a3.at[u, :, block_of(other, 128)], r3.at[u, d - 1], s3.at[u, d - 1], v3.at[u, d - 1], to_s, to_t
                )
        elif n == 4:
            total = a3[u, :, block(three, 128)].astype(F32)
            for d in range(1, 4):
                landed(r3.at[u, d - 1], v3.at[u, d - 1])
                total += r3[u, d - 1].astype(F32)
            mine = spot(u, place[one], place[two], place[three])
            mine[...] = total.astype(BF)
            for d in range(1, 4):
                _, to_s, to_t = partner(three, d)
                ship(mine, mine, s4.at[u, d - 1], v4.at[u, d - 1], to_s, to_t)
        elif n == 5:
            for d in range(1, 4):
                landed(spot(u, place[one], place[two], before_me(three, d)), v4.at[u, d - 1])
            mine = lines(u, place[one], place[two])
            for d in range(1, 4):
                _, to_s, to_t = partner(two, d)
                ship(mine, mine, s5.at[u, d - 1], v5.at[u, d - 1], to_s, to_t)
        elif n == 6:
            for d in range(1, 4):
                landed(lines(u, place[one], before_me(two, d)), v5.at[u, d - 1])
            mine = quarter(u, place[one])
            for d in range(1, 4):
                _, to_s, to_t = partner(one, d)
                ship(mine, mine, s6.at[u, d - 1], v6.at[u, d - 1], to_s, to_t)
        elif n == 7:
            for d in range(1, 4):
                landed(quarter(u, before_me(one, d)), v6.at[u, d - 1])
            ship(sums_ref.at[u, half], sums_ref.at[u, half], s7.at[u], v7.at[u], s, sibling)
        else:
            landed(sums_ref.at[u, other_half], v7.at[u])

    copies = [
        pltpu.make_async_copy(src, dst, load_sem.at[n])
        for n, (src, dst) in enumerate(
            ((table_hbm, table_ref), (og_hbm, og_ref), (w_out_hbm, w_out_ref), (w_in_hbm, w_in_ref))
        )
    ]
    for copy in copies:
        copy.start()

    target = owner_ref[...]
    line_e = lax.broadcasted_iota(jnp.int32, (OWNERS, TOK), 0)
    chosen_mask = line_e == target
    chosen = jnp.where(chosen_mask, 1.0, 0.0).astype(BF)
    above = jnp.where(
        lax.broadcasted_iota(jnp.int32, (TOK, TOK), 0) < lax.broadcasted_iota(jnp.int32, (TOK, TOK), 1), 1.0, 0.0
    ).astype(BF)
    before = dot(chosen, above)
    rank = jnp.sum(jnp.where(chosen_mask, before, 0.0), axis=0, keepdims=True).astype(jnp.int32)
    value = row_ref[...] + 1
    high = (value >> 7).astype(F32)
    low = (value & 127).astype(F32)
    message = jnp.where(line_e == rank, high, 0.0) + jnp.where(line_e == rank + SLOTS, low, 0.0)
    req_out[:, 0, :] = dot(chosen, message.astype(BF), 1, 1)
    pl.semaphore_wait(barrier, OWNERS - 1)

    def ask(p, carry):
        spread(req_out, req_in, req_send, req_recv, s, t, lax.rem(s + p, 8), lambda index: index)
        return carry

    lax.fori_loop(0, 8, ask, 0)

    slot_row = target * 16 + rank
    spot_col[...] = jnp.broadcast_to(slot_row.astype(F32), (128, TOK)).T.astype(jnp.int32)
    live = live_rows(0, TOK)
    copies[1].wait()
    copies[2].wait()
    upstream[...] = (og_ref[...].astype(F32) * live).astype(BF)
    jgrad[...] = dot(upstream[...], w_out_ref[...], 1, 1)
    number = lax.broadcasted_iota(jnp.int32, (OWNERS * SLOTS, OWNERS), 0)
    lane_s = lax.broadcasted_iota(jnp.int32, (OWNERS * SLOTS, OWNERS), 1)
    expand = jnp.where((number >> 3) == lane_s, 1.0, 0.0).astype(BF)
    landed(req_in, req_recv)
    values = dot(expand, req_in[:, 0, :].astype(BF))
    own = number & 7
    asked = (
        jnp.sum(
            jnp.where(lane_s == own, values * 128.0, 0.0) + jnp.where(lane_s == own + SLOTS, values, 0.0),
            axis=1,
            keepdims=True,
        )
        - 1.0
    )
    wide = jnp.broadcast_to(asked, (OWNERS * SLOTS, 128))
    asked_col[...] = wide
    asked_ref[...] = wide.T[:8]

    copies[0].wait()

    def gather(p, carry):
        q = lax.rem(s + p, 8)
        column = asked_col[pl.ds(pl.multiple_of(q * 128, 128), 128), :][:, :1].astype(jnp.int32)
        hit = lax.broadcasted_iota(jnp.int32, (128, ROWS), 1) == column
        rows = dot(jnp.where(hit, 1.0, 0.0).astype(BF), table_ref[...])
        both = jnp.concatenate(
            [rows[:, :256].reshape(16, SLOTS, 256), rows[:, 256:].reshape(16, SLOTS, 256)], axis=1
        )
        found[pl.ds(pl.multiple_of(q * 256, 256), 256), :] = both.reshape(256, 256).astype(BF)
        spread(found, fetched, row_send, row_recv, s, t, q, sixteen)
        return carry

    lax.fori_loop(0, 8, gather, 0)
    def pick_tile(r, carry):
        rows = pl.ds(pl.multiple_of(r * TILE, TILE), TILE)
        at = lax.broadcasted_iota(jnp.int32, (TILE, ROWS), 1)
        spots = spot_col[rows, :][:, :1]
        pick_one[rows, :] = jnp.where(at == spots, 1.0, 0.0).astype(BF)
        pick_two[rows, :] = jnp.where(at == spots + SLOTS, 1.0, 0.0).astype(BF)
        return carry

    lax.fori_loop(0, TOK // TILE, pick_tile, 0)
    dq_acc[...] = jnp.zeros_like(dq_acc)
    dkv_acc[...] = jnp.zeros_like(dkv_acc)
    copies[3].wait()
    landed(fetched, row_recv)

    def norm_tile(r, carry):
        rows = pl.ds(pl.multiple_of(r * TILE, TILE), TILE)
        x_ref[rows, :256] = dot(pick_one[rows, :], fetched[...]).astype(BF)
        x_ref[rows, 256:] = dot(pick_two[rows, :], fetched[...]).astype(BF)
        x = x_ref[rows, :].astype(F32)
        mean = jnp.mean(x, -1, keepdims=True)
        cent = x - mean
        var = jnp.mean(cent * cent, -1, keepdims=True)
        normed[rows, :] = (cent * lax.rsqrt(var + EPS) * gin_ref[...]).astype(BF)
        return carry

    lax.fori_loop(0, TOK // TILE, norm_tile, 0)

    def project(first, columns):
        pre = dot(normed[...], w_in_ref[:, pl.ds(first, columns)])
        half = 0.5 * pre
        th = jnp.tanh(half)
        slope[:, pl.ds(first, columns)] = 0.5 * (1.0 + th) * (1.0 + half - half * th)
        return half + half * th

    far_first = [lax.rem(cx + d, HEADS) for d in (2, 1, 3, 0)]
    for h in far_first:
        column = pl.multiple_of(h * HEAD, HEAD)
        kv_out[h, :, :HEAD] = project(3 * WIDTH + column, HEAD).astype(BF)
        kv_out[h, :, HEAD:] = (project(WIDTH + column, HEAD) * live).astype(BF)
        to = worker(h)
        push(kv_out.at[h], kv_in.at[s], kv_send.at[h], kv_recv.at[s], *to)
        q_out[h] = project(2 * WIDTH + column, HEAD).astype(BF)
        push(q_out.at[h], q_in.at[slot_of_s], q_send.at[h], q_recv.at[slot_of_s], *to)

    gate[:, :256] = project(0, 256).astype(BF)
    gate[:, 256:] = project(256, 256).astype(BF)
    normed_t[...] = normed[...].T

    def scatter_tile(q, carry):
        rows = pl.ds(pl.multiple_of(q * 256, 256), 256)
        at = lax.broadcasted_iota(jnp.int32, (256, TOK), 0) + q * 256
        put_one[rows, :] = jnp.where(at == slot_row, 1.0, 0.0).astype(BF)
        put_two[rows, :] = jnp.where(at == slot_row + SLOTS, 1.0, 0.0).astype(BF)
        return carry

    lax.fori_loop(0, 8, scatter_tile, 0)

    def take(k):
        d = mine_of(k)
        landed(kv_in.at[d], kv_recv.at[d])
        pltpu.make_async_remote_copy(
            src_ref=kv_in.at[d], dst_ref=kv_in.at[d], send_sem=fwd_send.at[k], recv_sem=kv_recv.at[d],
            device_id=(s, sibling), device_id_type=MESH,
        ).start()

    row = lax.broadcasted_iota(jnp.int32, (TOK, TOK), 0)
    col = lax.broadcasted_iota(jnp.int32, (TOK, TOK), 1)

    def forward_pair(k, j, diagonal):
        half = dot(q_in[k], kv_in[j, :, :HEAD], 1, 1) * (0.5 * SCALE)
        w = half + half * jnp.tanh(half)
        if diagonal:
            w = jnp.where(col <= row, w, 0.0)
        return dot(w.astype(BF), kv_in[j, :, HEAD:])

    take(0)

    def forward(k, carry):
        i = mine_of(k)

        @pl.when(k < 3)
        def _():
            take(k + 1)

        landed(q_in.at[k], q_recv.at[k])
        o = other_of(k)
        landed(kv_in.at[o], kv_recv.at[o])
        m_acc[...] = forward_pair(k, i, True)

        def inner(j, c):
            m_acc[...] += forward_pair(k, j, False)
            return c

        lax.fori_loop(0, i, inner, 0)
        m = m_acc[...]
        shift = jnp.mean(m, -1, keepdims=True).astype(BF).astype(F32)
        mix_out[k, :TOK, :] = (m - shift).astype(BF)
        wide = jnp.broadcast_to(shift, (TOK, HEAD))
        lines = jnp.zeros((16, HEAD), F32)
        line = lax.broadcasted_iota(jnp.int32, (16, HEAD), 0)
        for b in range(TOK // HEAD):
            lines += jnp.where(line == b, wide[b * HEAD : (b + 1) * HEAD].T[:16], 0.0)
        mix_out[k, TOK:, :] = lines.astype(BF)
        push(mix_out.at[k], mix_in.at[head], mix_send.at[k], mix_recv.at[head], i, base + user_core)
        return carry

    lax.fori_loop(0, 4, forward, 0)

    for h in range(HEADS):
        landed(mix_in.at[h], mix_recv.at[h])

    def post_tile(r, carry):
        start = pl.multiple_of(r * TILE, TILE)
        rows = pl.ds(start, TILE)
        alive = live_rows(start, TILE)
        pick = (lax.broadcasted_iota(jnp.int32, (16, HEAD), 0) == r).astype(F32).astype(BF)
        m = jnp.concatenate(
            [mix_in[h, rows, :].astype(F32) + dot(mix_in[h, TOK:, :], pick, 0, 0) for h in range(HEADS)], axis=1
        ) * alive
        mean = jnp.mean(m, -1, keepdims=True)
        cent = m - mean
        var = jnp.mean(cent * cent, -1, keepdims=True)
        rstd = lax.rsqrt(var + EPS)
        n = cent * rstd
        ng = n * gout_ref[...]
        g = gate[rows, :].astype(F32)
        jg = jgrad[rows, :]
        joined[rows, :] = (ng * g).astype(BF)
        pback[rows, :WIDTH] = (jg * ng * slope[rows, :WIDTH]).astype(BF)
        dn = jg * g * gout_ref[...]
        dm = rstd * (dn - jnp.mean(dn, -1, keepdims=True) - n * jnp.mean(dn * n, -1, keepdims=True))
        dm = (dm * alive).astype(BF)
        for h in range(HEADS):
            dm_out[h, rows, :] = dm[:, h * HEAD : (h + 1) * HEAD]
        return carry

    lax.fori_loop(0, TOK // TILE, post_tile, 0)
    for h in far_first:
        push(dm_out.at[h], dm_in.at[slot_of_s], dm_send.at[h], dm_recv.at[slot_of_s], *worker(h))

    terms[4] = (dot(joined[...], upstream[...], 0, 0) * factor).astype(BF)
    terms[0] = (dot(normed_t[...], pback[:, :WIDTH]) * factor).astype(BF)
    for u in EARLY:
        step(u, 0)
    hidden_ref[...] = ((dot(joined[...], w_out_ref[...]) + x_ref[...].astype(F32)) * live).astype(BF)
    nback[...] = dot(pback[:, :WIDTH], w_in_ref[:, :WIDTH], 1, 1)
    for u in EARLY:
        step(u, 1)

    for k in range(4):
        landed(dm_in.at[k], dm_recv.at[k])

    def backward_pair(k, j, diagonal):
        q, dm = q_in[k], dm_in[k]
        half = dot(kv_in[j, :, :HEAD], q, 1, 1) * (0.5 * SCALE)
        th = jnp.tanh(half)
        ht = half * th
        w = half + ht
        sb = dot(kv_in[j, :, HEAD:], dm, 1, 1) * ((0.5 + 0.5 * th) * (1.0 + half - ht))
        if diagonal:
            w = jnp.where(row <= col, w, 0.0)
            sb = jnp.where(row <= col, sb, 0.0)
        sb = sb.astype(BF)
        dkv_acc[j, :, HEAD:] += dot(w.astype(BF), dm)
        dkv_acc[j, :, :HEAD] += dot(sb, q)
        dq_acc[k] += dot(sb, kv_in[j, :, :HEAD], 0, 0)

    def send_back(out, into, send, recv, k):
        push(out.at[k], into.at[head], send.at[k], recv.at[head], mine_of(k), base + user_core)

    def finish_query(k):
        dq_out[k] = (dq_acc[k] * SCALE).astype(BF)
        send_back(dq_out, dq_in, dq_send, dq_recv, k)

    def finish_key(j):
        m = j // 2

        @pl.when(mine_of(m) == j)
        def _():
            landed(part_in.at[m], part_recv.at[m])
            total = dkv_acc[j] + part_in[m].astype(F32)
            dkv_out[m, :, :HEAD] = (total[:, :HEAD] * SCALE).astype(BF)
            dkv_out[m, :, HEAD:] = total[:, HEAD:].astype(BF)
            send_back(dkv_out, dkv_in, dkv_send, dkv_recv, m)

    def key_block(n):
        return jnp.where(upward, n, 7 - n)

    def backward(n, carry):
        j = key_block(n)
        m = j // 2
        i = mine_of(m)

        @pl.when(i == j)
        def _():
            backward_pair(m, j, True)

        def inner(k, c):
            backward_pair(k, j, False)
            return c

        lax.fori_loop(jnp.where(i > j, m, m + 1), 4, inner, 0)

        @pl.when(i != j)
        def _():
            part_out[m] = dkv_acc[j].astype(BF)
            pltpu.make_async_remote_copy(
                src_ref=part_out.at[m], dst_ref=part_in.at[m], send_sem=part_send.at[m], recv_sem=part_recv.at[m],
                device_id=(s, sibling), device_id_type=MESH,
            ).start()

        @pl.when(jnp.logical_and(i == j, upward))
        def _():
            finish_query(m)

        @pl.when(n > 0)
        def _():
            finish_key(key_block(n - 1))

        return carry

    lax.fori_loop(0, 8, backward, 0)

    @pl.when(jnp.logical_not(upward))
    def _():
        for k in range(4):
            finish_query(k)

    finish_key(key_block(7))
    for u in EARLY:
        step(u, 2)

    for h in range(HEADS):
        landed(dq_in.at[h], dq_recv.at[h])
        landed(dkv_in.at[h], dkv_recv.at[h])

    def gate_tile(r, carry):
        start = pl.multiple_of(r * TILE, TILE)
        rows = pl.ds(start, TILE)
        alive = live_rows(start, TILE)
        for h in range(HEADS):
            for first, piece in (
                (WIDTH, dkv_in[h, rows, HEAD:].astype(F32) * alive),
                (2 * WIDTH, dq_in[h, rows, :].astype(F32)),
                (3 * WIDTH, dkv_in[h, rows, :HEAD].astype(F32)),
            ):
                c = first + h * HEAD
                pback[rows, c : c + HEAD] = (piece * slope[rows, c : c + HEAD]).astype(BF)
        return carry

    lax.fori_loop(0, TOK // TILE, gate_tile, 0)
    for u in LATE:
        terms[u] = (dot(normed_t[...], pback[:, u * WIDTH : (u + 1) * WIDTH]) * factor).astype(BF)
        step(u, 0)
    for u in EARLY:
        step(u, 3)

    def back_tile(r, carry):
        rows = pl.ds(pl.multiple_of(r * TILE, TILE), TILE)
        nb = nback[rows, :] + dot(pback[rows, WIDTH:], w_in_ref[:, WIDTH:], 1, 1)
        x = x_ref[rows, :].astype(F32)
        mean = jnp.mean(x, -1, keepdims=True)
        cent = x - mean
        var = jnp.mean(cent * cent, -1, keepdims=True)
        rstd = lax.rsqrt(var + EPS)
        n = cent * rstd
        dn = nb * gin_ref[...]
        dx = rstd * (dn - jnp.mean(dn, -1, keepdims=True) - n * jnp.mean(dn * n, -1, keepdims=True))
        egrad[rows, :] = (dx + upstream[rows, :].astype(F32)).astype(BF)
        return carry

    lax.fori_loop(0, 2, back_tile, 0)
    for u in LATE:
        step(u, 1)
    for u in EARLY:
        step(u, 4)
    lax.fori_loop(2, 4, back_tile, 0)
    for u in LATE:
        step(u, 2)
    for u in EARLY:
        step(u, 5)

    landed(found.at[pl.ds(0, (OWNERS - 1) * 16)], row_send)

    def scatter(p, carry):
        q = lax.rem(s + p, 8)
        rows = pl.ds(pl.multiple_of(q * 256, 256), 256)
        found[rows, :] = (dot(put_one[rows, :], egrad[:, :256]) + dot(put_two[rows, :], egrad[:, 256:])).astype(BF)
        spread(found, incoming_ref, back_send, back_recv, s, t, q, sixteen)
        return carry

    for n in range(4):
        lax.fori_loop(2 * n, 2 * n + 2, scatter, 0)
        for u in LATE:
            step(u, n + 3)
        if n < 3:
            for u in EARLY:
                step(u, n + 6)
    for n in range(7, 9):
        for u in LATE:
            step(u, n)
    landed(incoming_ref, back_recv)
    landed(found.at[pl.ds(0, (OWNERS - 1) * 16)], back_send)
    landed(req_out.at[pl.ds(0, OWNERS - 1)], req_send)

    for h in range(HEADS):
        to = worker(h)
        left(kv_out.at[h], kv_send.at[h], *to)
        left(q_out.at[h], q_send.at[h], *to)
        left(dm_out.at[h], dm_send.at[h], *to)
        landed(kv_in.at[mine_of(h)], fwd_send.at[h])
        landed(part_out.at[h], part_send.at[h])
        back = (mine_of(h), base + user_core)
        left(mix_out.at[h], mix_send.at[h], *back)
        left(dq_out.at[h], dq_send.at[h], *back)
        left(dkv_out.at[h], dkv_send.at[h], *back)


    for u in range(len(ORDERS)):
        one, two, three = ORDERS[u]
        landed(terms.at[u, other_half], s0.at[u])
        landed(sums_ref.at[u, half], s7.at[u])
        for d in range(3):
            landed(r1.at[u, d], s1.at[u, d])
            landed(r2.at[u, d], s2.at[u, d])
            landed(r3.at[u, d], s3.at[u, d])
            landed(spot(u, place[one], place[two], place[three]), s4.at[u, d])
            landed(lines(u, place[one], place[two]), s5.at[u, d])
            landed(quarter(u, place[one]), s6.at[u, d])


def layer_step(length, owner, item_row, item_table, out_grad, gain_in, gain_out, w_in, w_out, factor):
    vm, far = pl.BlockSpec(memory_space=pltpu.VMEM), pl.BlockSpec(memory_space=pl.ANY)
    dma = pltpu.SemaphoreType.DMA
    n = len(ORDERS)

    def buf(*shape, dtype=BF):
        return pltpu.VMEM(shape, dtype)

    square = buf(TOK, WIDTH)
    wide = buf(TOK, WIDTH, dtype=F32)
    heads, pairs, carried = buf(4, TOK, HEAD), buf(4, TOK, 2 * HEAD), buf(4, TOK + 16, HEAD)
    message = buf(OWNERS, 1, 128, dtype=F32)
    blocks = [
        buf(ROWS, WIDTH), square, buf(WIDTH, 4 * WIDTH), square,
        square, square, buf(n, WIDTH, WIDTH), square, square, buf(TOK, 4 * WIDTH, dtype=F32), square, square,
        square, wide, wide, buf(TOK, 4 * WIDTH),
        heads, pairs, heads, buf(8, TOK, 2 * HEAD), carried, carried, heads, heads,
        buf(4, TOK, HEAD, dtype=F32), buf(8, TOK, 2 * HEAD, dtype=F32),
        pairs, pairs, heads, pairs, heads, pairs, buf(TOK, HEAD, dtype=F32),
        message, message, buf(OWNERS * SLOTS, 128, dtype=F32), buf(ROWS, 256), buf(ROWS, 256),
        buf(TOK, 128, dtype=jnp.int32), buf(TOK, ROWS), buf(TOK, ROWS), buf(ROWS, TOK), buf(ROWS, TOK),
        buf(n, 256, WIDTH), buf(n, 256, WIDTH), buf(n, 3, 64, WIDTH), buf(n, 64, WIDTH),
        buf(n, 3, 16, WIDTH), buf(n, 16, WIDTH), buf(n, 3, 16, 128),
    ]
    one, three = dma((n,)), dma((n, 3))
    sems = [dma((c,)) for c in (4, 4, 4, 8, 4, 4, 4, 4, 4, 4, 4, 4, 4, 4, 4)]
    sems += [dma((4,))] + [dma] * 6 + [one] * 2 + [three] * 12 + [one] * 2
    return pl.pallas_call(
        functools.partial(step_kernel, factor),
        out_shape=(
            jax.ShapeDtypeStruct((TOK, WIDTH), BF),
            jax.ShapeDtypeStruct((ROWS, 256), BF),
            jax.ShapeDtypeStruct((n, WIDTH, WIDTH), BF),
            jax.ShapeDtypeStruct((8, OWNERS * SLOTS), F32),
        ),
        in_specs=[pl.BlockSpec(memory_space=pltpu.SMEM), vm, vm, far, far, vm, vm, far, far],
        out_specs=(vm,) * 4,
        scratch_shapes=blocks + sems,
        compiler_params=pltpu.CompilerParams(
            collective_id=0, has_side_effects=True, vmem_limit_bytes=62 * 1024 * 1024
        ),
    )(length, owner, item_row, item_table, out_grad, gain_in.reshape(1, -1), gain_out.reshape(1, -1), w_in, w_out)


def finish_kernel(incoming_ref, asked_ref, sums_ref, out_ref, w_in_ref, w_out_ref, rows):
    @pl.when(pl.program_id(0) == 0)
    def _():
        for q in range(8):
            both = incoming_ref[q * 256 : (q + 1) * 256, :].astype(F32).reshape(16, 16, 256)
            part = slice(q * 128, (q + 1) * 128)
            rows[part, :256] = both[:, :SLOTS].reshape(128, 256).astype(BF)
            rows[part, 256:] = both[:, SLOTS:].reshape(128, 256).astype(BF)

    at = lax.broadcasted_iota(jnp.int32, (256, OWNERS * SLOTS), 0) + pl.program_id(0) * 256
    hit = at == asked_ref[...][:1].astype(jnp.int32)
    out_ref[...] = dot(jnp.where(hit, 1.0, 0.0).astype(BF), rows[...])
    for u in range(4):
        w_in_ref[:, u * WIDTH : (u + 1) * WIDTH] = sums_ref[u].astype(F32)
    w_out_ref[...] = sums_ref[4].astype(F32)


def finish(incoming, asked, sums):
    n = len(ORDERS)
    return pl.pallas_call(
        finish_kernel,
        grid=(8,),
        out_shape=(
            jax.ShapeDtypeStruct((ROWS, WIDTH), F32),
            jax.ShapeDtypeStruct((WIDTH, 4 * WIDTH), F32),
            jax.ShapeDtypeStruct((WIDTH, WIDTH), F32),
        ),
        in_specs=[
            pl.BlockSpec((ROWS, 256), lambda i: (0, 0)),
            pl.BlockSpec((8, OWNERS * SLOTS), lambda i: (0, 0)),
            pl.BlockSpec((n, 64, WIDTH), lambda i: (0, i, 0)),
        ],
        out_specs=(
            pl.BlockSpec((256, WIDTH), lambda i: (i, 0)),
            pl.BlockSpec((64, 4 * WIDTH), lambda i: (i, 0)),
            pl.BlockSpec((64, WIDTH), lambda i: (i, 0)),
        ),
        scratch_shapes=[pltpu.VMEM((OWNERS * SLOTS, WIDTH), BF)],
        compiler_params=pltpu.CompilerParams(vmem_limit_bytes=60 * 1024 * 1024),
    )(incoming, asked, sums)


def local(item_table, owner, item_row, lengths, gain_in, gain_out, w_in, w_out, out_grad):
    factor = (TOK * OWNERS) ** (-0.5)
    hidden, incoming, sums, asked = layer_step(
        lengths, owner.reshape(1, TOK), item_row, item_table, out_grad[0], gain_in, gain_out, w_in, w_out, factor
    )
    table_grad, w_in_grad, w_out_grad = finish(incoming, asked, sums)
    return (hidden[None], table_grad, w_in_grad, w_out_grad)


def solution(mesh):
    placed = (
        P(("seq", "table"), None),
        P("table", "seq", None),
        P("table", "seq"),
        P("table"),
        P(),
        P(),
        P(),
        P(),
        P("table", "seq", None),
    )
    return jax.shard_map(
        local,
        mesh=mesh,
        in_specs=placed,
        out_specs=(P("table", "seq", None), P(("seq", "table"), None), P(), P()),
        check_vma=False,
    )
```

```python
import functools

import jax
import jax.numpy as jnp
from jax import lax
from jax.experimental import pallas as pl
from jax.experimental.pallas import tpu as pltpu
from jax.sharding import PartitionSpec as P

HEADS = 4
HEAD = 128
TOK = 512
WIDTH = 512
TILE = 128
SCALE = HEAD ** (-0.5)
EPS = 1e-05
MESH = pl.DeviceIdType.MESH
BF = jnp.bfloat16
F32 = jnp.float32


def dot(a, b, ca=1, cb=0):
    return lax.dot_general(a, b, (((ca,), (cb,)), ((), ())), preferred_element_type=F32)


def landed(ref, sem):
    pltpu.make_async_copy(ref, ref, sem).wait()


OWNERS = 128
SLOTS = 8
ROWS = 2048


def greet_all(s, t):
    barrier = pltpu.get_barrier_semaphore()
    me = s * 16 + t

    def greet(d, carry):
        other = lax.rem(me + d, OWNERS)
        pl.semaphore_signal(
            barrier, inc=1, device_id=(other // 16, lax.rem(other, 16)), device_id_type=MESH
        )
        return carry

    lax.fori_loop(1, OWNERS, greet, 0)
    return barrier


def send_rows(src, dst, send, recv, s, t, to_s, to_t, take, place):
    mine = jnp.logical_and(to_s == s, to_t == t)

    @pl.when(mine)
    def _():
        pltpu.make_async_copy(src.at[take], dst.at[place], recv).start()

    @pl.when(jnp.logical_not(mine))
    def _():
        pltpu.make_async_remote_copy(
            src_ref=src.at[take], dst_ref=dst.at[place], send_sem=send, recv_sem=recv,
            device_id=(to_s, to_t), device_id_type=MESH,
        ).start()


def sixteen(index):
    return pl.ds(pl.multiple_of(index * 16, 16), 16)


def spread(src, dst, send, recv, s, t, to_s, part):
    send_rows(src, dst, send, recv, s, t, to_s, t, part(to_s * 16 + t), part(s * 16 + t))
    for p in range(1, 16):
        to_t = lax.rem(t + p, 16)
        pltpu.make_async_remote_copy(
            src_ref=src.at[part(to_s * 16 + to_t)], dst_ref=dst.at[part(s * 16 + t)], send_sem=send, recv_sem=recv,
            device_id=(to_s, to_t), device_id_type=MESH,
        ).start()


ORDERS = ("zxy", "xyz", "yzx", "zxy", "zyx")
EARLY = (0, 4)
LATE = (1, 2, 3)


def step_kernel(
    factor,
    len_ref, owner_ref, row_ref, table_hbm, og_hbm, gin_ref, gout_ref, w_in_hbm, w_out_hbm,
    hidden_ref, rows_ref, sums_ref, asked_ref,
    table_ref, og_ref, w_in_ref, w_out_ref, incoming, x_ref, egrad, terms, normed, normed_t, slope, gate, upstream, joined, jgrad, nback, pback,
    q_out, kv_out, q_in, kv_in, mix_out, mix_in, dm_out, dm_in,
    dq_acc, dkv_acc, part_out, part_in, dq_out, dkv_out, dq_in, dkv_in, m_acc,
    req_out, req_in, asked_col, found, fetched, spot_col, pick_one, pick_two, put_one, put_two,
    r0, a1, r1, a2, r2, a3, r3,
    q_send, q_recv, kv_send, kv_recv, fwd_send, mix_send, mix_recv, dm_send, dm_recv,
    part_send, part_recv, dq_send, dq_recv, dkv_send, dkv_recv,
    load_sem, req_send, req_recv, row_send, row_recv, back_send, back_recv,
    s0, v0, s1, v1, s2, v2, s3, v3, s4, v4, s5, v5, s6, v6, s7, v7,
):
    s = lax.axis_index("seq")
    t = lax.axis_index("table")
    me = s * 16 + t
    core = lax.rem(t, 2)
    base = t - core
    head = lax.rem(s, HEADS)
    user_core = lax.rem(lax.rem(s, HEADS) + s // HEADS, 2)
    upward = user_core == 1
    sibling = base + 1 - core
    part_of_s = lax.rem((s + 1) // 2, 2)
    slot_of_s = s // 2
    cx, cz = lax.rem(s, 4), t // 4
    cy = lax.rem(t // 2, 2) * 2 + s // 4
    barrier = greet_all(s, t)

    def push(src, dst, send, recv, to_s, to_t):
        mine = jnp.logical_and(to_s == s, to_t == t)

        @pl.when(mine)
        def _():
            pltpu.make_async_copy(src, dst, recv).start()

        @pl.when(jnp.logical_not(mine))
        def _():
            pltpu.make_async_remote_copy(
                src_ref=src, dst_ref=dst, send_sem=send, recv_sem=recv,
                device_id=(to_s, to_t), device_id_type=MESH,
            ).start()

    def left(src, send, to_s, to_t):
        @pl.when(jnp.logical_not(jnp.logical_and(to_s == s, to_t == t)))
        def _():
            landed(src, send)

    def worker(h):
        return lax.rem(core + h, 2) * HEADS + h, base + part_of_s

    def mine_of(k):
        return 2 * k + lax.rem(k + core, 2)

    def other_of(k):
        return 2 * k + lax.rem(k + core + 1, 2)

    length = len_ref[0]

    def live_rows(start, count):
        pos = s * TOK + start + lax.broadcasted_iota(jnp.int32, (count, 1), 0)
        return (pos < length).astype(F32)

    place = {"x": cx, "y": cy, "z": cz}

    def partner(axis, d):
        other = lax.rem(place[axis] + d, 4)
        if axis == "x":
            return other, s - cx + other, t
        if axis == "y":
            return other, lax.rem(other, 2) * 4 + cx, cz * 4 + (other // 2) * 2 + core
        return other, s, other * 4 + lax.rem(t, 4)

    def ship(src, dst, send, recv, to_s, to_t):
        pltpu.make_async_remote_copy(
            src_ref=src, dst_ref=dst, send_sem=send, recv_sem=recv,
            device_id=(to_s, to_t), device_id_type=MESH,
        ).start()

    half = pl.ds(pl.multiple_of(core * 256, 256), 256)
    other_half = pl.ds(pl.multiple_of(256 - core * 256, 256), 256)

    def block_of(index, size):
        return pl.ds(pl.multiple_of(index * size, size), size)

    def block(axis, size):
        return block_of(place[axis], size)

    def spot(u, first, second, third):
        return sums_ref.at[u, block_of(core * 16 + first * 4 + second, 16), block_of(third, 128)]

    def lines(u, first, second):
        return sums_ref.at[u, block_of(core * 16 + first * 4 + second, 16)]

    def quarter(u, first):
        return sums_ref.at[u, block_of(core * 4 + first, 64)]

    def before_me(axis, d):
        return lax.rem(place[axis] + 4 - d, 4)

    def step(u, n):
        one, two, three = ORDERS[u]
        if n == 0:
            ship(terms.at[u, other_half], r0.at[u], s0.at[u], v0.at[u], s, sibling)
        elif n == 1:
            landed(r0.at[u], v0.at[u])
            a1[u] = (terms[u, half, :].astype(F32) + r0[u].astype(F32)).astype(BF)
            for d in range(1, 4):
                other, to_s, to_t = partner(one, d)
                ship(a1.at[u, block_of(other, 64)], r1.at[u, d - 1], s1.at[u, d - 1], v1.at[u, d - 1], to_s, to_t)
        elif n == 2:
            total = a1[u, block(one, 64), :].astype(F32)
            for d in range(1, 4):
                landed(r1.at[u, d - 1], v1.at[u, d - 1])
                total += r1[u, d - 1].astype(F32)
            a2[u] = total.astype(BF)
            for d in range(1, 4):
                other, to_s, to_t = partner(two, d)
                ship(a2.at[u, block_of(other, 16)], r2.at[u, d - 1], s2.at[u, d - 1], v2.at[u, d - 1], to_s, to_t)
        elif n == 3:
            total = a2[u, block(two, 16), :].astype(F32)
            for d in range(1, 4):
                landed(r2.at[u, d - 1], v2.at[u, d - 1])
                total += r2[u, d - 1].astype(F32)
            a3[u] = total.astype(BF)
            for d in range(1, 4):
                other, to_s, to_t = partner(three, d)
                ship(
                    a3.at[u, :, block_of(other, 128)], r3.at[u, d - 1], s3.at[u, d - 1], v3.at[u, d - 1], to_s, to_t
                )
        elif n == 4:
            total = a3[u, :, block(three, 128)].astype(F32)
            for d in range(1, 4):
                landed(r3.at[u, d - 1], v3.at[u, d - 1])
                total += r3[u, d - 1].astype(F32)
            mine = spot(u, place[one], place[two], place[three])
            mine[...] = total.astype(BF)
            for d in range(1, 4):
                _, to_s, to_t = partner(three, d)
                ship(mine, mine, s4.at[u, d - 1], v4.at[u, d - 1], to_s, to_t)
        elif n == 5:
            for d in range(1, 4):
                landed(spot(u, place[one], place[two], before_me(three, d)), v4.at[u, d - 1])
            mine = lines(u, place[one], place[two])
            for d in range(1, 4):
                _, to_s, to_t = partner(two, d)
                ship(mine, mine, s5.at[u, d - 1], v5.at[u, d - 1], to_s, to_t)
        elif n == 6:
            for d in range(1, 4):
                landed(lines(u, place[one], before_me(two, d)), v5.at[u, d - 1])
            mine = quarter(u, place[one])
            for d in range(1, 4):
                _, to_s, to_t = partner(one, d)
                ship(mine, mine, s6.at[u, d - 1], v6.at[u, d - 1], to_s, to_t)
        elif n == 7:
            for d in range(1, 4):
                landed(quarter(u, before_me(one, d)), v6.at[u, d - 1])
            ship(sums_ref.at[u, half], sums_ref.at[u, half], s7.at[u], v7.at[u], s, sibling)
        else:
            landed(sums_ref.at[u, other_half], v7.at[u])

    copies = [
        pltpu.make_async_copy(src, dst, load_sem.at[n])
        for n, (src, dst) in enumerate(
            ((table_hbm, table_ref), (og_hbm, og_ref), (w_out_hbm, w_out_ref), (w_in_hbm, w_in_ref))
        )
    ]
    for copy in copies:
        copy.start()

    target = owner_ref[...]
    line_e = lax.broadcasted_iota(jnp.int32, (OWNERS, TOK), 0)
    chosen_mask = line_e == target
    chosen = jnp.where(chosen_mask, 1.0, 0.0).astype(BF)
    above = jnp.where(
        lax.broadcasted_iota(jnp.int32, (TOK, TOK), 0) < lax.broadcasted_iota(jnp.int32, (TOK, TOK), 1), 1.0, 0.0
    ).astype(BF)
    before = dot(chosen, above)
    rank = jnp.sum(jnp.where(chosen_mask, before, 0.0), axis=0, keepdims=True).astype(jnp.int32)
    value = row_ref[...] + 1
    high = (value >> 7).astype(F32)
    low = (value & 127).astype(F32)
    message = jnp.where(line_e == rank, high, 0.0) + jnp.where(line_e == rank + SLOTS, low, 0.0)
    req_out[:, 0, :] = dot(chosen, message.astype(BF), 1, 1)
    pl.semaphore_wait(barrier, OWNERS - 1)

    def ask(p, carry):
        spread(req_out, req_in, req_send, req_recv, s, t, lax.rem(s + p, 8), lambda index: index)
        return carry

    lax.fori_loop(0, 8, ask, 0)

    slot_row = target * 16 + rank
    spot_col[...] = jnp.broadcast_to(slot_row.astype(F32), (128, TOK)).T.astype(jnp.int32)
    live = live_rows(0, TOK)
    copies[1].wait()
    copies[2].wait()
    upstream[...] = (og_ref[...].astype(F32) * live).astype(BF)
    jgrad[...] = dot(upstream[...], w_out_ref[...], 1, 1)
    number = lax.broadcasted_iota(jnp.int32, (OWNERS * SLOTS, OWNERS), 0)
    lane_s = lax.broadcasted_iota(jnp.int32, (OWNERS * SLOTS, OWNERS), 1)
    expand = jnp.where((number >> 3) == lane_s, 1.0, 0.0).astype(BF)
    landed(req_in, req_recv)
    values = dot(expand, req_in[:, 0, :].astype(BF))
    own = number & 7
    asked = (
        jnp.sum(
            jnp.where(lane_s == own, values * 128.0, 0.0) + jnp.where(lane_s == own + SLOTS, values, 0.0),
            axis=1,
            keepdims=True,
        )
        - 1.0
    )
    wide = jnp.broadcast_to(asked, (OWNERS * SLOTS, 128))
    asked_col[...] = wide
    asked_ref[...] = wide.T[:8]

    copies[0].wait()

    def gather(p, carry):
        q = lax.rem(s + p, 8)
        column = asked_col[pl.ds(pl.multiple_of(q * 128, 128), 128), :][:, :1].astype(jnp.int32)
        hit = lax.broadcasted_iota(jnp.int32, (128, ROWS), 1) == column
        rows = dot(jnp.where(hit, 1.0, 0.0).astype(BF), table_ref[...])
        both = jnp.concatenate(
            [rows[:, :256].reshape(16, SLOTS, 256), rows[:, 256:].reshape(16, SLOTS, 256)], axis=1
        )
        found[pl.ds(pl.multiple_of(q * 256, 256), 256), :] = both.reshape(256, 256).astype(BF)
        spread(found, fetched, row_send, row_recv, s, t, q, sixteen)
        return carry

    lax.fori_loop(0, 8, gather, 0)
    def pick_tile(r, carry):
        rows = pl.ds(pl.multiple_of(r * TILE, TILE), TILE)
        at = lax.broadcasted_iota(jnp.int32, (TILE, ROWS), 1)
        spots = spot_col[rows, :][:, :1]
        pick_one[rows, :] = jnp.where(at == spots, 1.0, 0.0).astype(BF)
        pick_two[rows, :] = jnp.where(at == spots + SLOTS, 1.0, 0.0).astype(BF)
        return carry

    lax.fori_loop(0, TOK // TILE, pick_tile, 0)
    dq_acc[...] = jnp.zeros_like(dq_acc)
    dkv_acc[...] = jnp.zeros_like(dkv_acc)
    copies[3].wait()
    landed(fetched, row_recv)

    def norm_tile(r, carry):
        rows = pl.ds(pl.multiple_of(r * TILE, TILE), TILE)
        x_ref[rows, :256] = dot(pick_one[rows, :], fetched[...]).astype(BF)
        x_ref[rows, 256:] = dot(pick_two[rows, :], fetched[...]).astype(BF)
        x = x_ref[rows, :].astype(F32)
        mean = jnp.mean(x, -1, keepdims=True)
        cent = x - mean
        var = jnp.mean(cent * cent, -1, keepdims=True)
        normed[rows, :] = (cent * lax.rsqrt(var + EPS) * gin_ref[...]).astype(BF)
        return carry

    lax.fori_loop(0, TOK // TILE, norm_tile, 0)

    def project(first, columns):
        pre = dot(normed[...], w_in_ref[:, pl.ds(first, columns)])
        half = 0.5 * pre
        th = jnp.tanh(half)
        slope[:, pl.ds(first, columns)] = 0.5 * (1.0 + th) * (1.0 + half - half * th)
        return half + half * th

    far_first = [lax.rem(cx + d, HEADS) for d in (2, 1, 3, 0)]
    for h in far_first:
        column = pl.multiple_of(h * HEAD, HEAD)
        kv_out[h, :, :HEAD] = project(3 * WIDTH + column, HEAD).astype(BF)
        kv_out[h, :, HEAD:] = (project(WIDTH + column, HEAD) * live).astype(BF)
        to = worker(h)
        push(kv_out.at[h], kv_in.at[s], kv_send.at[h], kv_recv.at[s], *to)
        q_out[h] = project(2 * WIDTH + column, HEAD).astype(BF)
        push(q_out.at[h], q_in.at[slot_of_s], q_send.at[h], q_recv.at[slot_of_s], *to)

    gate[:, :256] = project(0, 256).astype(BF)
    gate[:, 256:] = project(256, 256).astype(BF)
    normed_t[...] = normed[...].T

    def scatter_tile(q, carry):
        rows = pl.ds(pl.multiple_of(q * 256, 256), 256)
        at = lax.broadcasted_iota(jnp.int32, (256, TOK), 0) + q * 256
        put_one[rows, :] = jnp.where(at == slot_row, 1.0, 0.0).astype(BF)
        put_two[rows, :] = jnp.where(at == slot_row + SLOTS, 1.0, 0.0).astype(BF)
        return carry

    lax.fori_loop(0, 8, scatter_tile, 0)

    def take(k):
        d = mine_of(k)
        landed(kv_in.at[d], kv_recv.at[d])
        pltpu.make_async_remote_copy(
            src_ref=kv_in.at[d], dst_ref=kv_in.at[d], send_sem=fwd_send.at[k], recv_sem=kv_recv.at[d],
            device_id=(s, sibling), device_id_type=MESH,
        ).start()

    row = lax.broadcasted_iota(jnp.int32, (TOK, TOK), 0)
    col = lax.broadcasted_iota(jnp.int32, (TOK, TOK), 1)

    def forward_pair(k, j, diagonal):
        half = dot(q_in[k], kv_in[j, :, :HEAD], 1, 1) * (0.5 * SCALE)
        w = half + half * jnp.tanh(half)
        if diagonal:
            w = jnp.where(col <= row, w, 0.0)
        return dot(w.astype(BF), kv_in[j, :, HEAD:])

    def take_one(k, carry):
        take(k)
        return carry

    lax.fori_loop(0, jnp.where(upward, 1, 4), take_one, 0)

    def arrive(k, carry):
        landed(q_in.at[k], q_recv.at[k])
        o = other_of(k)
        landed(kv_in.at[o], kv_recv.at[o])
        return carry

    def forward(n, carry):
        k = jnp.where(upward, n, 3 - n)
        i = mine_of(k)

        @pl.when(jnp.logical_and(n < 3, upward))
        def _():
            take(n + 1)

        first = jnp.where(upward, n, 0)
        lax.fori_loop(first, jnp.where(upward, n + 1, jnp.where(n == 0, 4, 0)), arrive, 0)
        m_acc[...] = forward_pair(k, i, True)

        def inner(j, c):
            m_acc[...] += forward_pair(k, j, False)
            return c

        lax.fori_loop(0, i, inner, 0)
        m = m_acc[...]
        shift = jnp.mean(m, -1, keepdims=True).astype(BF).astype(F32)
        mix_out[k, :TOK, :] = (m - shift).astype(BF)
        wide = jnp.broadcast_to(shift, (TOK, HEAD))
        lines = jnp.zeros((16, HEAD), F32)
        line = lax.broadcasted_iota(jnp.int32, (16, HEAD), 0)
        for b in range(TOK // HEAD):
            lines += jnp.where(line == b, wide[b * HEAD : (b + 1) * HEAD].T[:16], 0.0)
        mix_out[k, TOK:, :] = lines.astype(BF)
        push(mix_out.at[k], mix_in.at[head], mix_send.at[k], mix_recv.at[head], i, base + user_core)
        return carry

    lax.fori_loop(0, 4, forward, 0)

    for h in range(HEADS):
        landed(mix_in.at[h], mix_recv.at[h])

    def post_tile(r, carry):
        start = pl.multiple_of(r * TILE, TILE)
        rows = pl.ds(start, TILE)
        alive = live_rows(start, TILE)
        pick = (lax.broadcasted_iota(jnp.int32, (16, HEAD), 0) == r).astype(F32).astype(BF)
        m = jnp.concatenate(
            [mix_in[h, rows, :].astype(F32) + dot(mix_in[h, TOK:, :], pick, 0, 0) for h in range(HEADS)], axis=1
        ) * alive
        mean = jnp.mean(m, -1, keepdims=True)
        cent = m - mean
        var = jnp.mean(cent * cent, -1, keepdims=True)
        rstd = lax.rsqrt(var + EPS)
        n = cent * rstd
        ng = n * gout_ref[...]
        g = gate[rows, :].astype(F32)
        jg = jgrad[rows, :]
        joined[rows, :] = (ng * g).astype(BF)
        pback[rows, :WIDTH] = (jg * ng * slope[rows, :WIDTH]).astype(BF)
        dn = jg * g * gout_ref[...]
        dm = rstd * (dn - jnp.mean(dn, -1, keepdims=True) - n * jnp.mean(dn * n, -1, keepdims=True))
        dm = (dm * alive).astype(BF)
        for h in range(HEADS):
            dm_out[h, rows, :] = dm[:, h * HEAD : (h + 1) * HEAD]
        return carry

    for part in range(2):
        lax.fori_loop(2 * part, 2 * part + 2, post_tile, 0)
        rows = pl.ds(part * 256, 256)
        for h in far_first:
            push(
                dm_out.at[h, rows], dm_in.at[slot_of_s, rows], dm_send.at[h, part], dm_recv.at[slot_of_s, part],
                *worker(h),
            )

    terms[4] = (dot(joined[...], upstream[...], 0, 0) * factor).astype(BF)
    terms[0] = (dot(normed_t[...], pback[:, :WIDTH]) * factor).astype(BF)
    for u in EARLY:
        step(u, 0)
    hidden_ref[...] = ((dot(joined[...], w_out_ref[...]) + x_ref[...].astype(F32)) * live).astype(BF)
    nback[...] = dot(pback[:, :WIDTH], w_in_ref[:, :WIDTH], 1, 1)
    for u in EARLY:
        step(u, 1)

    for k in range(4):
        for part in range(2):
            landed(dm_in.at[k, pl.ds(part * 256, 256)], dm_recv.at[k, part])

    def backward_pair(k, j, diagonal):
        q, dm = q_in[k], dm_in[k]
        half = dot(kv_in[j, :, :HEAD], q, 1, 1) * (0.5 * SCALE)
        th = jnp.tanh(half)
        ht = half * th
        w = half + ht
        sb = dot(kv_in[j, :, HEAD:], dm, 1, 1) * ((0.5 + 0.5 * th) * (1.0 + half - ht))
        if diagonal:
            w = jnp.where(row <= col, w, 0.0)
            sb = jnp.where(row <= col, sb, 0.0)
        sb = sb.astype(BF)
        dkv_acc[j, :, HEAD:] += dot(w.astype(BF), dm)
        dkv_acc[j, :, :HEAD] += dot(sb, q)
        dq_acc[k] += dot(sb, kv_in[j, :, :HEAD], 0, 0)

    def send_back(out, into, send, recv, k):
        push(out.at[k], into.at[head], send.at[k], recv.at[head], mine_of(k), base + user_core)

    def finish_query(k):
        dq_out[k] = (dq_acc[k] * SCALE).astype(BF)
        send_back(dq_out, dq_in, dq_send, dq_recv, k)

    def finish_key(j):
        m = j // 2

        @pl.when(mine_of(m) == j)
        def _():
            landed(part_in.at[m], part_recv.at[m])
            total = dkv_acc[j] + part_in[m].astype(F32)
            dkv_out[m, :, :HEAD] = (total[:, :HEAD] * SCALE).astype(BF)
            dkv_out[m, :, HEAD:] = total[:, HEAD:].astype(BF)
            send_back(dkv_out, dkv_in, dkv_send, dkv_recv, m)

    def key_block(n):
        return jnp.where(upward, n, 7 - n)

    def backward(n, carry):
        j = key_block(n)
        m = j // 2
        i = mine_of(m)

        @pl.when(i == j)
        def _():
            backward_pair(m, j, True)

        def inner(k, c):
            backward_pair(k, j, False)
            return c

        lax.fori_loop(jnp.where(i > j, m, m + 1), 4, inner, 0)

        @pl.when(i != j)
        def _():
            part_out[m] = dkv_acc[j].astype(BF)
            pltpu.make_async_remote_copy(
                src_ref=part_out.at[m], dst_ref=part_in.at[m], send_sem=part_send.at[m], recv_sem=part_recv.at[m],
                device_id=(s, sibling), device_id_type=MESH,
            ).start()

        @pl.when(jnp.logical_and(i == j, upward))
        def _():
            finish_query(m)

        @pl.when(n > 0)
        def _():
            finish_key(key_block(n - 1))

        return carry

    lax.fori_loop(0, 8, backward, 0)

    @pl.when(jnp.logical_not(upward))
    def _():
        for k in range(4):
            finish_query(k)

    finish_key(key_block(7))
    for u in EARLY:
        step(u, 2)

    for h in range(HEADS):
        landed(dq_in.at[h], dq_recv.at[h])
        landed(dkv_in.at[h], dkv_recv.at[h])

    def gate_tile(r, carry):
        start = pl.multiple_of(r * TILE, TILE)
        rows = pl.ds(start, TILE)
        alive = live_rows(start, TILE)
        for h in range(HEADS):
            for first, piece in (
                (WIDTH, dkv_in[h, rows, HEAD:].astype(F32) * alive),
                (2 * WIDTH, dq_in[h, rows, :].astype(F32)),
                (3 * WIDTH, dkv_in[h, rows, :HEAD].astype(F32)),
            ):
                c = first + h * HEAD
                pback[rows, c : c + HEAD] = (piece * slope[rows, c : c + HEAD]).astype(BF)
        return carry

    lax.fori_loop(0, TOK // TILE, gate_tile, 0)
    for u in LATE:
        terms[u] = (dot(normed_t[...], pback[:, u * WIDTH : (u + 1) * WIDTH]) * factor).astype(BF)
        step(u, 0)
    for u in EARLY:
        step(u, 3)

    def back_tile(r, carry):
        rows = pl.ds(pl.multiple_of(r * TILE, TILE), TILE)
        nb = nback[rows, :] + dot(pback[rows, WIDTH:], w_in_ref[:, WIDTH:], 1, 1)
        x = x_ref[rows, :].astype(F32)
        mean = jnp.mean(x, -1, keepdims=True)
        cent = x - mean
        var = jnp.mean(cent * cent, -1, keepdims=True)
        rstd = lax.rsqrt(var + EPS)
        n = cent * rstd
        dn = nb * gin_ref[...]
        dx = rstd * (dn - jnp.mean(dn, -1, keepdims=True) - n * jnp.mean(dn * n, -1, keepdims=True))
        egrad[rows, :] = (dx + upstream[rows, :].astype(F32)).astype(BF)
        return carry

    lax.fori_loop(0, 2, back_tile, 0)
    for u in LATE:
        step(u, 1)
    for u in EARLY:
        step(u, 4)
    lax.fori_loop(2, 4, back_tile, 0)
    for u in LATE:
        step(u, 2)
    for u in EARLY:
        step(u, 5)

    landed(found.at[pl.ds(0, (OWNERS - 1) * 16)], row_send)

    def scatter(p, carry):
        q = lax.rem(s + p, 8)
        rows = pl.ds(pl.multiple_of(q * 256, 256), 256)
        found[rows, :] = (dot(put_one[rows, :], egrad[:, :256]) + dot(put_two[rows, :], egrad[:, 256:])).astype(BF)
        spread(found, incoming, back_send, back_recv, s, t, q, sixteen)
        return carry

    for n in range(4):
        lax.fori_loop(2 * n, 2 * n + 2, scatter, 0)
        for u in LATE:
            step(u, n + 3)
        if n < 3:
            for u in EARLY:
                step(u, n + 6)
    for u in LATE:
        step(u, 7)
    landed(incoming, back_recv)

    def order_tile(q, carry):
        both = incoming[pl.ds(pl.multiple_of(q * 256, 256), 256), :].astype(F32).reshape(16, 16, 256)
        part = pl.ds(pl.multiple_of(q * 128, 128), 128)
        rows_ref[part, :256] = both[:, :SLOTS].reshape(128, 256).astype(BF)
        rows_ref[part, 256:] = both[:, SLOTS:].reshape(128, 256).astype(BF)
        return carry

    lax.fori_loop(0, 8, order_tile, 0)
    for u in LATE:
        step(u, 8)
    landed(found.at[pl.ds(0, (OWNERS - 1) * 16)], back_send)
    landed(req_out.at[pl.ds(0, OWNERS - 1)], req_send)

    for h in range(HEADS):
        to = worker(h)
        left(kv_out.at[h], kv_send.at[h], *to)
        left(q_out.at[h], q_send.at[h], *to)
        for part in range(2):
            left(dm_out.at[h, pl.ds(part * 256, 256)], dm_send.at[h, part], *to)
        landed(kv_in.at[mine_of(h)], fwd_send.at[h])
        landed(part_out.at[h], part_send.at[h])
        back = (mine_of(h), base + user_core)
        left(mix_out.at[h], mix_send.at[h], *back)
        left(dq_out.at[h], dq_send.at[h], *back)
        left(dkv_out.at[h], dkv_send.at[h], *back)


    for u in range(len(ORDERS)):
        one, two, three = ORDERS[u]
        landed(terms.at[u, other_half], s0.at[u])
        landed(sums_ref.at[u, half], s7.at[u])
        for d in range(3):
            landed(r1.at[u, d], s1.at[u, d])
            landed(r2.at[u, d], s2.at[u, d])
            landed(r3.at[u, d], s3.at[u, d])
            landed(spot(u, place[one], place[two], place[three]), s4.at[u, d])
            landed(lines(u, place[one], place[two]), s5.at[u, d])
            landed(quarter(u, place[one]), s6.at[u, d])


def layer_step(length, owner, item_row, item_table, out_grad, gain_in, gain_out, w_in, w_out, factor):
    vm, far = pl.BlockSpec(memory_space=pltpu.VMEM), pl.BlockSpec(memory_space=pl.ANY)
    dma = pltpu.SemaphoreType.DMA
    n = len(ORDERS)

    def buf(*shape, dtype=BF):
        return pltpu.VMEM(shape, dtype)

    square = buf(TOK, WIDTH)
    wide = buf(TOK, WIDTH, dtype=F32)
    heads, pairs, carried = buf(4, TOK, HEAD), buf(4, TOK, 2 * HEAD), buf(4, TOK + 16, HEAD)
    message = buf(OWNERS, 1, 128, dtype=F32)
    blocks = [
        buf(ROWS, WIDTH), square, buf(WIDTH, 4 * WIDTH), square, buf(ROWS, 256),
        square, square, buf(n, WIDTH, WIDTH), square, square, buf(TOK, 4 * WIDTH, dtype=F32), square, square,
        square, wide, wide, buf(TOK, 4 * WIDTH),
        heads, pairs, heads, buf(8, TOK, 2 * HEAD), carried, carried, heads, heads,
        buf(4, TOK, HEAD, dtype=F32), buf(8, TOK, 2 * HEAD, dtype=F32),
        pairs, pairs, heads, pairs, heads, pairs, buf(TOK, HEAD, dtype=F32),
        message, message, buf(OWNERS * SLOTS, 128, dtype=F32), buf(ROWS, 256), buf(ROWS, 256),
        buf(TOK, 128, dtype=jnp.int32), buf(TOK, ROWS), buf(TOK, ROWS), buf(ROWS, TOK), buf(ROWS, TOK),
        buf(n, 256, WIDTH), buf(n, 256, WIDTH), buf(n, 3, 64, WIDTH), buf(n, 64, WIDTH),
        buf(n, 3, 16, WIDTH), buf(n, 16, WIDTH), buf(n, 3, 16, 128),
    ]
    one, three = dma((n,)), dma((n, 3))
    sems = [dma((c,)) for c in (4, 4, 4, 8, 4, 4, 4)] + [dma((4, 2))] * 2 + [dma((4,))] * 6
    sems += [dma((4,))] + [dma] * 6 + [one] * 2 + [three] * 12 + [one] * 2
    return pl.pallas_call(
        functools.partial(step_kernel, factor),
        out_shape=(
            jax.ShapeDtypeStruct((TOK, WIDTH), BF),
            jax.ShapeDtypeStruct((OWNERS * SLOTS, WIDTH), BF),
            jax.ShapeDtypeStruct((n, WIDTH, WIDTH), BF),
            jax.ShapeDtypeStruct((8, OWNERS * SLOTS), F32),
        ),
        in_specs=[pl.BlockSpec(memory_space=pltpu.SMEM), vm, vm, far, far, vm, vm, far, far],
        out_specs=(vm,) * 4,
        scratch_shapes=blocks + sems,
        compiler_params=pltpu.CompilerParams(
            collective_id=0, has_side_effects=True, vmem_limit_bytes=62 * 1024 * 1024
        ),
    )(length, owner, item_row, item_table, out_grad, gain_in.reshape(1, -1), gain_out.reshape(1, -1), w_in, w_out)


def finish_kernel(rows_ref, asked_ref, sums_ref, out_ref, w_in_ref, w_out_ref):
    at = lax.broadcasted_iota(jnp.int32, (256, OWNERS * SLOTS), 0) + pl.program_id(0) * 256
    hit = at == asked_ref[...][:1].astype(jnp.int32)
    out_ref[...] = dot(jnp.where(hit, 1.0, 0.0).astype(BF), rows_ref[...])
    for u in range(4):
        w_in_ref[:, u * WIDTH : (u + 1) * WIDTH] = sums_ref[u].astype(F32)
    w_out_ref[...] = sums_ref[4].astype(F32)


def finish(rows, asked, sums):
    n = len(ORDERS)
    return pl.pallas_call(
        finish_kernel,
        grid=(8,),
        out_shape=(
            jax.ShapeDtypeStruct((ROWS, WIDTH), F32),
            jax.ShapeDtypeStruct((WIDTH, 4 * WIDTH), F32),
            jax.ShapeDtypeStruct((WIDTH, WIDTH), F32),
        ),
        in_specs=[
            pl.BlockSpec((OWNERS * SLOTS, WIDTH), lambda i: (0, 0)),
            pl.BlockSpec((8, OWNERS * SLOTS), lambda i: (0, 0)),
            pl.BlockSpec((n, 64, WIDTH), lambda i: (0, i, 0)),
        ],
        out_specs=(
            pl.BlockSpec((256, WIDTH), lambda i: (i, 0)),
            pl.BlockSpec((64, 4 * WIDTH), lambda i: (i, 0)),
            pl.BlockSpec((64, WIDTH), lambda i: (i, 0)),
        ),
        compiler_params=pltpu.CompilerParams(vmem_limit_bytes=60 * 1024 * 1024),
    )(rows, asked, sums)


def local(item_table, owner, item_row, lengths, gain_in, gain_out, w_in, w_out, out_grad):
    factor = (TOK * OWNERS) ** (-0.5)
    hidden, rows, sums, asked = layer_step(
        lengths, owner.reshape(1, TOK), item_row, item_table, out_grad[0], gain_in, gain_out, w_in, w_out, factor
    )
    table_grad, w_in_grad, w_out_grad = finish(rows, asked, sums)
    return (hidden[None], table_grad, w_in_grad, w_out_grad)


def solution(mesh):
    placed = (
        P(("seq", "table"), None),
        P("table", "seq", None),
        P("table", "seq"),
        P("table"),
        P(),
        P(),
        P(),
        P(),
        P("table", "seq", None),
    )
    return jax.shard_map(
        local,
        mesh=mesh,
        in_specs=placed,
        out_specs=(P("table", "seq", None), P(("seq", "table"), None), P(), P()),
        check_vma=False,
    )
```

```python
import functools

import jax
import jax.numpy as jnp
from jax import lax
from jax.experimental import pallas as pl
from jax.experimental.pallas import tpu as pltpu
from jax.sharding import PartitionSpec as P

HEADS = 4
HEAD = 128
TOK = 512
WIDTH = 512
TILE = 128
SCALE = HEAD ** (-0.5)
EPS = 1e-05
MESH = pl.DeviceIdType.MESH
BF = jnp.bfloat16
F32 = jnp.float32


def dot(a, b, ca=1, cb=0):
    return lax.dot_general(a, b, (((ca,), (cb,)), ((), ())), preferred_element_type=F32)


def landed(ref, sem):
    pltpu.make_async_copy(ref, ref, sem).wait()


OWNERS = 128
SLOTS = 8
ROWS = 2048


def greet_all(s, t):
    barrier = pltpu.get_barrier_semaphore()
    me = s * 16 + t

    def greet(d, carry):
        other = lax.rem(me + d, OWNERS)
        pl.semaphore_signal(
            barrier, inc=1, device_id=(other // 16, lax.rem(other, 16)), device_id_type=MESH
        )
        return carry

    lax.fori_loop(1, OWNERS, greet, 0)
    return barrier


def send_rows(src, dst, send, recv, s, t, to_s, to_t, take, place):
    mine = jnp.logical_and(to_s == s, to_t == t)

    @pl.when(mine)
    def _():
        pltpu.make_async_copy(src.at[take], dst.at[place], recv).start()

    @pl.when(jnp.logical_not(mine))
    def _():
        pltpu.make_async_remote_copy(
            src_ref=src.at[take], dst_ref=dst.at[place], send_sem=send, recv_sem=recv,
            device_id=(to_s, to_t), device_id_type=MESH,
        ).start()


def sixteen(index):
    return pl.ds(pl.multiple_of(index * 16, 16), 16)


def spread(src, dst, send, recv, s, t, to_s, part):
    send_rows(src, dst, send, recv, s, t, to_s, t, part(to_s * 16 + t), part(s * 16 + t))
    for p in range(1, 16):
        to_t = lax.rem(t + p, 16)
        pltpu.make_async_remote_copy(
            src_ref=src.at[part(to_s * 16 + to_t)], dst_ref=dst.at[part(s * 16 + t)], send_sem=send, recv_sem=recv,
            device_id=(to_s, to_t), device_id_type=MESH,
        ).start()


ORDERS = ("zxy", "xyz", "yzx", "zxy", "zyx")
EARLY = (0, 4)
LATE = (1, 2, 3)


def step_kernel(
    factor,
    len_ref, owner_ref, row_ref, table_hbm, og_hbm, gin_ref, gout_ref, w_in_hbm, w_out_hbm,
    hidden_ref, rows_ref, sums_ref, asked_ref,
    table_ref, og_ref, w_in_ref, w_out_ref, incoming, x_ref, egrad, terms, normed, normed_t, slope, gate, upstream, joined, jgrad, nback, pback,
    q_out, kv_out, q_in, kv_in, mix_out, mix_in, dm_out, dm_in,
    dq_acc, dkv_acc, part_out, part_in, dq_out, dkv_out, dq_in, dkv_in, m_acc,
    req_out, req_in, asked_col, found, fetched, spot_col, pick_one, pick_two, put_one, put_two,
    r0, a1, r1, a2, r2, a3, r3,
    q_send, q_recv, kv_send, kv_recv, fwd_send, mix_send, mix_recv, dm_send, dm_recv,
    part_send, part_recv, dq_send, dq_recv, dkv_send, dkv_recv,
    load_sem, req_send, req_recv, row_send, row_recv, back_send, back_recv,
    s0, v0, s1, v1, s2, v2, s3, v3, s4, v4, s5, v5, s6, v6, s7, v7,
):
    s = lax.axis_index("seq")
    t = lax.axis_index("table")
    me = s * 16 + t
    core = lax.rem(t, 2)
    base = t - core
    head = lax.rem(s, HEADS)
    user_core = lax.rem(lax.rem(s, HEADS) + s // HEADS, 2)
    upward = user_core == 1
    sibling = base + 1 - core
    part_of_s = lax.rem((s + 1) // 2, 2)
    slot_of_s = s // 2
    cx, cz = lax.rem(s, 4), t // 4
    cy = lax.rem(t // 2, 2) * 2 + s // 4
    barrier = greet_all(s, t)

    def push(src, dst, send, recv, to_s, to_t):
        mine = jnp.logical_and(to_s == s, to_t == t)

        @pl.when(mine)
        def _():
            pltpu.make_async_copy(src, dst, recv).start()

        @pl.when(jnp.logical_not(mine))
        def _():
            pltpu.make_async_remote_copy(
                src_ref=src, dst_ref=dst, send_sem=send, recv_sem=recv,
                device_id=(to_s, to_t), device_id_type=MESH,
            ).start()

    def left(src, send, to_s, to_t):
        @pl.when(jnp.logical_not(jnp.logical_and(to_s == s, to_t == t)))
        def _():
            landed(src, send)

    def worker(h):
        return lax.rem(core + h, 2) * HEADS + h, base + part_of_s

    def mine_of(k):
        return 2 * k + lax.rem(k + core, 2)

    def other_of(k):
        return 2 * k + lax.rem(k + core + 1, 2)

    length = len_ref[0]

    def live_rows(start, count):
        pos = s * TOK + start + lax.broadcasted_iota(jnp.int32, (count, 1), 0)
        return (pos < length).astype(F32)

    place = {"x": cx, "y": cy, "z": cz}

    def partner(axis, d):
        other = lax.rem(place[axis] + d, 4)
        if axis == "x":
            return other, s - cx + other, t
        if axis == "y":
            return other, lax.rem(other, 2) * 4 + cx, cz * 4 + (other // 2) * 2 + core
        return other, s, other * 4 + lax.rem(t, 4)

    def ship(src, dst, send, recv, to_s, to_t):
        pltpu.make_async_remote_copy(
            src_ref=src, dst_ref=dst, send_sem=send, recv_sem=recv,
            device_id=(to_s, to_t), device_id_type=MESH,
        ).start()

    half = pl.ds(pl.multiple_of(core * 256, 256), 256)
    other_half = pl.ds(pl.multiple_of(256 - core * 256, 256), 256)

    def block_of(index, size):
        return pl.ds(pl.multiple_of(index * size, size), size)

    def block(axis, size):
        return block_of(place[axis], size)

    def spot(u, first, second, third):
        return sums_ref.at[u, block_of(core * 16 + first * 4 + second, 16), block_of(third, 128)]

    def lines(u, first, second):
        return sums_ref.at[u, block_of(core * 16 + first * 4 + second, 16)]

    def quarter(u, first):
        return sums_ref.at[u, block_of(core * 4 + first, 64)]

    def before_me(axis, d):
        return lax.rem(place[axis] + 4 - d, 4)

    def step(u, n):
        one, two, three = ORDERS[u]
        if n == 0:
            ship(terms.at[u, other_half], r0.at[u], s0.at[u], v0.at[u], s, sibling)
        elif n == 1:
            landed(r0.at[u], v0.at[u])
            a1[u] = (terms[u, half, :].astype(F32) + r0[u].astype(F32)).astype(BF)
            for d in range(1, 4):
                other, to_s, to_t = partner(one, d)
                ship(a1.at[u, block_of(other, 64)], r1.at[u, d - 1], s1.at[u, d - 1], v1.at[u, d - 1], to_s, to_t)
        elif n == 2:
            total = a1[u, block(one, 64), :].astype(F32)
            for d in range(1, 4):
                landed(r1.at[u, d - 1], v1.at[u, d - 1])
                total += r1[u, d - 1].astype(F32)
            a2[u] = total.astype(BF)
            for d in range(1, 4):
                other, to_s, to_t = partner(two, d)
                ship(a2.at[u, block_of(other, 16)], r2.at[u, d - 1], s2.at[u, d - 1], v2.at[u, d - 1], to_s, to_t)
        elif n == 3:
            total = a2[u, block(two, 16), :].astype(F32)
            for d in range(1, 4):
                landed(r2.at[u, d - 1], v2.at[u, d - 1])
                total += r2[u, d - 1].astype(F32)
            a3[u] = total.astype(BF)
            for d in range(1, 4):
                other, to_s, to_t = partner(three, d)
                ship(
                    a3.at[u, :, block_of(other, 128)], r3.at[u, d - 1], s3.at[u, d - 1], v3.at[u, d - 1], to_s, to_t
                )
        elif n == 4:
            total = a3[u, :, block(three, 128)].astype(F32)
            for d in range(1, 4):
                landed(r3.at[u, d - 1], v3.at[u, d - 1])
                total += r3[u, d - 1].astype(F32)
            mine = spot(u, place[one], place[two], place[three])
            mine[...] = total.astype(BF)
            for d in range(1, 4):
                _, to_s, to_t = partner(three, d)
                ship(mine, mine, s4.at[u, d - 1], v4.at[u, d - 1], to_s, to_t)
        elif n == 5:
            for d in range(1, 4):
                landed(spot(u, place[one], place[two], before_me(three, d)), v4.at[u, d - 1])
            mine = lines(u, place[one], place[two])
            for d in range(1, 4):
                _, to_s, to_t = partner(two, d)
                ship(mine, mine, s5.at[u, d - 1], v5.at[u, d - 1], to_s, to_t)
        elif n == 6:
            for d in range(1, 4):
                landed(lines(u, place[one], before_me(two, d)), v5.at[u, d - 1])
            mine = quarter(u, place[one])
            for d in range(1, 4):
                _, to_s, to_t = partner(one, d)
                ship(mine, mine, s6.at[u, d - 1], v6.at[u, d - 1], to_s, to_t)
        elif n == 7:
            for d in range(1, 4):
                landed(quarter(u, before_me(one, d)), v6.at[u, d - 1])
            ship(sums_ref.at[u, half], sums_ref.at[u, half], s7.at[u], v7.at[u], s, sibling)
        else:
            landed(sums_ref.at[u, other_half], v7.at[u])

    copies = [
        pltpu.make_async_copy(src, dst, load_sem.at[n])
        for n, (src, dst) in enumerate(
            ((table_hbm, table_ref), (og_hbm, og_ref), (w_out_hbm, w_out_ref), (w_in_hbm, w_in_ref))
        )
    ]
    for copy in copies:
        copy.start()

    target = owner_ref[...]
    line_e = lax.broadcasted_iota(jnp.int32, (OWNERS, TOK), 0)
    chosen_mask = line_e == target
    chosen = jnp.where(chosen_mask, 1.0, 0.0).astype(BF)
    above = jnp.where(
        lax.broadcasted_iota(jnp.int32, (TOK, TOK), 0) < lax.broadcasted_iota(jnp.int32, (TOK, TOK), 1), 1.0, 0.0
    ).astype(BF)
    before = dot(chosen, above)
    rank = jnp.sum(jnp.where(chosen_mask, before, 0.0), axis=0, keepdims=True).astype(jnp.int32)
    value = row_ref[...] + 1
    high = (value >> 7).astype(F32)
    low = (value & 127).astype(F32)
    message = jnp.where(line_e == rank, high, 0.0) + jnp.where(line_e == rank + SLOTS, low, 0.0)
    req_out[:, 0, :] = dot(chosen, message.astype(BF), 1, 1)
    pl.semaphore_wait(barrier, OWNERS - 1)

    def ask(p, carry):
        spread(req_out, req_in, req_send, req_recv, s, t, lax.rem(s + p, 8), lambda index: index)
        return carry

    lax.fori_loop(0, 8, ask, 0)

    slot_row = target * 16 + rank
    spot_col[...] = jnp.broadcast_to(slot_row.astype(F32), (128, TOK)).T.astype(jnp.int32)
    live = live_rows(0, TOK)
    copies[1].wait()
    copies[2].wait()
    upstream[...] = (og_ref[...].astype(F32) * live).astype(BF)
    jgrad[...] = dot(upstream[...], w_out_ref[...], 1, 1)
    number = lax.broadcasted_iota(jnp.int32, (OWNERS * SLOTS, OWNERS), 0)
    lane_s = lax.broadcasted_iota(jnp.int32, (OWNERS * SLOTS, OWNERS), 1)
    expand = jnp.where((number >> 3) == lane_s, 1.0, 0.0).astype(BF)
    landed(req_in, req_recv)
    values = dot(expand, req_in[:, 0, :].astype(BF))
    own = number & 7
    asked = (
        jnp.sum(
            jnp.where(lane_s == own, values * 128.0, 0.0) + jnp.where(lane_s == own + SLOTS, values, 0.0),
            axis=1,
            keepdims=True,
        )
        - 1.0
    )
    wide = jnp.broadcast_to(asked, (OWNERS * SLOTS, 128))
    asked_col[...] = wide
    asked_ref[...] = wide.T[:8]

    copies[0].wait()

    def gather(p, carry):
        q = lax.rem(s + p, 8)
        column = asked_col[pl.ds(pl.multiple_of(q * 128, 128), 128), :][:, :1].astype(jnp.int32)
        hit = lax.broadcasted_iota(jnp.int32, (128, ROWS), 1) == column
        rows = dot(jnp.where(hit, 1.0, 0.0).astype(BF), table_ref[...])
        both = jnp.concatenate(
            [rows[:, :256].reshape(16, SLOTS, 256), rows[:, 256:].reshape(16, SLOTS, 256)], axis=1
        )
        found[pl.ds(pl.multiple_of(q * 256, 256), 256), :] = both.reshape(256, 256).astype(BF)
        spread(found, fetched, row_send, row_recv, s, t, q, sixteen)
        return carry

    lax.fori_loop(0, 8, gather, 0)
    def pick_tile(r, carry):
        rows = pl.ds(pl.multiple_of(r * TILE, TILE), TILE)
        at = lax.broadcasted_iota(jnp.int32, (TILE, ROWS), 1)
        spots = spot_col[rows, :][:, :1]
        pick_one[rows, :] = jnp.where(at == spots, 1.0, 0.0).astype(BF)
        pick_two[rows, :] = jnp.where(at == spots + SLOTS, 1.0, 0.0).astype(BF)
        return carry

    lax.fori_loop(0, TOK // TILE, pick_tile, 0)
    dq_acc[...] = jnp.zeros_like(dq_acc)
    dkv_acc[...] = jnp.zeros_like(dkv_acc)
    copies[3].wait()
    landed(fetched, row_recv)

    def norm_tile(r, carry):
        rows = pl.ds(pl.multiple_of(r * TILE, TILE), TILE)
        x_ref[rows, :256] = dot(pick_one[rows, :], fetched[...]).astype(BF)
        x_ref[rows, 256:] = dot(pick_two[rows, :], fetched[...]).astype(BF)
        x = x_ref[rows, :].astype(F32)
        mean = jnp.mean(x, -1, keepdims=True)
        cent = x - mean
        var = jnp.mean(cent * cent, -1, keepdims=True)
        normed[rows, :] = (cent * lax.rsqrt(var + EPS) * gin_ref[...]).astype(BF)
        return carry

    lax.fori_loop(0, TOK // TILE, norm_tile, 0)

    def project(first, columns):
        pre = dot(normed[...], w_in_ref[:, pl.ds(first, columns)])
        half = 0.5 * pre
        th = jnp.tanh(half)
        slope[:, pl.ds(first, columns)] = 0.5 * (1.0 + th) * (1.0 + half - half * th)
        return half + half * th

    far_first = [lax.rem(cx + d, HEADS) for d in (2, 1, 3, 0)]
    for h in far_first:
        column = pl.multiple_of(h * HEAD, HEAD)
        kv_out[h, :, :HEAD] = project(3 * WIDTH + column, HEAD).astype(BF)
        kv_out[h, :, HEAD:] = (project(WIDTH + column, HEAD) * live).astype(BF)
        to = worker(h)
        push(kv_out.at[h], kv_in.at[s], kv_send.at[h], kv_recv.at[s], *to)
        q_out[h] = project(2 * WIDTH + column, HEAD).astype(BF)
        push(q_out.at[h], q_in.at[slot_of_s], q_send.at[h], q_recv.at[slot_of_s], *to)

    gate[:, :256] = project(0, 256).astype(BF)
    gate[:, 256:] = project(256, 256).astype(BF)
    normed_t[...] = normed[...].T

    def scatter_tile(q, carry):
        rows = pl.ds(pl.multiple_of(q * 256, 256), 256)
        at = lax.broadcasted_iota(jnp.int32, (256, TOK), 0) + q * 256
        put_one[rows, :] = jnp.where(at == slot_row, 1.0, 0.0).astype(BF)
        put_two[rows, :] = jnp.where(at == slot_row + SLOTS, 1.0, 0.0).astype(BF)
        return carry

    lax.fori_loop(0, 8, scatter_tile, 0)

    def take(k):
        d = mine_of(k)
        landed(kv_in.at[d], kv_recv.at[d])
        pltpu.make_async_remote_copy(
            src_ref=kv_in.at[d], dst_ref=kv_in.at[d], send_sem=fwd_send.at[k], recv_sem=kv_recv.at[d],
            device_id=(s, sibling), device_id_type=MESH,
        ).start()

    row = lax.broadcasted_iota(jnp.int32, (TOK, TOK), 0)
    col = lax.broadcasted_iota(jnp.int32, (TOK, TOK), 1)

    def forward_pair(k, j, diagonal):
        half = dot(q_in[k], kv_in[j, :, :HEAD], 1, 1) * (0.5 * SCALE)
        w = half + half * jnp.tanh(half)
        if diagonal:
            w = jnp.where(col <= row, w, 0.0)
        return dot(w.astype(BF), kv_in[j, :, HEAD:])

    def take_one(k, carry):
        take(k)
        return carry

    lax.fori_loop(0, jnp.where(upward, 1, 4), take_one, 0)

    def arrive(k, carry):
        landed(q_in.at[k], q_recv.at[k])
        o = other_of(k)
        landed(kv_in.at[o], kv_recv.at[o])
        return carry

    def forward(n, carry):
        k = jnp.where(upward, n, 3 - n)
        i = mine_of(k)

        @pl.when(jnp.logical_and(n < 3, upward))
        def _():
            take(n + 1)

        first = jnp.where(upward, n, 0)
        lax.fori_loop(first, jnp.where(upward, n + 1, jnp.where(n == 0, 4, 0)), arrive, 0)
        m_acc[...] = forward_pair(k, i, True)

        def inner(j, c):
            m_acc[...] += forward_pair(k, j, False)
            return c

        lax.fori_loop(0, i, inner, 0)
        m = m_acc[...]
        shift = jnp.mean(m, -1, keepdims=True).astype(BF).astype(F32)
        mix_out[k, :TOK, :] = (m - shift).astype(BF)
        wide = jnp.broadcast_to(shift, (TOK, HEAD))
        lines = jnp.zeros((16, HEAD), F32)
        line = lax.broadcasted_iota(jnp.int32, (16, HEAD), 0)
        for b in range(TOK // HEAD):
            lines += jnp.where(line == b, wide[b * HEAD : (b + 1) * HEAD].T[:16], 0.0)
        mix_out[k, TOK:, :] = lines.astype(BF)
        push(mix_out.at[k], mix_in.at[head], mix_send.at[k], mix_recv.at[head], i, base + user_core)
        return carry

    lax.fori_loop(0, 4, forward, 0)

    for h in range(HEADS):
        landed(mix_in.at[h], mix_recv.at[h])

    def post_tile(r, carry):
        start = pl.multiple_of(r * TILE, TILE)
        rows = pl.ds(start, TILE)
        alive = live_rows(start, TILE)
        pick = (lax.broadcasted_iota(jnp.int32, (16, HEAD), 0) == r).astype(F32).astype(BF)
        m = jnp.concatenate(
            [mix_in[h, rows, :].astype(F32) + dot(mix_in[h, TOK:, :], pick, 0, 0) for h in range(HEADS)], axis=1
        ) * alive
        mean = jnp.mean(m, -1, keepdims=True)
        cent = m - mean
        var = jnp.mean(cent * cent, -1, keepdims=True)
        rstd = lax.rsqrt(var + EPS)
        n = cent * rstd
        ng = n * gout_ref[...]
        g = gate[rows, :].astype(F32)
        jg = jgrad[rows, :]
        joined[rows, :] = (ng * g).astype(BF)
        pback[rows, :WIDTH] = (jg * ng * slope[rows, :WIDTH]).astype(BF)
        dn = jg * g * gout_ref[...]
        dm = rstd * (dn - jnp.mean(dn, -1, keepdims=True) - n * jnp.mean(dn * n, -1, keepdims=True))
        dm = (dm * alive).astype(BF)
        for h in range(HEADS):
            dm_out[h, rows, :] = dm[:, h * HEAD : (h + 1) * HEAD]
        return carry

    for part in range(2):
        lax.fori_loop(2 * part, 2 * part + 2, post_tile, 0)
        rows = pl.ds(part * 256, 256)
        for h in far_first:
            push(
                dm_out.at[h, rows], dm_in.at[slot_of_s, rows], dm_send.at[h, part], dm_recv.at[slot_of_s, part],
                *worker(h),
            )

    terms[4] = (dot(joined[...], upstream[...], 0, 0) * factor).astype(BF)
    terms[0] = (dot(normed_t[...], pback[:, :WIDTH]) * factor).astype(BF)
    for u in EARLY:
        step(u, 0)
    hidden_ref[...] = ((dot(joined[...], w_out_ref[...]) + x_ref[...].astype(F32)) * live).astype(BF)
    nback[...] = dot(pback[:, :WIDTH], w_in_ref[:, :WIDTH], 1, 1)
    for u in EARLY:
        step(u, 1)

    for k in range(4):
        for part in range(2):
            landed(dm_in.at[k, pl.ds(part * 256, 256)], dm_recv.at[k, part])

    def backward_pair(k, j, diagonal):
        q, dm = q_in[k], dm_in[k]
        half = dot(kv_in[j, :, :HEAD], q, 1, 1) * (0.5 * SCALE)
        th = jnp.tanh(half)
        ht = half * th
        w = half + ht
        sb = dot(kv_in[j, :, HEAD:], dm, 1, 1) * ((0.5 + 0.5 * th) * (1.0 + half - ht))
        if diagonal:
            w = jnp.where(row <= col, w, 0.0)
            sb = jnp.where(row <= col, sb, 0.0)
        sb = sb.astype(BF)
        dkv_acc[j, :, HEAD:] += dot(w.astype(BF), dm)
        dkv_acc[j, :, :HEAD] += dot(sb, q)
        dq_acc[k] += dot(sb, kv_in[j, :, :HEAD], 0, 0)

    def send_back(out, into, send, recv, k):
        push(out.at[k], into.at[head], send.at[k], recv.at[head], mine_of(k), base + user_core)

    def finish_query(k):
        dq_out[k] = (dq_acc[k] * SCALE).astype(BF)
        send_back(dq_out, dq_in, dq_send, dq_recv, k)

    def finish_key(j):
        m = j // 2

        @pl.when(mine_of(m) == j)
        def _():
            landed(part_in.at[m], part_recv.at[m])
            total = dkv_acc[j] + part_in[m].astype(F32)
            dkv_out[m, :, :HEAD] = (total[:, :HEAD] * SCALE).astype(BF)
            dkv_out[m, :, HEAD:] = total[:, HEAD:].astype(BF)
            send_back(dkv_out, dkv_in, dkv_send, dkv_recv, m)

    def key_block(n):
        return jnp.where(upward, n, 7 - n)

    def backward(n, carry):
        j = key_block(n)
        m = j // 2
        i = mine_of(m)

        @pl.when(i == j)
        def _():
            backward_pair(m, j, True)

        def inner(k, c):
            backward_pair(k, j, False)
            return c

        lax.fori_loop(jnp.where(i > j, m, m + 1), 4, inner, 0)

        @pl.when(i != j)
        def _():
            part_out[m] = dkv_acc[j].astype(BF)
            pltpu.make_async_remote_copy(
                src_ref=part_out.at[m], dst_ref=part_in.at[m], send_sem=part_send.at[m], recv_sem=part_recv.at[m],
                device_id=(s, sibling), device_id_type=MESH,
            ).start()

        @pl.when(jnp.logical_and(i == j, upward))
        def _():
            finish_query(m)

        @pl.when(n > 0)
        def _():
            finish_key(key_block(n - 1))

        return carry

    lax.fori_loop(0, 8, backward, 0)

    @pl.when(jnp.logical_not(upward))
    def _():
        for k in range(4):
            finish_query(k)

    finish_key(key_block(7))
    for u in EARLY:
        step(u, 2)

    for h in range(HEADS):
        landed(dq_in.at[h], dq_recv.at[h])
        landed(dkv_in.at[h], dkv_recv.at[h])

    def gate_tile(r, carry):
        start = pl.multiple_of(r * TILE, TILE)
        rows = pl.ds(start, TILE)
        alive = live_rows(start, TILE)
        for h in range(HEADS):
            for first, piece in (
                (WIDTH, dkv_in[h, rows, HEAD:].astype(F32) * alive),
                (2 * WIDTH, dq_in[h, rows, :].astype(F32)),
                (3 * WIDTH, dkv_in[h, rows, :HEAD].astype(F32)),
            ):
                c = first + h * HEAD
                pback[rows, c : c + HEAD] = (piece * slope[rows, c : c + HEAD]).astype(BF)
        return carry

    lax.fori_loop(0, TOK // TILE, gate_tile, 0)
    for u in LATE:
        terms[u] = (dot(normed_t[...], pback[:, u * WIDTH : (u + 1) * WIDTH]) * factor).astype(BF)
        step(u, 0)
    for u in EARLY:
        step(u, 3)

    def back_tile(r, carry):
        rows = pl.ds(pl.multiple_of(r * TILE, TILE), TILE)
        nb = nback[rows, :] + dot(pback[rows, WIDTH:], w_in_ref[:, WIDTH:], 1, 1)
        x = x_ref[rows, :].astype(F32)
        mean = jnp.mean(x, -1, keepdims=True)
        cent = x - mean
        var = jnp.mean(cent * cent, -1, keepdims=True)
        rstd = lax.rsqrt(var + EPS)
        n = cent * rstd
        dn = nb * gin_ref[...]
        dx = rstd * (dn - jnp.mean(dn, -1, keepdims=True) - n * jnp.mean(dn * n, -1, keepdims=True))
        egrad[rows, :] = (dx + upstream[rows, :].astype(F32)).astype(BF)
        return carry

    lax.fori_loop(0, 2, back_tile, 0)
    for u in LATE:
        step(u, 1)
    for u in EARLY:
        step(u, 4)
    lax.fori_loop(2, 4, back_tile, 0)
    for u in LATE:
        step(u, 2)
    for u in EARLY:
        step(u, 5)

    landed(found.at[pl.ds(0, (OWNERS - 1) * 16)], row_send)

    def scatter(p, carry):
        q = lax.rem(s + p, 8)
        rows = pl.ds(pl.multiple_of(q * 256, 256), 256)
        found[rows, :] = (dot(put_one[rows, :], egrad[:, :256]) + dot(put_two[rows, :], egrad[:, 256:])).astype(BF)
        spread(found, incoming, back_send, back_recv, s, t, q, sixteen)
        return carry

    for n in range(4):
        lax.fori_loop(2 * n, 2 * n + 2, scatter, 0)
        for u in LATE:
            step(u, n + 3)
        if n < 3:
            for u in EARLY:
                step(u, n + 6)
    for u in LATE:
        step(u, 7)
    landed(incoming, back_recv)

    def order_tile(q, carry):
        both = incoming[pl.ds(pl.multiple_of(q * 256, 256), 256), :].astype(F32).reshape(16, 16, 256)
        part = pl.ds(pl.multiple_of(q * 128, 128), 128)
        rows_ref[part, :256] = both[:, :SLOTS].reshape(128, 256).astype(BF)
        rows_ref[part, 256:] = both[:, SLOTS:].reshape(128, 256).astype(BF)
        return carry

    lax.fori_loop(0, 8, order_tile, 0)
    for u in LATE:
        step(u, 8)
    landed(found.at[pl.ds(0, (OWNERS - 1) * 16)], back_send)
    landed(req_out.at[pl.ds(0, OWNERS - 1)], req_send)

    for h in range(HEADS):
        to = worker(h)
        left(kv_out.at[h], kv_send.at[h], *to)
        left(q_out.at[h], q_send.at[h], *to)
        for part in range(2):
            left(dm_out.at[h, pl.ds(part * 256, 256)], dm_send.at[h, part], *to)
        landed(kv_in.at[mine_of(h)], fwd_send.at[h])
        landed(part_out.at[h], part_send.at[h])
        back = (mine_of(h), base + user_core)
        left(mix_out.at[h], mix_send.at[h], *back)
        left(dq_out.at[h], dq_send.at[h], *back)
        left(dkv_out.at[h], dkv_send.at[h], *back)


    for u in range(len(ORDERS)):
        one, two, three = ORDERS[u]
        landed(terms.at[u, other_half], s0.at[u])
        landed(sums_ref.at[u, half], s7.at[u])
        for d in range(3):
            landed(r1.at[u, d], s1.at[u, d])
            landed(r2.at[u, d], s2.at[u, d])
            landed(r3.at[u, d], s3.at[u, d])
            landed(spot(u, place[one], place[two], place[three]), s4.at[u, d])
            landed(lines(u, place[one], place[two]), s5.at[u, d])
            landed(quarter(u, place[one]), s6.at[u, d])


def layer_step(length, owner, item_row, item_table, out_grad, gain_in, gain_out, w_in, w_out, factor):
    vm, far = pl.BlockSpec(memory_space=pltpu.VMEM), pl.BlockSpec(memory_space=pl.ANY)
    dma = pltpu.SemaphoreType.DMA
    n = len(ORDERS)

    def buf(*shape, dtype=BF):
        return pltpu.VMEM(shape, dtype)

    square = buf(TOK, WIDTH)
    wide = buf(TOK, WIDTH, dtype=F32)
    heads, pairs, carried = buf(4, TOK, HEAD), buf(4, TOK, 2 * HEAD), buf(4, TOK + 16, HEAD)
    message = buf(OWNERS, 1, 128, dtype=F32)
    blocks = [
        buf(ROWS, WIDTH), square, buf(WIDTH, 4 * WIDTH), square, buf(ROWS, 256),
        square, square, buf(n, WIDTH, WIDTH), square, square, buf(TOK, 4 * WIDTH, dtype=F32), square, square,
        square, wide, wide, buf(TOK, 4 * WIDTH),
        heads, pairs, heads, buf(8, TOK, 2 * HEAD), carried, carried, heads, heads,
        buf(4, TOK, HEAD, dtype=F32), buf(8, TOK, 2 * HEAD, dtype=F32),
        pairs, pairs, heads, pairs, heads, pairs, buf(TOK, HEAD, dtype=F32),
        message, message, buf(OWNERS * SLOTS, 128, dtype=F32), buf(ROWS, 256), buf(ROWS, 256),
        buf(TOK, 128, dtype=jnp.int32), buf(TOK, ROWS), buf(TOK, ROWS), buf(ROWS, TOK), buf(ROWS, TOK),
        buf(n, 256, WIDTH), buf(n, 256, WIDTH), buf(n, 3, 64, WIDTH), buf(n, 64, WIDTH),
        buf(n, 3, 16, WIDTH), buf(n, 16, WIDTH), buf(n, 3, 16, 128),
    ]
    one, three = dma((n,)), dma((n, 3))
    sems = [dma((c,)) for c in (4, 4, 4, 8, 4, 4, 4)] + [dma((4, 2))] * 2 + [dma((4,))] * 6
    sems += [dma((4,))] + [dma] * 6 + [one] * 2 + [three] * 12 + [one] * 2
    return pl.pallas_call(
        functools.partial(step_kernel, factor),
        out_shape=(
            jax.ShapeDtypeStruct((TOK, WIDTH), BF),
            jax.ShapeDtypeStruct((OWNERS * SLOTS, WIDTH), BF),
            jax.ShapeDtypeStruct((n, WIDTH, WIDTH), BF),
            jax.ShapeDtypeStruct((8, OWNERS * SLOTS), F32),
        ),
        in_specs=[pl.BlockSpec(memory_space=pltpu.SMEM), vm, vm, far, far, vm, vm, far, far],
        out_specs=(vm,) * 4,
        scratch_shapes=blocks + sems,
        compiler_params=pltpu.CompilerParams(
            collective_id=0, has_side_effects=True, vmem_limit_bytes=62 * 1024 * 1024
        ),
    )(length, owner, item_row, item_table, out_grad, gain_in.reshape(1, -1), gain_out.reshape(1, -1), w_in, w_out)


def finish_kernel(rows_ref, asked_ref, sums_ref, layer_ref, out_ref, w_in_ref, w_out_ref, hidden_ref):
    hidden_ref[...] = layer_ref[...]
    at = lax.broadcasted_iota(jnp.int32, (1024, OWNERS * SLOTS), 0) + pl.program_id(0) * 1024
    hit = at == asked_ref[...][:1].astype(jnp.int32)
    out_ref[...] = dot(jnp.where(hit, 1.0, 0.0).astype(BF), rows_ref[...])
    for u in range(4):
        w_in_ref[:, u * WIDTH : (u + 1) * WIDTH] = sums_ref[u].astype(F32)
    w_out_ref[...] = sums_ref[4].astype(F32)


def finish(rows, asked, sums, hidden):
    n = len(ORDERS)
    return pl.pallas_call(
        finish_kernel,
        grid=(2,),
        out_shape=(
            jax.ShapeDtypeStruct((ROWS, WIDTH), F32),
            jax.ShapeDtypeStruct((WIDTH, 4 * WIDTH), F32),
            jax.ShapeDtypeStruct((WIDTH, WIDTH), F32),
            jax.ShapeDtypeStruct((TOK, WIDTH), BF),
        ),
        in_specs=[
            pl.BlockSpec((OWNERS * SLOTS, WIDTH), lambda i: (0, 0)),
            pl.BlockSpec((8, OWNERS * SLOTS), lambda i: (0, 0)),
            pl.BlockSpec((n, 256, WIDTH), lambda i: (0, i, 0)),
            pl.BlockSpec((256, WIDTH), lambda i: (i, 0)),
        ],
        out_specs=(
            pl.BlockSpec((1024, WIDTH), lambda i: (i, 0)),
            pl.BlockSpec((256, 4 * WIDTH), lambda i: (i, 0)),
            pl.BlockSpec((256, WIDTH), lambda i: (i, 0)),
            pl.BlockSpec((256, WIDTH), lambda i: (i, 0)),
        ),
        compiler_params=pltpu.CompilerParams(vmem_limit_bytes=60 * 1024 * 1024),
    )(rows, asked, sums, hidden)


def local(item_table, owner, item_row, lengths, gain_in, gain_out, w_in, w_out, out_grad):
    factor = (TOK * OWNERS) ** (-0.5)
    hidden, rows, sums, asked = layer_step(
        lengths, owner.reshape(1, TOK), item_row, item_table, out_grad[0], gain_in, gain_out, w_in, w_out, factor
    )
    table_grad, w_in_grad, w_out_grad, hidden = finish(rows, asked, sums, hidden)
    return (hidden[None], table_grad, w_in_grad, w_out_grad)


def solution(mesh):
    placed = (
        P(("seq", "table"), None),
        P("table", "seq", None),
        P("table", "seq"),
        P("table"),
        P(),
        P(),
        P(),
        P(),
        P("table", "seq", None),
    )
    return jax.shard_map(
        local,
        mesh=mesh,
        in_specs=placed,
        out_specs=(P("table", "seq", None), P(("seq", "table"), None), P(), P()),
        check_vma=False,
    )
```

```python
import functools

import jax
import jax.numpy as jnp
from jax import lax
from jax.experimental import pallas as pl
from jax.experimental.pallas import tpu as pltpu
from jax.sharding import PartitionSpec as P

HEADS = 4
HEAD = 128
TOK = 512
WIDTH = 512
TILE = 128
SCALE = HEAD ** (-0.5)
EPS = 1e-05
MESH = pl.DeviceIdType.MESH
BF = jnp.bfloat16
F32 = jnp.float32


def dot(a, b, ca=1, cb=0):
    return lax.dot_general(a, b, (((ca,), (cb,)), ((), ())), preferred_element_type=F32)


def landed(ref, sem):
    pltpu.make_async_copy(ref, ref, sem).wait()


OWNERS = 128
SLOTS = 8
ROWS = 2048


def greet_all(s, t):
    barrier = pltpu.get_barrier_semaphore()
    me = s * 16 + t

    def greet(d, carry):
        other = lax.rem(me + d, OWNERS)
        pl.semaphore_signal(
            barrier, inc=1, device_id=(other // 16, lax.rem(other, 16)), device_id_type=MESH
        )
        return carry

    lax.fori_loop(1, OWNERS, greet, 0)
    return barrier


def send_rows(src, dst, send, recv, s, t, to_s, to_t, take, place):
    mine = jnp.logical_and(to_s == s, to_t == t)

    @pl.when(mine)
    def _():
        pltpu.make_async_copy(src.at[take], dst.at[place], recv).start()

    @pl.when(jnp.logical_not(mine))
    def _():
        pltpu.make_async_remote_copy(
            src_ref=src.at[take], dst_ref=dst.at[place], send_sem=send, recv_sem=recv,
            device_id=(to_s, to_t), device_id_type=MESH,
        ).start()


def sixteen(index):
    return pl.ds(pl.multiple_of(index * 16, 16), 16)


def spread(src, dst, send, recv, s, t, to_s, part):
    send_rows(src, dst, send, recv, s, t, to_s, t, part(to_s * 16 + t), part(s * 16 + t))
    for p in range(1, 16):
        to_t = lax.rem(t + p, 16)
        pltpu.make_async_remote_copy(
            src_ref=src.at[part(to_s * 16 + to_t)], dst_ref=dst.at[part(s * 16 + t)], send_sem=send, recv_sem=recv,
            device_id=(to_s, to_t), device_id_type=MESH,
        ).start()


ORDERS = ("zxy", "xyz", "yzx", "zxy", "zyx")
EARLY = (0, 4)
LATE = (1, 2, 3)


def step_kernel(
    factor,
    len_ref, owner_ref, row_ref, table_hbm, og_hbm, gin_ref, gout_ref, w_in_hbm, w_out_hbm,
    hidden_ref, rows_ref, sums_ref, asked_ref,
    table_ref, og_ref, w_in_ref, w_out_ref, incoming, x_ref, egrad, terms, normed, normed_t, slope, gate, upstream, joined, jgrad, nback, pback,
    q_out, kv_out, q_in, kv_in, mix_out, mix_in, dm_out, dm_in,
    dq_acc, dkv_acc, part_out, part_in, dq_out, dkv_out, dq_in, dkv_in, m_acc,
    req_out, req_in, asked_col, found, fetched, spot_col, pick_one, pick_two, put_one, put_two,
    r0, a1, r1, a2, r2, a3, r3,
    q_send, q_recv, kv_send, kv_recv, fwd_send, mix_send, mix_recv, dm_send, dm_recv,
    part_send, part_recv, dq_send, dq_recv, dkv_send, dkv_recv,
    load_sem, req_send, req_recv, row_send, row_recv, back_send, back_recv,
    s0, v0, s1, v1, s2, v2, s3, v3, s4, v4, s5, v5, s6, v6, s7, v7,
):
    s = lax.axis_index("seq")
    t = lax.axis_index("table")
    me = s * 16 + t
    core = lax.rem(t, 2)
    base = t - core
    head = lax.rem(s, HEADS)
    user_core = lax.rem(lax.rem(s, HEADS) + s // HEADS, 2)
    upward = user_core == 1
    sibling = base + 1 - core
    part_of_s = lax.rem((s + 1) // 2, 2)
    slot_of_s = s // 2
    cx, cz = lax.rem(s, 4), t // 4
    cy = lax.rem(t // 2, 2) * 2 + s // 4
    barrier = greet_all(s, t)

    def push(src, dst, send, recv, to_s, to_t):
        mine = jnp.logical_and(to_s == s, to_t == t)

        @pl.when(mine)
        def _():
            pltpu.make_async_copy(src, dst, recv).start()

        @pl.when(jnp.logical_not(mine))
        def _():
            pltpu.make_async_remote_copy(
                src_ref=src, dst_ref=dst, send_sem=send, recv_sem=recv,
                device_id=(to_s, to_t), device_id_type=MESH,
            ).start()

    def left(src, send, to_s, to_t):
        @pl.when(jnp.logical_not(jnp.logical_and(to_s == s, to_t == t)))
        def _():
            landed(src, send)

    def worker(h):
        return lax.rem(core + h, 2) * HEADS + h, base + part_of_s

    def mine_of(k):
        return 2 * k + lax.rem(k + core, 2)

    def other_of(k):
        return 2 * k + lax.rem(k + core + 1, 2)

    length = len_ref[0]

    def live_rows(start, count):
        pos = s * TOK + start + lax.broadcasted_iota(jnp.int32, (count, 1), 0)
        return (pos < length).astype(F32)

    place = {"x": cx, "y": cy, "z": cz}

    def partner(axis, d):
        other = lax.rem(place[axis] + d, 4)
        if axis == "x":
            return other, s - cx + other, t
        if axis == "y":
            return other, lax.rem(other, 2) * 4 + cx, cz * 4 + (other // 2) * 2 + core
        return other, s, other * 4 + lax.rem(t, 4)

    def ship(src, dst, send, recv, to_s, to_t):
        pltpu.make_async_remote_copy(
            src_ref=src, dst_ref=dst, send_sem=send, recv_sem=recv,
            device_id=(to_s, to_t), device_id_type=MESH,
        ).start()

    half = pl.ds(pl.multiple_of(core * 256, 256), 256)
    other_half = pl.ds(pl.multiple_of(256 - core * 256, 256), 256)

    def block_of(index, size):
        return pl.ds(pl.multiple_of(index * size, size), size)

    def block(axis, size):
        return block_of(place[axis], size)

    def spot(u, first, second, third):
        return sums_ref.at[u, block_of(core * 16 + first * 4 + second, 16), block_of(third, 128)]

    def lines(u, first, second):
        return sums_ref.at[u, block_of(core * 16 + first * 4 + second, 16)]

    def quarter(u, first):
        return sums_ref.at[u, block_of(core * 4 + first, 64)]

    def before_me(axis, d):
        return lax.rem(place[axis] + 4 - d, 4)

    def step(u, n):
        one, two, three = ORDERS[u]
        if n == 0:
            ship(terms.at[u, other_half], r0.at[u], s0.at[u], v0.at[u], s, sibling)
        elif n == 1:
            landed(r0.at[u], v0.at[u])
            a1[u] = (terms[u, half, :].astype(F32) + r0[u].astype(F32)).astype(BF)
            for d in range(1, 4):
                other, to_s, to_t = partner(one, d)
                ship(a1.at[u, block_of(other, 64)], r1.at[u, d - 1], s1.at[u, d - 1], v1.at[u, d - 1], to_s, to_t)
        elif n == 2:
            total = a1[u, block(one, 64), :].astype(F32)
            for d in range(1, 4):
                landed(r1.at[u, d - 1], v1.at[u, d - 1])
                total += r1[u, d - 1].astype(F32)
            a2[u] = total.astype(BF)
            for d in range(1, 4):
                other, to_s, to_t = partner(two, d)
                ship(a2.at[u, block_of(other, 16)], r2.at[u, d - 1], s2.at[u, d - 1], v2.at[u, d - 1], to_s, to_t)
        elif n == 3:
            total = a2[u, block(two, 16), :].astype(F32)
            for d in range(1, 4):
                landed(r2.at[u, d - 1], v2.at[u, d - 1])
                total += r2[u, d - 1].astype(F32)
            a3[u] = total.astype(BF)
            for d in range(1, 4):
                other, to_s, to_t = partner(three, d)
                ship(
                    a3.at[u, :, block_of(other, 128)], r3.at[u, d - 1], s3.at[u, d - 1], v3.at[u, d - 1], to_s, to_t
                )
        elif n == 4:
            total = a3[u, :, block(three, 128)].astype(F32)
            for d in range(1, 4):
                landed(r3.at[u, d - 1], v3.at[u, d - 1])
                total += r3[u, d - 1].astype(F32)
            mine = spot(u, place[one], place[two], place[three])
            mine[...] = total.astype(BF)
            for d in range(1, 4):
                _, to_s, to_t = partner(three, d)
                ship(mine, mine, s4.at[u, d - 1], v4.at[u, d - 1], to_s, to_t)
        elif n == 5:
            for d in range(1, 4):
                landed(spot(u, place[one], place[two], before_me(three, d)), v4.at[u, d - 1])
            mine = lines(u, place[one], place[two])
            for d in range(1, 4):
                _, to_s, to_t = partner(two, d)
                ship(mine, mine, s5.at[u, d - 1], v5.at[u, d - 1], to_s, to_t)
        elif n == 6:
            for d in range(1, 4):
                landed(lines(u, place[one], before_me(two, d)), v5.at[u, d - 1])
            mine = quarter(u, place[one])
            for d in range(1, 4):
                _, to_s, to_t = partner(one, d)
                ship(mine, mine, s6.at[u, d - 1], v6.at[u, d - 1], to_s, to_t)
        elif n == 7:
            for d in range(1, 4):
                landed(quarter(u, before_me(one, d)), v6.at[u, d - 1])
            ship(sums_ref.at[u, half], sums_ref.at[u, half], s7.at[u], v7.at[u], s, sibling)
        else:
            landed(sums_ref.at[u, other_half], v7.at[u])

    copies = [
        pltpu.make_async_copy(src, dst, load_sem.at[n])
        for n, (src, dst) in enumerate(
            ((table_hbm, table_ref), (og_hbm, og_ref), (w_out_hbm, w_out_ref), (w_in_hbm, w_in_ref))
        )
    ]
    for copy in copies:
        copy.start()

    target = owner_ref[...]
    line_e = lax.broadcasted_iota(jnp.int32, (OWNERS, TOK), 0)
    chosen_mask = line_e == target
    chosen = jnp.where(chosen_mask, 1.0, 0.0).astype(BF)
    above = jnp.where(
        lax.broadcasted_iota(jnp.int32, (TOK, TOK), 0) < lax.broadcasted_iota(jnp.int32, (TOK, TOK), 1), 1.0, 0.0
    ).astype(BF)
    before = dot(chosen, above)
    rank = jnp.sum(jnp.where(chosen_mask, before, 0.0), axis=0, keepdims=True).astype(jnp.int32)
    value = row_ref[...] + 1
    high = (value >> 7).astype(F32)
    low = (value & 127).astype(F32)
    message = jnp.where(line_e == rank, high, 0.0) + jnp.where(line_e == rank + SLOTS, low, 0.0)
    req_out[:, 0, :] = dot(chosen, message.astype(BF), 1, 1)
    pl.semaphore_wait(barrier, OWNERS - 1)

    def ask(p, carry):
        spread(req_out, req_in, req_send, req_recv, s, t, lax.rem(s + p, 8), lambda index: index)
        return carry

    lax.fori_loop(0, 8, ask, 0)

    slot_row = target * 16 + rank
    spot_col[...] = jnp.broadcast_to(slot_row.astype(F32), (128, TOK)).T.astype(jnp.int32)
    live = live_rows(0, TOK)
    copies[1].wait()
    copies[2].wait()
    upstream[...] = (og_ref[...].astype(F32) * live).astype(BF)
    jgrad[...] = dot(upstream[...], w_out_ref[...], 1, 1)
    number = lax.broadcasted_iota(jnp.int32, (OWNERS * SLOTS, OWNERS), 0)
    lane_s = lax.broadcasted_iota(jnp.int32, (OWNERS * SLOTS, OWNERS), 1)
    expand = jnp.where((number >> 3) == lane_s, 1.0, 0.0).astype(BF)
    landed(req_in, req_recv)
    values = dot(expand, req_in[:, 0, :].astype(BF))
    own = number & 7
    asked = (
        jnp.sum(
            jnp.where(lane_s == own, values * 128.0, 0.0) + jnp.where(lane_s == own + SLOTS, values, 0.0),
            axis=1,
            keepdims=True,
        )
        - 1.0
    )
    wide = jnp.broadcast_to(asked, (OWNERS * SLOTS, 128))
    asked_col[...] = wide
    asked_ref[...] = wide.T[:8]

    copies[0].wait()

    def gather(p, carry):
        q = lax.rem(s // 2 + p, 4)
        column = asked_col[pl.ds(pl.multiple_of(q * 256, 256), 256), :][:, :1].astype(jnp.int32)
        hit = lax.broadcasted_iota(jnp.int32, (256, ROWS), 1) == column
        rows = dot(jnp.where(hit, 1.0, 0.0).astype(BF), table_ref[...])
        both = jnp.concatenate(
            [rows[:, :256].reshape(32, SLOTS, 256), rows[:, 256:].reshape(32, SLOTS, 256)], axis=1
        )
        found[pl.ds(pl.multiple_of(q * 512, 512), 512), :] = both.reshape(512, 256).astype(BF)

        def side(e, c):
            spread(found, fetched, row_send, row_recv, s, t, 2 * q + lax.rem(s + e, 2), sixteen)
            return c

        lax.fori_loop(0, 2, side, 0)
        return carry

    lax.fori_loop(0, 4, gather, 0)

    def pick_tile(r, carry):
        rows = pl.ds(pl.multiple_of(r * TILE, TILE), TILE)
        at = lax.broadcasted_iota(jnp.int32, (TILE, ROWS), 1)
        spots = spot_col[rows, :][:, :1]
        pick_one[rows, :] = jnp.where(at == spots, 1.0, 0.0).astype(BF)
        pick_two[rows, :] = jnp.where(at == spots + SLOTS, 1.0, 0.0).astype(BF)
        return carry

    lax.fori_loop(0, TOK // TILE, pick_tile, 0)
    dq_acc[...] = jnp.zeros_like(dq_acc)
    dkv_acc[...] = jnp.zeros_like(dkv_acc)
    copies[3].wait()
    landed(fetched, row_recv)

    x_ref[:, :256] = dot(pick_one[...], fetched[...]).astype(BF)
    x_ref[:, 256:] = dot(pick_two[...], fetched[...]).astype(BF)

    def norm_tile(r, carry):
        rows = pl.ds(pl.multiple_of(r * TILE, TILE), TILE)
        x = x_ref[rows, :].astype(F32)
        mean = jnp.mean(x, -1, keepdims=True)
        cent = x - mean
        var = jnp.mean(cent * cent, -1, keepdims=True)
        normed[rows, :] = (cent * lax.rsqrt(var + EPS) * gin_ref[...]).astype(BF)
        return carry

    lax.fori_loop(0, TOK // TILE, norm_tile, 0)

    def project(first, columns):
        pre = dot(normed[...], w_in_ref[:, pl.ds(first, columns)])
        half = 0.5 * pre
        th = jnp.tanh(half)
        slope[:, pl.ds(first, columns)] = 0.5 * (1.0 + th) * (1.0 + half - half * th)
        return half + half * th

    far_first = [lax.rem(cx + d, HEADS) for d in (2, 1, 3, 0)]
    for h in far_first:
        column = pl.multiple_of(h * HEAD, HEAD)
        kv_out[h, :, :HEAD] = project(3 * WIDTH + column, HEAD).astype(BF)
        kv_out[h, :, HEAD:] = (project(WIDTH + column, HEAD) * live).astype(BF)
        to = worker(h)
        push(kv_out.at[h], kv_in.at[s], kv_send.at[h], kv_recv.at[s], *to)
        q_out[h] = project(2 * WIDTH + column, HEAD).astype(BF)
        push(q_out.at[h], q_in.at[slot_of_s], q_send.at[h], q_recv.at[slot_of_s], *to)

    gate[:, :256] = project(0, 256).astype(BF)
    gate[:, 256:] = project(256, 256).astype(BF)
    normed_t[...] = normed[...].T

    def scatter_tile(q, carry):
        rows = pl.ds(pl.multiple_of(q * 256, 256), 256)
        at = lax.broadcasted_iota(jnp.int32, (256, TOK), 0) + q * 256
        put_one[rows, :] = jnp.where(at == slot_row, 1.0, 0.0).astype(BF)
        put_two[rows, :] = jnp.where(at == slot_row + SLOTS, 1.0, 0.0).astype(BF)
        return carry

    lax.fori_loop(0, 8, scatter_tile, 0)

    def take(k):
        d = mine_of(k)
        landed(kv_in.at[d], kv_recv.at[d])
        pltpu.make_async_remote_copy(
            src_ref=kv_in.at[d], dst_ref=kv_in.at[d], send_sem=fwd_send.at[k], recv_sem=kv_recv.at[d],
            device_id=(s, sibling), device_id_type=MESH,
        ).start()

    row = lax.broadcasted_iota(jnp.int32, (TOK, TOK), 0)
    col = lax.broadcasted_iota(jnp.int32, (TOK, TOK), 1)

    def forward_pair(k, j, diagonal):
        half = dot(q_in[k], kv_in[j, :, :HEAD], 1, 1) * (0.5 * SCALE)
        w = half + half * jnp.tanh(half)
        if diagonal:
            w = jnp.where(col <= row, w, 0.0)
        return dot(w.astype(BF), kv_in[j, :, HEAD:])

    def take_one(k, carry):
        take(k)
        return carry

    lax.fori_loop(0, jnp.where(upward, 1, 4), take_one, 0)

    def arrive(k, carry):
        landed(q_in.at[k], q_recv.at[k])
        o = other_of(k)
        landed(kv_in.at[o], kv_recv.at[o])
        return carry

    def forward(n, carry):
        k = jnp.where(upward, n, 3 - n)
        i = mine_of(k)

        @pl.when(jnp.logical_and(n < 3, upward))
        def _():
            take(n + 1)

        first = jnp.where(upward, n, 0)
        lax.fori_loop(first, jnp.where(upward, n + 1, jnp.where(n == 0, 4, 0)), arrive, 0)
        m_acc[...] = forward_pair(k, i, True)

        def inner(j, c):
            m_acc[...] += forward_pair(k, j, False)
            return c

        lax.fori_loop(0, i, inner, 0)
        m = m_acc[...]
        shift = jnp.mean(m, -1, keepdims=True).astype(BF).astype(F32)
        mix_out[k, :TOK, :] = (m - shift).astype(BF)
        wide = jnp.broadcast_to(shift, (TOK, HEAD))
        lines = jnp.zeros((16, HEAD), F32)
        line = lax.broadcasted_iota(jnp.int32, (16, HEAD), 0)
        for b in range(TOK // HEAD):
            lines += jnp.where(line == b, wide[b * HEAD : (b + 1) * HEAD].T[:16], 0.0)
        mix_out[k, TOK:, :] = lines.astype(BF)
        push(mix_out.at[k], mix_in.at[head], mix_send.at[k], mix_recv.at[head], i, base + user_core)
        return carry

    lax.fori_loop(0, 4, forward, 0)

    for h in range(HEADS):
        landed(mix_in.at[h], mix_recv.at[h])

    def post_tile(r, carry):
        start = pl.multiple_of(r * TILE, TILE)
        rows = pl.ds(start, TILE)
        alive = live_rows(start, TILE)
        pick = (lax.broadcasted_iota(jnp.int32, (16, HEAD), 0) == r).astype(F32).astype(BF)
        m = jnp.concatenate(
            [mix_in[h, rows, :].astype(F32) + dot(mix_in[h, TOK:, :], pick, 0, 0) for h in range(HEADS)], axis=1
        ) * alive
        mean = jnp.mean(m, -1, keepdims=True)
        cent = m - mean
        var = jnp.mean(cent * cent, -1, keepdims=True)
        rstd = lax.rsqrt(var + EPS)
        n = cent * rstd
        ng = n * gout_ref[...]
        g = gate[rows, :].astype(F32)
        jg = jgrad[rows, :]
        joined[rows, :] = (ng * g).astype(BF)
        pback[rows, :WIDTH] = (jg * ng * slope[rows, :WIDTH]).astype(BF)
        dn = jg * g * gout_ref[...]
        dm = rstd * (dn - jnp.mean(dn, -1, keepdims=True) - n * jnp.mean(dn * n, -1, keepdims=True))
        dm = (dm * alive).astype(BF)
        for h in range(HEADS):
            dm_out[h, rows, :] = dm[:, h * HEAD : (h + 1) * HEAD]
        return carry

    for part in range(2):
        lax.fori_loop(2 * part, 2 * part + 2, post_tile, 0)
        rows = pl.ds(part * 256, 256)
        for h in far_first:
            push(
                dm_out.at[h, rows], dm_in.at[slot_of_s, rows], dm_send.at[h, part], dm_recv.at[slot_of_s, part],
                *worker(h),
            )

    terms[4] = (dot(joined[...], upstream[...], 0, 0) * factor).astype(BF)
    terms[0] = (dot(normed_t[...], pback[:, :WIDTH]) * factor).astype(BF)
    for u in EARLY:
        step(u, 0)
    hidden_ref[...] = ((dot(joined[...], w_out_ref[...]) + x_ref[...].astype(F32)) * live).astype(BF)
    nback[...] = dot(pback[:, :WIDTH], w_in_ref[:, :WIDTH], 1, 1)
    for u in EARLY:
        step(u, 1)

    for k in range(4):
        for part in range(2):
            landed(dm_in.at[k, pl.ds(part * 256, 256)], dm_recv.at[k, part])

    def backward_pair(k, j, diagonal):
        q, dm = q_in[k], dm_in[k]
        half = dot(kv_in[j, :, :HEAD], q, 1, 1) * (0.5 * SCALE)
        th = jnp.tanh(half)
        ht = half * th
        w = half + ht
        sb = dot(kv_in[j, :, HEAD:], dm, 1, 1) * ((0.5 + 0.5 * th) * (1.0 + half - ht))
        if diagonal:
            w = jnp.where(row <= col, w, 0.0)
            sb = jnp.where(row <= col, sb, 0.0)
        sb = sb.astype(BF)
        dkv_acc[j, :, HEAD:] += dot(w.astype(BF), dm)
        dkv_acc[j, :, :HEAD] += dot(sb, q)
        dq_acc[k] += dot(sb, kv_in[j, :, :HEAD], 0, 0)

    def send_back(out, into, send, recv, k):
        push(out.at[k], into.at[head], send.at[k], recv.at[head], mine_of(k), base + user_core)

    def finish_query(k):
        dq_out[k] = (dq_acc[k] * SCALE).astype(BF)
        send_back(dq_out, dq_in, dq_send, dq_recv, k)

    def finish_key(j):
        m = j // 2

        @pl.when(mine_of(m) == j)
        def _():
            landed(part_in.at[m], part_recv.at[m])
            total = dkv_acc[j] + part_in[m].astype(F32)
            dkv_out[m, :, :HEAD] = (total[:, :HEAD] * SCALE).astype(BF)
            dkv_out[m, :, HEAD:] = total[:, HEAD:].astype(BF)
            send_back(dkv_out, dkv_in, dkv_send, dkv_recv, m)

    def key_block(n):
        return jnp.where(upward, n, 7 - n)

    def backward(n, carry):
        j = key_block(n)
        m = j // 2
        i = mine_of(m)

        @pl.when(i == j)
        def _():
            backward_pair(m, j, True)

        def inner(k, c):
            backward_pair(k, j, False)
            return c

        lax.fori_loop(jnp.where(i > j, m, m + 1), 4, inner, 0)

        @pl.when(i != j)
        def _():
            part_out[m] = dkv_acc[j].astype(BF)
            pltpu.make_async_remote_copy(
                src_ref=part_out.at[m], dst_ref=part_in.at[m], send_sem=part_send.at[m], recv_sem=part_recv.at[m],
                device_id=(s, sibling), device_id_type=MESH,
            ).start()

        @pl.when(jnp.logical_and(i == j, upward))
        def _():
            finish_query(m)

        @pl.when(n > 0)
        def _():
            finish_key(key_block(n - 1))

        return carry

    lax.fori_loop(0, 8, backward, 0)

    @pl.when(jnp.logical_not(upward))
    def _():
        for k in range(4):
            finish_query(k)

    finish_key(key_block(7))
    for u in EARLY:
        step(u, 2)

    for h in range(HEADS):
        landed(dq_in.at[h], dq_recv.at[h])
        landed(dkv_in.at[h], dkv_recv.at[h])

    def gate_tile(r, carry):
        start = pl.multiple_of(r * TILE, TILE)
        rows = pl.ds(start, TILE)
        alive = live_rows(start, TILE)
        for h in range(HEADS):
            for first, piece in (
                (WIDTH, dkv_in[h, rows, HEAD:].astype(F32) * alive),
                (2 * WIDTH, dq_in[h, rows, :].astype(F32)),
                (3 * WIDTH, dkv_in[h, rows, :HEAD].astype(F32)),
            ):
                c = first + h * HEAD
                pback[rows, c : c + HEAD] = (piece * slope[rows, c : c + HEAD]).astype(BF)
        return carry

    lax.fori_loop(0, TOK // TILE, gate_tile, 0)
    for u in LATE:
        terms[u] = (dot(normed_t[...], pback[:, u * WIDTH : (u + 1) * WIDTH]) * factor).astype(BF)
        step(u, 0)
    for u in EARLY:
        step(u, 3)

    def back_tile(r, carry):
        rows = pl.ds(pl.multiple_of(r * TILE, TILE), TILE)
        nb = nback[rows, :]
        x = x_ref[rows, :].astype(F32)
        mean = jnp.mean(x, -1, keepdims=True)
        cent = x - mean
        var = jnp.mean(cent * cent, -1, keepdims=True)
        rstd = lax.rsqrt(var + EPS)
        n = cent * rstd
        dn = nb * gin_ref[...]
        dx = rstd * (dn - jnp.mean(dn, -1, keepdims=True) - n * jnp.mean(dn * n, -1, keepdims=True))
        egrad[rows, :] = (dx + upstream[rows, :].astype(F32)).astype(BF)
        return carry

    nback[:256, :] += dot(pback[:256, WIDTH:], w_in_ref[:, WIDTH:], 1, 1)
    lax.fori_loop(0, 2, back_tile, 0)
    for u in LATE:
        step(u, 1)
    for u in EARLY:
        step(u, 4)
    nback[256:, :] += dot(pback[256:, WIDTH:], w_in_ref[:, WIDTH:], 1, 1)
    lax.fori_loop(2, 4, back_tile, 0)
    for u in LATE:
        step(u, 2)
    for u in EARLY:
        step(u, 5)

    landed(found.at[pl.ds(0, (OWNERS - 1) * 16)], row_send)

    def scatter(p, carry):
        q = lax.rem(s + p, 8)
        rows = pl.ds(pl.multiple_of(q * 256, 256), 256)
        found[rows, :] = (dot(put_one[rows, :], egrad[:, :256]) + dot(put_two[rows, :], egrad[:, 256:])).astype(BF)
        spread(found, incoming, back_send, back_recv, s, t, q, sixteen)
        return carry

    for n in range(4):
        lax.fori_loop(2 * n, 2 * n + 2, scatter, 0)
        for u in LATE:
            step(u, n + 3)
        if n < 3:
            for u in EARLY:
                step(u, n + 6)
    for u in LATE:
        step(u, 7)
    landed(incoming, back_recv)

    def order_tile(q, carry):
        both = incoming[pl.ds(pl.multiple_of(q * 256, 256), 256), :].astype(F32).reshape(16, 16, 256)
        part = pl.ds(pl.multiple_of(q * 128, 128), 128)
        rows_ref[part, :256] = both[:, :SLOTS].reshape(128, 256).astype(BF)
        rows_ref[part, 256:] = both[:, SLOTS:].reshape(128, 256).astype(BF)
        return carry

    lax.fori_loop(0, 8, order_tile, 0)
    for u in LATE:
        step(u, 8)
    landed(found.at[pl.ds(0, (OWNERS - 1) * 16)], back_send)
    landed(req_out.at[pl.ds(0, OWNERS - 1)], req_send)

    for h in range(HEADS):
        to = worker(h)
        left(kv_out.at[h], kv_send.at[h], *to)
        left(q_out.at[h], q_send.at[h], *to)
        for part in range(2):
            left(dm_out.at[h, pl.ds(part * 256, 256)], dm_send.at[h, part], *to)
        landed(kv_in.at[mine_of(h)], fwd_send.at[h])
        landed(part_out.at[h], part_send.at[h])
        back = (mine_of(h), base + user_core)
        left(mix_out.at[h], mix_send.at[h], *back)
        left(dq_out.at[h], dq_send.at[h], *back)
        left(dkv_out.at[h], dkv_send.at[h], *back)


    for u in range(len(ORDERS)):
        one, two, three = ORDERS[u]
        landed(terms.at[u, other_half], s0.at[u])
        landed(sums_ref.at[u, half], s7.at[u])
        for d in range(3):
            landed(r1.at[u, d], s1.at[u, d])
            landed(r2.at[u, d], s2.at[u, d])
            landed(r3.at[u, d], s3.at[u, d])
            landed(spot(u, place[one], place[two], place[three]), s4.at[u, d])
            landed(lines(u, place[one], place[two]), s5.at[u, d])
            landed(quarter(u, place[one]), s6.at[u, d])


def layer_step(length, owner, item_row, item_table, out_grad, gain_in, gain_out, w_in, w_out, factor):
    vm, far = pl.BlockSpec(memory_space=pltpu.VMEM), pl.BlockSpec(memory_space=pl.ANY)
    dma = pltpu.SemaphoreType.DMA
    n = len(ORDERS)

    def buf(*shape, dtype=BF):
        return pltpu.VMEM(shape, dtype)

    square = buf(TOK, WIDTH)
    wide = buf(TOK, WIDTH, dtype=F32)
    heads, pairs, carried = buf(4, TOK, HEAD), buf(4, TOK, 2 * HEAD), buf(4, TOK + 16, HEAD)
    message = buf(OWNERS, 1, 128, dtype=F32)
    blocks = [
        buf(ROWS, WIDTH), square, buf(WIDTH, 4 * WIDTH), square, buf(ROWS, 256),
        square, square, buf(n, WIDTH, WIDTH), square, square, buf(TOK, 4 * WIDTH, dtype=F32), square, square,
        square, wide, wide, buf(TOK, 4 * WIDTH),
        heads, pairs, heads, buf(8, TOK, 2 * HEAD), carried, carried, heads, heads,
        buf(4, TOK, HEAD, dtype=F32), buf(8, TOK, 2 * HEAD, dtype=F32),
        pairs, pairs, heads, pairs, heads, pairs, buf(TOK, HEAD, dtype=F32),
        message, message, buf(OWNERS * SLOTS, 128, dtype=F32), buf(ROWS, 256), buf(ROWS, 256),
        buf(TOK, 128, dtype=jnp.int32), buf(TOK, ROWS), buf(TOK, ROWS), buf(ROWS, TOK), buf(ROWS, TOK),
        buf(n, 256, WIDTH), buf(n, 256, WIDTH), buf(n, 3, 64, WIDTH), buf(n, 64, WIDTH),
        buf(n, 3, 16, WIDTH), buf(n, 16, WIDTH), buf(n, 3, 16, 128),
    ]
    one, three = dma((n,)), dma((n, 3))
    sems = [dma((c,)) for c in (4, 4, 4, 8, 4, 4, 4)] + [dma((4, 2))] * 2 + [dma((4,))] * 6
    sems += [dma((4,))] + [dma] * 6 + [one] * 2 + [three] * 12 + [one] * 2
    return pl.pallas_call(
        functools.partial(step_kernel, factor),
        out_shape=(
            jax.ShapeDtypeStruct((TOK, WIDTH), BF),
            jax.ShapeDtypeStruct((OWNERS * SLOTS, WIDTH), BF),
            jax.ShapeDtypeStruct((n, WIDTH, WIDTH), BF),
            jax.ShapeDtypeStruct((8, OWNERS * SLOTS), F32),
        ),
        in_specs=[pl.BlockSpec(memory_space=pltpu.SMEM), vm, vm, far, far, vm, vm, far, far],
        out_specs=(vm,) * 4,
        scratch_shapes=blocks + sems,
        compiler_params=pltpu.CompilerParams(
            collective_id=0, has_side_effects=True, vmem_limit_bytes=62 * 1024 * 1024
        ),
    )(length, owner, item_row, item_table, out_grad, gain_in.reshape(1, -1), gain_out.reshape(1, -1), w_in, w_out)


def finish_kernel(rows_ref, asked_ref, sums_ref, layer_ref, out_ref, w_in_ref, w_out_ref, hidden_ref):
    hidden_ref[...] = layer_ref[...]
    at = lax.broadcasted_iota(jnp.int32, (1024, OWNERS * SLOTS), 0) + pl.program_id(0) * 1024
    hit = at == asked_ref[...][:1].astype(jnp.int32)
    out_ref[...] = dot(jnp.where(hit, 1.0, 0.0).astype(BF), rows_ref[...])
    for u in range(4):
        w_in_ref[:, u * WIDTH : (u + 1) * WIDTH] = sums_ref[u].astype(F32)
    w_out_ref[...] = sums_ref[4].astype(F32)


def finish(rows, asked, sums, hidden):
    n = len(ORDERS)
    return pl.pallas_call(
        finish_kernel,
        grid=(2,),
        out_shape=(
            jax.ShapeDtypeStruct((ROWS, WIDTH), F32),
            jax.ShapeDtypeStruct((WIDTH, 4 * WIDTH), F32),
            jax.ShapeDtypeStruct((WIDTH, WIDTH), F32),
            jax.ShapeDtypeStruct((TOK, WIDTH), BF),
        ),
        in_specs=[
            pl.BlockSpec((OWNERS * SLOTS, WIDTH), lambda i: (0, 0)),
            pl.BlockSpec((8, OWNERS * SLOTS), lambda i: (0, 0)),
            pl.BlockSpec((n, 256, WIDTH), lambda i: (0, i, 0)),
            pl.BlockSpec((256, WIDTH), lambda i: (i, 0)),
        ],
        out_specs=(
            pl.BlockSpec((1024, WIDTH), lambda i: (i, 0)),
            pl.BlockSpec((256, 4 * WIDTH), lambda i: (i, 0)),
            pl.BlockSpec((256, WIDTH), lambda i: (i, 0)),
            pl.BlockSpec((256, WIDTH), lambda i: (i, 0)),
        ),
        compiler_params=pltpu.CompilerParams(vmem_limit_bytes=60 * 1024 * 1024),
    )(rows, asked, sums, hidden)


def local(item_table, owner, item_row, lengths, gain_in, gain_out, w_in, w_out, out_grad):
    factor = (TOK * OWNERS) ** (-0.5)
    hidden, rows, sums, asked = layer_step(
        lengths, owner.reshape(1, TOK), item_row, item_table, out_grad[0], gain_in, gain_out, w_in, w_out, factor
    )
    table_grad, w_in_grad, w_out_grad, hidden = finish(rows, asked, sums, hidden)
    return (hidden[None], table_grad, w_in_grad, w_out_grad)


def solution(mesh):
    placed = (
        P(("seq", "table"), None),
        P("table", "seq", None),
        P("table", "seq"),
        P("table"),
        P(),
        P(),
        P(),
        P(),
        P("table", "seq", None),
    )
    return jax.shard_map(
        local,
        mesh=mesh,
        in_specs=placed,
        out_specs=(P("table", "seq", None), P(("seq", "table"), None), P(), P()),
        check_vma=False,
    )
```

```python
import functools

import jax
import jax.numpy as jnp
from jax import lax
from jax.experimental import pallas as pl
from jax.experimental.pallas import tpu as pltpu
from jax.sharding import PartitionSpec as P

HEADS = 4
HEAD = 128
TOK = 512
WIDTH = 512
TILE = 128
SCALE = HEAD ** (-0.5)
EPS = 1e-05
MESH = pl.DeviceIdType.MESH
BF = jnp.bfloat16
F32 = jnp.float32


def dot(a, b, ca=1, cb=0):
    return lax.dot_general(a, b, (((ca,), (cb,)), ((), ())), preferred_element_type=F32)


def landed(ref, sem):
    pltpu.make_async_copy(ref, ref, sem).wait()


OWNERS = 128
SLOTS = 8
ROWS = 2048


def greet_all(s, t):
    barrier = pltpu.get_barrier_semaphore()
    me = s * 16 + t

    def greet(d, carry):
        other = lax.rem(me + d, OWNERS)
        pl.semaphore_signal(
            barrier, inc=1, device_id=(other // 16, lax.rem(other, 16)), device_id_type=MESH
        )
        return carry

    lax.fori_loop(1, OWNERS, greet, 0)
    return barrier


def send_rows(src, dst, send, recv, s, t, to_s, to_t, take, place):
    mine = jnp.logical_and(to_s == s, to_t == t)

    @pl.when(mine)
    def _():
        pltpu.make_async_copy(src.at[take], dst.at[place], recv).start()

    @pl.when(jnp.logical_not(mine))
    def _():
        pltpu.make_async_remote_copy(
            src_ref=src.at[take], dst_ref=dst.at[place], send_sem=send, recv_sem=recv,
            device_id=(to_s, to_t), device_id_type=MESH,
        ).start()


def sixteen(index):
    return pl.ds(pl.multiple_of(index * 16, 16), 16)


def spread(src, dst, send, recv, s, t, to_s, part):
    send_rows(src, dst, send, recv, s, t, to_s, t, part(to_s * 16 + t), part(s * 16 + t))
    for p in range(1, 16):
        to_t = lax.rem(t + p, 16)
        pltpu.make_async_remote_copy(
            src_ref=src.at[part(to_s * 16 + to_t)], dst_ref=dst.at[part(s * 16 + t)], send_sem=send, recv_sem=recv,
            device_id=(to_s, to_t), device_id_type=MESH,
        ).start()


ORDERS = ("zxy", "xyz", "yzx", "zxy", "zyx")
EARLY = (0, 4)
LATE = (1, 2, 3)


def step_kernel(
    factor,
    len_ref, owner_ref, row_ref, table_hbm, og_hbm, gin_ref, gout_ref, w_in_hbm, w_out_hbm,
    hidden_ref, rows_ref, sums_ref, asked_ref,
    table_ref, og_ref, w_in_ref, w_out_ref, incoming, x_ref, egrad, terms, normed, normed_t, slope, gate, upstream, joined, jgrad, nback, pback,
    q_out, kv_out, q_in, kv_in, mix_out, mix_in, dm_out, dm_in,
    dq_acc, dkv_acc, part_out, part_in, dq_out, dkv_out, dq_in, dkv_in, m_acc,
    req_out, req_in, asked_col, found, fetched, spot_col, pick_one, pick_two, put_one, put_two,
    r0, a1, r1, a2, r2, a3, r3,
    q_send, q_recv, kv_send, kv_recv, fwd_send, mix_send, mix_recv, dm_send, dm_recv,
    part_send, part_recv, dq_send, dq_recv, dkv_send, dkv_recv,
    load_sem, req_send, req_recv, row_send, row_recv, back_send, back_recv,
    s0, v0, s1, v1, s2, v2, s3, v3, s4, v4, s5, v5, s6, v6, s7, v7,
):
    s = lax.axis_index("seq")
    t = lax.axis_index("table")
    me = s * 16 + t
    core = lax.rem(t, 2)
    base = t - core
    head = lax.rem(s, HEADS)
    user_core = lax.rem(lax.rem(s, HEADS) + s // HEADS, 2)
    upward = user_core == 1
    sibling = base + 1 - core
    part_of_s = lax.rem((s + 1) // 2, 2)
    slot_of_s = s // 2
    cx, cz = lax.rem(s, 4), t // 4
    cy = lax.rem(t // 2, 2) * 2 + s // 4
    barrier = greet_all(s, t)

    def push(src, dst, send, recv, to_s, to_t):
        mine = jnp.logical_and(to_s == s, to_t == t)

        @pl.when(mine)
        def _():
            pltpu.make_async_copy(src, dst, recv).start()

        @pl.when(jnp.logical_not(mine))
        def _():
            pltpu.make_async_remote_copy(
                src_ref=src, dst_ref=dst, send_sem=send, recv_sem=recv,
                device_id=(to_s, to_t), device_id_type=MESH,
            ).start()

    def left(src, send, to_s, to_t):
        @pl.when(jnp.logical_not(jnp.logical_and(to_s == s, to_t == t)))
        def _():
            landed(src, send)

    def worker(h):
        return lax.rem(core + h, 2) * HEADS + h, base + part_of_s

    def mine_of(k):
        return 2 * k + lax.rem(k + core, 2)

    def other_of(k):
        return 2 * k + lax.rem(k + core + 1, 2)

    length = len_ref[0]

    def live_rows(start, count):
        pos = s * TOK + start + lax.broadcasted_iota(jnp.int32, (count, 1), 0)
        return (pos < length).astype(F32)

    place = {"x": cx, "y": cy, "z": cz}

    def partner(axis, d):
        other = lax.rem(place[axis] + d, 4)
        if axis == "x":
            return other, s - cx + other, t
        if axis == "y":
            return other, lax.rem(other, 2) * 4 + cx, cz * 4 + (other // 2) * 2 + core
        return other, s, other * 4 + lax.rem(t, 4)

    def ship(src, dst, send, recv, to_s, to_t):
        pltpu.make_async_remote_copy(
            src_ref=src, dst_ref=dst, send_sem=send, recv_sem=recv,
            device_id=(to_s, to_t), device_id_type=MESH,
        ).start()

    half = pl.ds(pl.multiple_of(core * 256, 256), 256)
    other_half = pl.ds(pl.multiple_of(256 - core * 256, 256), 256)

    def block_of(index, size):
        return pl.ds(pl.multiple_of(index * size, size), size)

    def block(axis, size):
        return block_of(place[axis], size)

    def spot(u, first, second, third):
        return sums_ref.at[u, block_of(core * 16 + first * 4 + second, 16), block_of(third, 128)]

    def lines(u, first, second):
        return sums_ref.at[u, block_of(core * 16 + first * 4 + second, 16)]

    def quarter(u, first):
        return sums_ref.at[u, block_of(core * 4 + first, 64)]

    def before_me(axis, d):
        return lax.rem(place[axis] + 4 - d, 4)

    def step(u, n):
        one, two, three = ORDERS[u]
        if n == 0:
            ship(terms.at[u, other_half], r0.at[u], s0.at[u], v0.at[u], s, sibling)
        elif n == 1:
            landed(r0.at[u], v0.at[u])
            a1[u] = (terms[u, half, :].astype(F32) + r0[u].astype(F32)).astype(BF)
            for d in range(1, 4):
                other, to_s, to_t = partner(one, d)
                ship(a1.at[u, block_of(other, 64)], r1.at[u, d - 1], s1.at[u, d - 1], v1.at[u, d - 1], to_s, to_t)
        elif n == 2:
            total = a1[u, block(one, 64), :].astype(F32)
            for d in range(1, 4):
                landed(r1.at[u, d - 1], v1.at[u, d - 1])
                total += r1[u, d - 1].astype(F32)
            a2[u] = total.astype(BF)
            for d in range(1, 4):
                other, to_s, to_t = partner(two, d)
                ship(a2.at[u, block_of(other, 16)], r2.at[u, d - 1], s2.at[u, d - 1], v2.at[u, d - 1], to_s, to_t)
        elif n == 3:
            total = a2[u, block(two, 16), :].astype(F32)
            for d in range(1, 4):
                landed(r2.at[u, d - 1], v2.at[u, d - 1])
                total += r2[u, d - 1].astype(F32)
            a3[u] = total.astype(BF)
            for d in range(1, 4):
                other, to_s, to_t = partner(three, d)
                ship(
                    a3.at[u, :, block_of(other, 128)], r3.at[u, d - 1], s3.at[u, d - 1], v3.at[u, d - 1], to_s, to_t
                )
        elif n == 4:
            total = a3[u, :, block(three, 128)].astype(F32)
            for d in range(1, 4):
                landed(r3.at[u, d - 1], v3.at[u, d - 1])
                total += r3[u, d - 1].astype(F32)
            mine = spot(u, place[one], place[two], place[three])
            mine[...] = total.astype(BF)
            for d in range(1, 4):
                _, to_s, to_t = partner(three, d)
                ship(mine, mine, s4.at[u, d - 1], v4.at[u, d - 1], to_s, to_t)
        elif n == 5:
            for d in range(1, 4):
                landed(spot(u, place[one], place[two], before_me(three, d)), v4.at[u, d - 1])
            mine = lines(u, place[one], place[two])
            for d in range(1, 4):
                _, to_s, to_t = partner(two, d)
                ship(mine, mine, s5.at[u, d - 1], v5.at[u, d - 1], to_s, to_t)
        elif n == 6:
            for d in range(1, 4):
                landed(lines(u, place[one], before_me(two, d)), v5.at[u, d - 1])
            mine = quarter(u, place[one])
            for d in range(1, 4):
                _, to_s, to_t = partner(one, d)
                ship(mine, mine, s6.at[u, d - 1], v6.at[u, d - 1], to_s, to_t)
        elif n == 7:
            for d in range(1, 4):
                landed(quarter(u, before_me(one, d)), v6.at[u, d - 1])
            ship(sums_ref.at[u, half], sums_ref.at[u, half], s7.at[u], v7.at[u], s, sibling)
        else:
            landed(sums_ref.at[u, other_half], v7.at[u])

    copies = [
        pltpu.make_async_copy(src, dst, load_sem.at[n])
        for n, (src, dst) in enumerate(
            ((table_hbm, table_ref), (og_hbm, og_ref), (w_out_hbm, w_out_ref), (w_in_hbm, w_in_ref))
        )
    ]
    for copy in copies:
        copy.start()

    target = owner_ref[...]
    line_e = lax.broadcasted_iota(jnp.int32, (OWNERS, TOK), 0)
    chosen_mask = line_e == target
    chosen = jnp.where(chosen_mask, 1.0, 0.0).astype(BF)
    above = jnp.where(
        lax.broadcasted_iota(jnp.int32, (TOK, TOK), 0) < lax.broadcasted_iota(jnp.int32, (TOK, TOK), 1), 1.0, 0.0
    ).astype(BF)
    before = dot(chosen, above)
    rank = jnp.sum(jnp.where(chosen_mask, before, 0.0), axis=0, keepdims=True).astype(jnp.int32)
    value = row_ref[...] + 1
    high = (value >> 7).astype(F32)
    low = (value & 127).astype(F32)
    message = jnp.where(line_e == rank, high, 0.0) + jnp.where(line_e == rank + SLOTS, low, 0.0)
    req_out[:, 0, :] = dot(chosen, message.astype(BF), 1, 1)
    pl.semaphore_wait(barrier, OWNERS - 1)

    def ask(p, carry):
        spread(req_out, req_in, req_send, req_recv, s, t, lax.rem(s + p, 8), lambda index: index)
        return carry

    lax.fori_loop(0, 8, ask, 0)

    slot_row = target * 16 + rank
    spot_col[...] = jnp.broadcast_to(slot_row.astype(F32), (128, TOK)).T.astype(jnp.int32)
    live = live_rows(0, TOK)
    copies[1].wait()
    copies[2].wait()
    upstream[...] = (og_ref[...].astype(F32) * live).astype(BF)
    jgrad[...] = dot(upstream[...], w_out_ref[...], 1, 1)
    number = lax.broadcasted_iota(jnp.int32, (OWNERS * SLOTS, OWNERS), 0)
    lane_s = lax.broadcasted_iota(jnp.int32, (OWNERS * SLOTS, OWNERS), 1)
    expand = jnp.where((number >> 3) == lane_s, 1.0, 0.0).astype(BF)
    landed(req_in, req_recv)
    values = dot(expand, req_in[:, 0, :].astype(BF))
    own = number & 7
    asked = (
        jnp.sum(
            jnp.where(lane_s == own, values * 128.0, 0.0) + jnp.where(lane_s == own + SLOTS, values, 0.0),
            axis=1,
            keepdims=True,
        )
        - 1.0
    )
    wide = jnp.broadcast_to(asked, (OWNERS * SLOTS, 128))
    asked_col[...] = wide
    asked_ref[...] = wide.T[:8]

    copies[0].wait()

    def gather(p, carry):
        q = lax.rem(s // 2 + p, 4)
        column = asked_col[pl.ds(pl.multiple_of(q * 256, 256), 256), :][:, :1].astype(jnp.int32)
        hit = lax.broadcasted_iota(jnp.int32, (256, ROWS), 1) == column
        rows = dot(jnp.where(hit, 1.0, 0.0).astype(BF), table_ref[...])
        both = jnp.concatenate(
            [rows[:, :256].reshape(32, SLOTS, 256), rows[:, 256:].reshape(32, SLOTS, 256)], axis=1
        )
        found[pl.ds(pl.multiple_of(q * 512, 512), 512), :] = both.reshape(512, 256).astype(BF)

        def side(e, c):
            spread(found, fetched, row_send, row_recv, s, t, 2 * q + lax.rem(s + e, 2), sixteen)
            return c

        lax.fori_loop(0, 2, side, 0)
        return carry

    lax.fori_loop(0, 4, gather, 0)

    def pick_tile(r, carry):
        rows = pl.ds(pl.multiple_of(r * TILE, TILE), TILE)
        at = lax.broadcasted_iota(jnp.int32, (TILE, ROWS), 1)
        spots = spot_col[rows, :][:, :1]
        pick_one[rows, :] = jnp.where(at == spots, 1.0, 0.0).astype(BF)
        pick_two[rows, :] = jnp.where(at == spots + SLOTS, 1.0, 0.0).astype(BF)
        return carry

    lax.fori_loop(0, TOK // TILE, pick_tile, 0)
    dq_acc[...] = jnp.zeros_like(dq_acc)
    dkv_acc[...] = jnp.zeros_like(dkv_acc)
    copies[3].wait()
    landed(fetched, row_recv)

    x_ref[:, :256] = dot(pick_one[...], fetched[...]).astype(BF)
    x_ref[:, 256:] = dot(pick_two[...], fetched[...]).astype(BF)

    def norm_tile(r, carry):
        rows = pl.ds(pl.multiple_of(r * TILE, TILE), TILE)
        x = x_ref[rows, :].astype(F32)
        mean = jnp.mean(x, -1, keepdims=True)
        cent = x - mean
        var = jnp.mean(cent * cent, -1, keepdims=True)
        normed[rows, :] = (cent * lax.rsqrt(var + EPS) * gin_ref[...]).astype(BF)
        return carry

    lax.fori_loop(0, TOK // TILE, norm_tile, 0)

    def project(first, columns):
        pre = dot(normed[...], w_in_ref[:, pl.ds(first, columns)])
        half = 0.5 * pre
        th = jnp.tanh(half)
        slope[:, pl.ds(first, columns)] = 0.5 * (1.0 + th) * (1.0 + half - half * th)
        return half + half * th

    far_first = [lax.rem(cx + d, HEADS) for d in (2, 1, 3, 0)]
    for h in far_first:
        column = pl.multiple_of(h * HEAD, HEAD)
        kv_out[h, :, :HEAD] = project(3 * WIDTH + column, HEAD).astype(BF)
        kv_out[h, :, HEAD:] = (project(WIDTH + column, HEAD) * live).astype(BF)
        to = worker(h)
        push(kv_out.at[h], kv_in.at[s], kv_send.at[h], kv_recv.at[s], *to)
        q_out[h] = project(2 * WIDTH + column, HEAD).astype(BF)
        push(q_out.at[h], q_in.at[slot_of_s], q_send.at[h], q_recv.at[slot_of_s], *to)

    gate[:, :256] = project(0, 256).astype(BF)
    gate[:, 256:] = project(256, 256).astype(BF)
    normed_t[...] = normed[...].T

    def scatter_tile(q, carry):
        rows = pl.ds(pl.multiple_of(q * 256, 256), 256)
        at = lax.broadcasted_iota(jnp.int32, (256, TOK), 0) + q * 256
        put_one[rows, :] = jnp.where(at == slot_row, 1.0, 0.0).astype(BF)
        put_two[rows, :] = jnp.where(at == slot_row + SLOTS, 1.0, 0.0).astype(BF)
        return carry

    lax.fori_loop(0, 8, scatter_tile, 0)

    def take(k):
        d = mine_of(k)
        landed(kv_in.at[d], kv_recv.at[d])
        pltpu.make_async_remote_copy(
            src_ref=kv_in.at[d], dst_ref=kv_in.at[d], send_sem=fwd_send.at[k], recv_sem=kv_recv.at[d],
            device_id=(s, sibling), device_id_type=MESH,
        ).start()

    row = lax.broadcasted_iota(jnp.int32, (TOK, TOK), 0)
    col = lax.broadcasted_iota(jnp.int32, (TOK, TOK), 1)

    def forward_pair(k, j, diagonal):
        half = dot(q_in[k], kv_in[j, :, :HEAD], 1, 1) * (0.5 * SCALE)
        w = half + half * jnp.tanh(half)
        if diagonal:
            w = jnp.where(col <= row, w, 0.0)
        return dot(w.astype(BF), kv_in[j, :, HEAD:])

    def take_one(k, carry):
        take(k)
        return carry

    lax.fori_loop(0, jnp.where(upward, 1, 4), take_one, 0)

    def arrive(k, carry):
        landed(q_in.at[k], q_recv.at[k])
        o = other_of(k)
        landed(kv_in.at[o], kv_recv.at[o])
        return carry

    def forward(n, carry):
        k = jnp.where(upward, n, 3 - n)
        i = mine_of(k)

        @pl.when(jnp.logical_and(n < 3, upward))
        def _():
            take(n + 1)

        first = jnp.where(upward, n, 0)
        lax.fori_loop(first, jnp.where(upward, n + 1, jnp.where(n == 0, 4, 0)), arrive, 0)
        m_acc[...] = forward_pair(k, i, True)

        def inner(j, c):
            m_acc[...] += forward_pair(k, j, False)
            return c

        lax.fori_loop(0, i, inner, 0)
        m = m_acc[...]
        shift = jnp.mean(m, -1, keepdims=True).astype(BF).astype(F32)
        mix_out[k, :TOK, :] = (m - shift).astype(BF)
        wide = jnp.broadcast_to(shift, (TOK, HEAD))
        lines = jnp.zeros((16, HEAD), F32)
        line = lax.broadcasted_iota(jnp.int32, (16, HEAD), 0)
        for b in range(TOK // HEAD):
            lines += jnp.where(line == b, wide[b * HEAD : (b + 1) * HEAD].T[:16], 0.0)
        mix_out[k, TOK:, :] = lines.astype(BF)
        push(mix_out.at[k], mix_in.at[head], mix_send.at[k], mix_recv.at[head], i, base + user_core)
        return carry

    lax.fori_loop(0, 4, forward, 0)

    for h in range(HEADS):
        landed(mix_in.at[h], mix_recv.at[h])

    def post_tile(r, carry):
        start = pl.multiple_of(r * TILE, TILE)
        rows = pl.ds(start, TILE)
        alive = live_rows(start, TILE)
        pick = (lax.broadcasted_iota(jnp.int32, (16, HEAD), 0) == r).astype(F32).astype(BF)
        m = jnp.concatenate(
            [mix_in[h, rows, :].astype(F32) + dot(mix_in[h, TOK:, :], pick, 0, 0) for h in range(HEADS)], axis=1
        ) * alive
        mean = jnp.mean(m, -1, keepdims=True)
        cent = m - mean
        var = jnp.mean(cent * cent, -1, keepdims=True)
        rstd = lax.rsqrt(var + EPS)
        n = cent * rstd
        ng = n * gout_ref[...]
        g = gate[rows, :].astype(F32)
        jg = jgrad[rows, :]
        joined[rows, :] = (ng * g).astype(BF)
        pback[rows, :WIDTH] = (jg * ng * slope[rows, :WIDTH]).astype(BF)
        dn = jg * g * gout_ref[...]
        dm = rstd * (dn - jnp.mean(dn, -1, keepdims=True) - n * jnp.mean(dn * n, -1, keepdims=True))
        dm = (dm * alive).astype(BF)
        for h in range(HEADS):
            dm_out[h, rows, :] = dm[:, h * HEAD : (h + 1) * HEAD]
        return carry

    for part in range(2):
        lax.fori_loop(2 * part, 2 * part + 2, post_tile, 0)
        rows = pl.ds(part * 256, 256)
        for h in far_first:
            push(
                dm_out.at[h, rows], dm_in.at[slot_of_s, rows], dm_send.at[h, part], dm_recv.at[slot_of_s, part],
                *worker(h),
            )

    terms[4] = (dot(joined[...], upstream[...], 0, 0) * factor).astype(BF)
    terms[0] = (dot(normed_t[...], pback[:, :WIDTH]) * factor).astype(BF)
    for u in EARLY:
        step(u, 0)
    hidden_ref[...] = ((dot(joined[...], w_out_ref[...]) + x_ref[...].astype(F32)) * live).astype(BF)
    nback[...] = dot(pback[:, :WIDTH], w_in_ref[:, :WIDTH], 1, 1)
    for u in EARLY:
        step(u, 1)

    for k in range(4):
        for part in range(2):
            landed(dm_in.at[k, pl.ds(part * 256, 256)], dm_recv.at[k, part])

    def backward_pair(k, j, diagonal):
        q, dm = q_in[k], dm_in[k]
        half = dot(kv_in[j, :, :HEAD], q, 1, 1) * (0.5 * SCALE)
        th = jnp.tanh(half)
        ht = half * th
        w = half + ht
        sb = dot(kv_in[j, :, HEAD:], dm, 1, 1) * ((0.5 + 0.5 * th) * (1.0 + half - ht))
        if diagonal:
            w = jnp.where(row <= col, w, 0.0)
            sb = jnp.where(row <= col, sb, 0.0)
        sb = sb.astype(BF)
        dkv_acc[j, :, HEAD:] += dot(w.astype(BF), dm)
        dkv_acc[j, :, :HEAD] += dot(sb, q)
        dq_acc[k] += dot(sb, kv_in[j, :, :HEAD], 0, 0)

    def send_back(out, into, send, recv, k):
        push(out.at[k], into.at[head], send.at[k], recv.at[head], mine_of(k), base + user_core)

    def finish_query(k):
        dq_out[k] = (dq_acc[k] * SCALE).astype(BF)
        send_back(dq_out, dq_in, dq_send, dq_recv, k)

    def finish_key(j):
        m = j // 2

        @pl.when(mine_of(m) == j)
        def _():
            landed(part_in.at[m], part_recv.at[m])
            total = dkv_acc[j] + part_in[m].astype(F32)
            dkv_out[m, :, :HEAD] = (total[:, :HEAD] * SCALE).astype(BF)
            dkv_out[m, :, HEAD:] = total[:, HEAD:].astype(BF)
            send_back(dkv_out, dkv_in, dkv_send, dkv_recv, m)

    def key_block(n):
        return jnp.where(upward, n, 7 - n)

    def backward(n, carry):
        j = key_block(n)
        m = j // 2
        i = mine_of(m)

        @pl.when(i == j)
        def _():
            backward_pair(m, j, True)

        def inner(k, c):
            backward_pair(k, j, False)
            return c

        lax.fori_loop(jnp.where(i > j, m, m + 1), 4, inner, 0)

        @pl.when(i != j)
        def _():
            part_out[m] = dkv_acc[j].astype(BF)
            pltpu.make_async_remote_copy(
                src_ref=part_out.at[m], dst_ref=part_in.at[m], send_sem=part_send.at[m], recv_sem=part_recv.at[m],
                device_id=(s, sibling), device_id_type=MESH,
            ).start()

        @pl.when(jnp.logical_and(i == j, upward))
        def _():
            finish_query(m)

        @pl.when(n > 0)
        def _():
            finish_key(key_block(n - 1))

        return carry

    lax.fori_loop(0, 8, backward, 0)

    @pl.when(jnp.logical_not(upward))
    def _():
        for k in range(4):
            finish_query(k)

    finish_key(key_block(7))
    for u in EARLY:
        step(u, 2)

    for h in range(HEADS):
        landed(dq_in.at[h], dq_recv.at[h])
        landed(dkv_in.at[h], dkv_recv.at[h])

    def gate_tile(r, carry):
        start = pl.multiple_of(r * TILE, TILE)
        rows = pl.ds(start, TILE)
        alive = live_rows(start, TILE)
        for h in range(HEADS):
            for first, piece in (
                (WIDTH, dkv_in[h, rows, HEAD:].astype(F32) * alive),
                (2 * WIDTH, dq_in[h, rows, :].astype(F32)),
                (3 * WIDTH, dkv_in[h, rows, :HEAD].astype(F32)),
            ):
                c = first + h * HEAD
                pback[rows, c : c + HEAD] = (piece * slope[rows, c : c + HEAD]).astype(BF)
        return carry

    lax.fori_loop(0, TOK // TILE, gate_tile, 0)
    for u in LATE:
        terms[u] = (dot(normed_t[...], pback[:, u * WIDTH : (u + 1) * WIDTH]) * factor).astype(BF)
        step(u, 0)
    for u in EARLY:
        step(u, 3)

    def back_tile(r, carry):
        rows = pl.ds(pl.multiple_of(r * TILE, TILE), TILE)
        nb = nback[rows, :]
        x = x_ref[rows, :].astype(F32)
        mean = jnp.mean(x, -1, keepdims=True)
        cent = x - mean
        var = jnp.mean(cent * cent, -1, keepdims=True)
        rstd = lax.rsqrt(var + EPS)
        n = cent * rstd
        dn = nb * gin_ref[...]
        dx = rstd * (dn - jnp.mean(dn, -1, keepdims=True) - n * jnp.mean(dn * n, -1, keepdims=True))
        egrad[rows, :] = (dx + upstream[rows, :].astype(F32)).astype(BF)
        return carry

    nback[:256, :] += dot(pback[:256, WIDTH:], w_in_ref[:, WIDTH:], 1, 1)
    lax.fori_loop(0, 2, back_tile, 0)
    for u in LATE:
        step(u, 1)
    for u in EARLY:
        step(u, 4)
    nback[256:, :] += dot(pback[256:, WIDTH:], w_in_ref[:, WIDTH:], 1, 1)
    lax.fori_loop(2, 4, back_tile, 0)
    for u in LATE:
        step(u, 2)
    for u in EARLY:
        step(u, 5)

    landed(found.at[pl.ds(0, (OWNERS - 1) * 16)], row_send)

    def scatter(p, carry):
        q = lax.rem(s // 2 + p, 4)
        rows = pl.ds(pl.multiple_of(q * 512, 512), 512)
        found[rows, :] = (dot(put_one[rows, :], egrad[:, :256]) + dot(put_two[rows, :], egrad[:, 256:])).astype(BF)

        def side(e, c):
            spread(found, incoming, back_send, back_recv, s, t, 2 * q + lax.rem(s + e, 2), sixteen)
            return c

        lax.fori_loop(0, 2, side, 0)
        return carry

    for n in range(4):
        scatter(n, 0)
        for u in LATE:
            step(u, n + 3)
        if n < 3:
            for u in EARLY:
                step(u, n + 6)
    for u in LATE:
        step(u, 7)
    landed(incoming, back_recv)

    def order_tile(q, carry):
        both = incoming[pl.ds(pl.multiple_of(q * 256, 256), 256), :].astype(F32).reshape(16, 16, 256)
        part = pl.ds(pl.multiple_of(q * 128, 128), 128)
        rows_ref[part, :256] = both[:, :SLOTS].reshape(128, 256).astype(BF)
        rows_ref[part, 256:] = both[:, SLOTS:].reshape(128, 256).astype(BF)
        return carry

    lax.fori_loop(0, 8, order_tile, 0)
    for u in LATE:
        step(u, 8)
    landed(found.at[pl.ds(0, (OWNERS - 1) * 16)], back_send)
    landed(req_out.at[pl.ds(0, OWNERS - 1)], req_send)

    for h in range(HEADS):
        to = worker(h)
        left(kv_out.at[h], kv_send.at[h], *to)
        left(q_out.at[h], q_send.at[h], *to)
        for part in range(2):
            left(dm_out.at[h, pl.ds(part * 256, 256)], dm_send.at[h, part], *to)
        landed(kv_in.at[mine_of(h)], fwd_send.at[h])
        landed(part_out.at[h], part_send.at[h])
        back = (mine_of(h), base + user_core)
        left(mix_out.at[h], mix_send.at[h], *back)
        left(dq_out.at[h], dq_send.at[h], *back)
        left(dkv_out.at[h], dkv_send.at[h], *back)


    for u in range(len(ORDERS)):
        one, two, three = ORDERS[u]
        landed(terms.at[u, other_half], s0.at[u])
        landed(sums_ref.at[u, half], s7.at[u])
        for d in range(3):
            landed(r1.at[u, d], s1.at[u, d])
            landed(r2.at[u, d], s2.at[u, d])
            landed(r3.at[u, d], s3.at[u, d])
            landed(spot(u, place[one], place[two], place[three]), s4.at[u, d])
            landed(lines(u, place[one], place[two]), s5.at[u, d])
            landed(quarter(u, place[one]), s6.at[u, d])


def layer_step(length, owner, item_row, item_table, out_grad, gain_in, gain_out, w_in, w_out, factor):
    vm, far = pl.BlockSpec(memory_space=pltpu.VMEM), pl.BlockSpec(memory_space=pl.ANY)
    dma = pltpu.SemaphoreType.DMA
    n = len(ORDERS)

    def buf(*shape, dtype=BF):
        return pltpu.VMEM(shape, dtype)

    square = buf(TOK, WIDTH)
    wide = buf(TOK, WIDTH, dtype=F32)
    heads, pairs, carried = buf(4, TOK, HEAD), buf(4, TOK, 2 * HEAD), buf(4, TOK + 16, HEAD)
    message = buf(OWNERS, 1, 128, dtype=F32)
    blocks = [
        buf(ROWS, WIDTH), square, buf(WIDTH, 4 * WIDTH), square, buf(ROWS, 256),
        square, square, buf(n, WIDTH, WIDTH), square, square, buf(TOK, 4 * WIDTH, dtype=F32), square, square,
        square, wide, wide, buf(TOK, 4 * WIDTH),
        heads, pairs, heads, buf(8, TOK, 2 * HEAD), carried, carried, heads, heads,
        buf(4, TOK, HEAD, dtype=F32), buf(8, TOK, 2 * HEAD, dtype=F32),
        pairs, pairs, heads, pairs, heads, pairs, buf(TOK, HEAD, dtype=F32),
        message, message, buf(OWNERS * SLOTS, 128, dtype=F32), buf(ROWS, 256), buf(ROWS, 256),
        buf(TOK, 128, dtype=jnp.int32), buf(TOK, ROWS), buf(TOK, ROWS), buf(ROWS, TOK), buf(ROWS, TOK),
        buf(n, 256, WIDTH), buf(n, 256, WIDTH), buf(n, 3, 64, WIDTH), buf(n, 64, WIDTH),
        buf(n, 3, 16, WIDTH), buf(n, 16, WIDTH), buf(n, 3, 16, 128),
    ]
    one, three = dma((n,)), dma((n, 3))
    sems = [dma((c,)) for c in (4, 4, 4, 8, 4, 4, 4)] + [dma((4, 2))] * 2 + [dma((4,))] * 6
    sems += [dma((4,))] + [dma] * 6 + [one] * 2 + [three] * 12 + [one] * 2
    return pl.pallas_call(
        functools.partial(step_kernel, factor),
        out_shape=(
            jax.ShapeDtypeStruct((TOK, WIDTH), BF),
            jax.ShapeDtypeStruct((OWNERS * SLOTS, WIDTH), BF),
            jax.ShapeDtypeStruct((n, WIDTH, WIDTH), BF),
            jax.ShapeDtypeStruct((8, OWNERS * SLOTS), F32),
        ),
        in_specs=[pl.BlockSpec(memory_space=pltpu.SMEM), vm, vm, far, far, vm, vm, far, far],
        out_specs=(vm,) * 4,
        scratch_shapes=blocks + sems,
        compiler_params=pltpu.CompilerParams(
            collective_id=0, has_side_effects=True, vmem_limit_bytes=62 * 1024 * 1024
        ),
    )(length, owner, item_row, item_table, out_grad, gain_in.reshape(1, -1), gain_out.reshape(1, -1), w_in, w_out)


def finish_kernel(rows_ref, asked_ref, sums_ref, layer_ref, out_ref, w_in_ref, w_out_ref, hidden_ref):
    hidden_ref[...] = layer_ref[...]
    at = lax.broadcasted_iota(jnp.int32, (1024, OWNERS * SLOTS), 0) + pl.program_id(0) * 1024
    hit = at == asked_ref[...][:1].astype(jnp.int32)
    out_ref[...] = dot(jnp.where(hit, 1.0, 0.0).astype(BF), rows_ref[...])
    for u in range(4):
        w_in_ref[:, u * WIDTH : (u + 1) * WIDTH] = sums_ref[u].astype(F32)
    w_out_ref[...] = sums_ref[4].astype(F32)


def finish(rows, asked, sums, hidden):
    n = len(ORDERS)
    return pl.pallas_call(
        finish_kernel,
        grid=(2,),
        out_shape=(
            jax.ShapeDtypeStruct((ROWS, WIDTH), F32),
            jax.ShapeDtypeStruct((WIDTH, 4 * WIDTH), F32),
            jax.ShapeDtypeStruct((WIDTH, WIDTH), F32),
            jax.ShapeDtypeStruct((TOK, WIDTH), BF),
        ),
        in_specs=[
            pl.BlockSpec((OWNERS * SLOTS, WIDTH), lambda i: (0, 0)),
            pl.BlockSpec((8, OWNERS * SLOTS), lambda i: (0, 0)),
            pl.BlockSpec((n, 256, WIDTH), lambda i: (0, i, 0)),
            pl.BlockSpec((256, WIDTH), lambda i: (i, 0)),
        ],
        out_specs=(
            pl.BlockSpec((1024, WIDTH), lambda i: (i, 0)),
            pl.BlockSpec((256, 4 * WIDTH), lambda i: (i, 0)),
            pl.BlockSpec((256, WIDTH), lambda i: (i, 0)),
            pl.BlockSpec((256, WIDTH), lambda i: (i, 0)),
        ),
        compiler_params=pltpu.CompilerParams(vmem_limit_bytes=60 * 1024 * 1024),
    )(rows, asked, sums, hidden)


def local(item_table, owner, item_row, lengths, gain_in, gain_out, w_in, w_out, out_grad):
    factor = (TOK * OWNERS) ** (-0.5)
    hidden, rows, sums, asked = layer_step(
        lengths, owner.reshape(1, TOK), item_row, item_table, out_grad[0], gain_in, gain_out, w_in, w_out, factor
    )
    table_grad, w_in_grad, w_out_grad, hidden = finish(rows, asked, sums, hidden)
    return (hidden[None], table_grad, w_in_grad, w_out_grad)


def solution(mesh):
    placed = (
        P(("seq", "table"), None),
        P("table", "seq", None),
        P("table", "seq"),
        P("table"),
        P(),
        P(),
        P(),
        P(),
        P("table", "seq", None),
    )
    return jax.shard_map(
        local,
        mesh=mesh,
        in_specs=placed,
        out_specs=(P("table", "seq", None), P(("seq", "table"), None), P(), P()),
        check_vma=False,
    )
```
